128 devices in a mesh: slab: 32 (over y_hi, x, z), sub: 4 (over y_lo, core).
Axes of the slice: x: 4, y: 4 (y_hi: 2, y_lo: 2; y = y_hi * 2 + y_lo), z: 4, core: 2. Of those that a mesh axis runs over, the one named last changes fastest.
Arguments:
- inputs: bfloat16 [64, 64, 64, 128], P('slab', 'sub'), may hold values from -6 to 6
- fine_cot: bfloat16 [64, 64, 64, 128], P('slab', 'sub'), may hold values from -6 to 6
- coarse_cot: bfloat16 [32, 32, 128, 64], P('slab', 'sub'), may hold values from -6 to 6
- weight_fine: bfloat16 [3, 3, 3, 64, 64], replicated, may hold values from -0.15625 to 0.15625
- weight_coarse: bfloat16 [3, 3, 3, 64, 128], replicated, may hold values from -0.15625 to 0.15625
Outputs:
- grad_input: bfloat16 [64, 64, 64, 128], P('slab', 'sub')
- grad_fine: float32 [3, 3, 3, 64, 64], replicated
- grad_coarse: float32 [3, 3, 3, 64, 128], replicated
The draws below stay inside these ranges and needn't reach their ends.
All inputs are finite; a program needn't handle non-finite values.
Results may differ from the reference program's by a relative error of at most 0.014.
Values may be sent and summed in bfloat16 or wider, within the bound.
No kernel may reach another device: no remote copies, remote signals or barrier semaphores. Data moves between devices by JAX's collectives and lax.ppermute only.
A program may use at most 64 MiB of HBM per device.

```python
import jax
import jax.numpy as jnp
from jax import lax

C_FINE = 64
C_COARSE = 128
DEPTH = 128
NX = 64
NY = 64


def block_scale(own_key, shape, shards, least, largest):
    def one(axis_at, parts):
        draws = jax.random.uniform(jax.random.fold_in(jax.random.fold_in(own_key, 6), axis_at), (parts,), jnp.float32, least / len(shards), largest / len(shards))
        return jnp.repeat(jnp.exp(draws), shape[axis_at] // parts).reshape((-1,) + (1,) * (len(shape) - axis_at - 1))

    factor_of = one(*shards[0])
    for cut in shards[1:]:
        factor_of = factor_of * one(*cut)
    return factor_of


def normal_values(own_key, dims, scale, bound, cuts=(), dtype=jnp.bfloat16):
    factor_of = block_scale(own_key, dims, cuts, -0.22, 0.18) if cuts else 1.0
    values = jax.random.normal(own_key, dims, jnp.float32) * scale * factor_of
    return jnp.minimum(jnp.maximum(values, -bound), bound).astype(dtype)


def setup_inputs(seed: int = 0) -> dict:
    arg_keys = jax.random.split(jax.random.key(seed), 6)
    return {
        "inputs": normal_values(arg_keys[0], (NX, NY, C_FINE, DEPTH), 1.0, 6.0, ((0, 32), (1, 4))),
        "fine_cot": normal_values(arg_keys[1], (NX, NY, C_FINE, DEPTH), 1.0, 6.0, ((0, 32), (1, 4))),
        "coarse_cot": normal_values(arg_keys[2], (NX // 2, NY // 2, C_COARSE, DEPTH // 2), 1.0, 6.0, ((0, 32), (1, 4))),
        "weight_fine": normal_values(arg_keys[3], (3, 3, 3, C_FINE, C_FINE), (27 * C_FINE) ** -0.5, 0.15625),
        "weight_coarse": normal_values(arg_keys[4], (3, 3, 3, C_FINE, C_COARSE), (27 * C_FINE) ** -0.5, 0.15625),
    }


def pad_space(field):
    return jnp.pad(field, ((1, 1), (1, 1), (0, 0), (1, 1)))

def convolve(padded, weight, rows, cols, depth):
    total = jnp.zeros((rows, cols, weight.shape[4], depth), jnp.float32)
    for i in range(3):
        for j in range(3):
            for k in range(3):
                window = padded[i:i + rows, j:j + cols, :, k:k + depth]
                total = total + jnp.einsum('xycz,co->xyoz', window, weight[i, j, k], precision=lax.Precision.HIGHEST)
    return total

def correlate(padded, grad, rows, cols, depth):
    terms = []
    for i in range(3):
        for j in range(3):
            for k in range(3):
                window = padded[i:i + rows, j:j + cols, :, k:k + depth]
                terms.append(jnp.einsum('xycz,xyoz->co', window, grad, precision=lax.Precision.HIGHEST))
    return jnp.stack(terms).reshape((3, 3, 3, padded.shape[2], grad.shape[2]))

def transpose_kernel(weight):
    return jnp.swapaxes(jnp.flip(weight, (0, 1, 2)), 3, 4)

def gate_slope(value):
    sig = jax.nn.sigmoid(value)
    return sig * (1.0 + value * (1.0 - sig))

def reference(inputs, fine_cot, coarse_cot, weight_fine, weight_coarse):
    rows, cols, chans, depth = inputs.shape
    wf = weight_fine.astype(jnp.float32)
    wc = weight_coarse.astype(jnp.float32)
    padded_in = pad_space(inputs).astype(jnp.float32)
    pre_fine = convolve(padded_in, wf, rows, cols, depth)
    act = jax.nn.silu(pre_fine).astype(jnp.bfloat16)
    blocks = act.astype(jnp.float32).reshape((rows // 2, 2, cols // 2, 2, chans, depth // 2, 2))
    pooled = lax.optimization_barrier(jnp.mean(blocks, axis=(1, 3, 6))).astype(jnp.bfloat16)
    padded_pool = pad_space(pooled).astype(jnp.float32)
    pre_coarse = convolve(padded_pool, wc, rows // 2, cols // 2, depth // 2)
    grad_pc = (coarse_cot.astype(jnp.float32) * gate_slope(pre_coarse)).astype(jnp.bfloat16)
    coarse_cells = jnp.float32(rows * cols * depth // 8)
    grad_coarse = correlate(padded_pool, grad_pc.astype(jnp.float32), rows // 2, cols // 2, depth // 2) / jnp.sqrt(coarse_cells)
    grad_pooled = convolve(pad_space(grad_pc).astype(jnp.float32), transpose_kernel(wc), rows // 2, cols // 2, depth // 2)
    spread = jnp.repeat(jnp.repeat(jnp.repeat(grad_pooled, 2, axis=0), 2, axis=1), 2, axis=3) * 0.125
    grad_pf = ((fine_cot.astype(jnp.float32) + spread) * gate_slope(pre_fine)).astype(jnp.bfloat16)
    fine_cells = jnp.float32(rows * cols * depth)
    grad_fine = correlate(padded_in, grad_pf.astype(jnp.float32), rows, cols, depth) / jnp.sqrt(fine_cells)
    grad_input = convolve(pad_space(grad_pf).astype(jnp.float32), transpose_kernel(wf), rows, cols, depth).astype(jnp.bfloat16)
    return (grad_input, grad_fine, grad_coarse)
```

```python
import functools

import jax
import jax.numpy as jnp
from jax import lax
from jax.experimental import pallas as pl
from jax.experimental.pallas import tpu as pltpu
from jax.sharding import PartitionSpec as P

L = 128
YH = 7
BF = jnp.bfloat16
F32 = jnp.float32
ROWS = 24
FINE_AT = 1728
VMEM = 56 * 1024 * 1024


def iota(shape, dim):
    return lax.broadcasted_iota(jnp.int32, shape, dim)


def shifted(tile, by, lane):
    out = pltpu.roll(tile, by % L, 1)
    keep = lane >= by if by > 0 else lane < L + by
    return jnp.where(keep, out, 0.0)


def combine(acc, rows, tiles, step, lane):
    out = []
    for t in range(tiles):
        part = acc[:, t * L : (t + 1) * L]
        out.append(
            shifted(part[:rows], step, lane)
            + part[rows : 2 * rows]
            + shifted(part[2 * rows :], -step, lane)
        )
    return out


def slopes(value):
    sig = jax.nn.sigmoid(value)
    return sig, sig * (1.0 + value * (1.0 - sig))


def dot(a, b):
    return jnp.dot(a, b, preferred_element_type=F32)


def spread_matrix():
    row, col = iota((L, 2 * L), 0), iota((L, 2 * L), 1)
    return jnp.where(row == (col // L) * 64 + (col % L) // 2, 1.0, 0.0).astype(BF)


def fine_kernel(flags, own, xlo, xhi, ylo, yhi, weight, v2, slope, pooled):
    f = [flags[i] > 0 for i in range(4)]
    ny = 16 + 2 * YH
    for x in range(4):
        ok = f[0] if x == 0 else f[1] if x == 3 else None
        for y in range(ny):
            if y < YH:
                tile, edge = ylo[x, y], f[2]
            elif y >= YH + 16:
                tile, edge = yhi[x, y - YH - 16], f[3]
            else:
                src = xlo[0] if x == 0 else xhi[0] if x == 3 else own[x - 1]
                tile, edge = src[y - YH], None
            for cond in (ok, edge):
                if cond is not None:
                    tile = jnp.where(cond, tile, jnp.zeros_like(tile))
            v2[x * 64 : (x + 1) * 64, y * L : (y + 1) * L] = tile
    lane = iota((128, L), 1)
    lane64 = iota((64, L), 1)
    row, col = iota((1024, L), 0), iota((1024, L), 1)
    pool = jnp.where(col == ((row // 256) % 2) * 64 + (row % L) // 2, 1.0, 0.0).astype(BF)
    for t in range(7):
        acc = None
        for j in range(3):
            term = dot(weight[j], v2[:, (4 * t + j) * L : (4 * t + j + 4) * L])
            acc = term if acc is None else acc + term
        acts = []
        for n, pre in enumerate(combine(acc, 128, 4, 1, lane)):
            sig, slp = slopes(pre)
            acts.append((pre * sig).astype(BF))
            at = 4 * t + n - 5
            if 0 <= at < 18:
                slope[:, at * L : (at + 1) * L] = slp
        cells = jnp.concatenate([a[:64] for a in acts] + [a[64:] for a in acts], axis=1)
        mean = dot(cells, pool) * 0.125
        yc = 2 * t + lane64 // 64
        keep = ((yc >= 3) | f[2]) & ((yc < 11) | f[3])
        pooled[:, t * L : (t + 1) * L] = jnp.where(keep, mean, 0.0).astype(BF)


def coarse_kernel(flags, own, lo, hi, cot_lo, cot, cot_hi, weight, p2, gpc, gpack):
    f = [flags[i] > 0 for i in range(4)]
    spread = spread_matrix()
    for t in range(7):
        at = slice(t * L, (t + 1) * L)
        zero = jnp.zeros((64, L), BF)
        rows = jnp.concatenate(
            [jnp.where(f[0], lo[:, at], zero), own[:, at], jnp.where(f[1], hi[:, at], zero)], axis=0
        )
        p2[:, 2 * t * L : (2 * t + 2) * L] = dot(rows, spread).astype(BF)
    lane = iota((128, L), 1)
    row, col = iota((2 * L, L), 0), iota((2 * L, L), 1)
    pack = jnp.where(
        (row % 2 == 0) & (col == (row // L) * 64 + (row % L) // 2), 1.0, 0.0
    ).astype(BF)
    for t in range(6):
        acc = None
        for j in range(3):
            term = dot(weight[j], p2[:, (2 * t + j) * L : (2 * t + j + 2) * L])
            acc = term if acc is None else acc + term
        if t == 0:
            cc = dot(cot_lo[...], spread)
        elif t == 5:
            cc = dot(cot_hi[...], spread)
        else:
            cc = jnp.concatenate(
                [dot(cot[2 * t - 2 + n], spread[:64, :L]) for n in range(2)], axis=1
            )
        out = []
        for n, pre in enumerate(combine(acc, 128, 2, 2, lane)):
            _, slp = slopes(pre)
            val = (cc[:, n * L : (n + 1) * L] * slp).astype(BF)
            if t == 0 or t == 5:
                val = jnp.where(f[2] if t == 0 else f[3], val, jnp.zeros_like(val))
            out.append(val)
        pair = jnp.concatenate(out, axis=1)
        gpc[:, 2 * t * L : (2 * t + 2) * L] = pair
        gpack[:, t * L : (t + 1) * L] = dot(pair, pack).astype(BF)


def nt(a, b):
    return lax.dot_general(a, b, (((1,), (1,)), ((), ())), preferred_element_type=F32)


def coarse_corr_kernel(scale, p2, gpc, out, g3):
    lane = iota((128, L), 1)
    for y in range(8):
        tile = gpc[:, (2 + y) * L : (3 + y) * L].astype(F32)
        at = slice(y * L, (y + 1) * L)
        g3[0:128, at] = shifted(tile, -2, lane).astype(BF)
        g3[128:256, at] = tile.astype(BF)
        g3[256:384, at] = shifted(tile, 2, lane).astype(BF)
    for j in range(3):
        res = nt(p2[:, (2 + j) * L : (10 + j) * L], g3[...]) * (0.5 * scale)
        for k in range(3):
            at = (3 * j + k) * 192
            out[at : at + 192, :] = res[:, k * L : (k + 1) * L].astype(BF)


def gpf_kernel(flags, own, lo, hi, weight, fc, fc_lo, fc_hi, slope, gpf, g2):
    f = [flags[i] > 0 for i in range(4)]
    spread = spread_matrix()
    zero = jnp.zeros((128, L), BF)
    for t in range(6):
        at = slice(t * L, (t + 1) * L)
        rows = jnp.concatenate(
            [jnp.where(f[0], lo[:, at], zero), own[:, at], jnp.where(f[1], hi[:, at], zero)], axis=0
        )
        g2[:, 2 * t * L : (2 * t + 2) * L] = dot(rows, spread).astype(BF)
    lane = iota((64, L), 1)
    for t in range(5):
        acc = None
        for j in range(3):
            term = dot(weight[j], g2[:, (2 * t + j) * L : (2 * t + j + 2) * L])
            acc = term if acc is None else acc + term
        for m, gp in enumerate(combine(acc, 64, 2, 2, lane)):
            m = 2 * t + m
            add = gp * 0.125
            for n in (2 * m - 1, 2 * m):
                if not 0 <= n < 18:
                    continue
                for x in range(2):
                    cot = fc_lo[x] if n == 0 else fc_hi[x] if n == 17 else fc[x, n - 1]
                    val = (cot.astype(F32) + add) * slope[x * 64 : (x + 1) * 64, n * L : (n + 1) * L]
                    if n == 0 or n == 17:
                        val = jnp.where(f[2] if n == 0 else f[3], val, 0.0)
                    gpf[x, n] = val.astype(BF)


def fine_corr_kernel(scale, v2, gpf, out, u3):
    lane = iota((64, L), 1)
    for y in range(16):
        at = slice(y * L, (y + 1) * L)
        for x in range(2):
            tile = gpf[x, y + 1].astype(F32)
            u3[x * 64 : x * 64 + 64, at] = shifted(tile, -1, lane).astype(BF)
            u3[128 + x * 64 : 192 + x * 64, at] = gpf[x, y + 1]
            u3[256 + x * 64 : 320 + x * 64, at] = shifted(tile, 1, lane).astype(BF)
    lane = iota((96, L), 1)
    for j in range(3):
        res = nt(v2[:, (YH - 1 + j) * L : (YH + 15 + j) * L], u3[...]) * scale
        for k in range(3):
            part = res[:, k * L : (k + 1) * L]
            both = part[:192] + pltpu.roll(part[64:], 64, 1)
            packed = jnp.where(lane < 64, both[:96], pltpu.roll(both[96:], 64, 1))
            at = (3 * j + k) * 96
            out[at : at + 96, :] = packed.astype(BF)


def input_grad_kernel(flags, own, lo, hi, weight, out, g2):
    f = [flags[i] > 0 for i in range(4)]
    for y in range(18):
        at = slice(y * L, (y + 1) * L)
        zero = jnp.zeros((64, L), BF)
        g2[0:64, at] = jnp.where(f[0], lo[0, y], zero)
        g2[64:128, at] = own[0, y]
        g2[128:192, at] = own[1, y]
        g2[192:256, at] = jnp.where(f[1], hi[0, y], zero)
    lane = iota((128, L), 1)
    for t in range(4):
        acc = None
        for j in range(3):
            term = dot(weight[j], g2[:, (4 * t + j) * L : (4 * t + j + 4) * L])
            acc = term if acc is None else acc + term
        for n, val in enumerate(combine(acc, 128, 4, 1, lane)):
            val = val.astype(BF)
            out[0, 4 * t + n] = val[:64]
            out[1, 4 * t + n] = val[64:]


def sum_kernel(parts, out):
    total = parts[0].astype(F32)
    for n in range(1, 128):
        total = total + parts[n].astype(F32)
    total = total.astype(BF)
    for n in range(128):
        out[n] = total


def unpack_kernel(got, fine, coarse):
    for j in range(3):
        for k in range(3):
            at = (3 * j + k) * 192
            for i in range(3):
                coarse[i, j, k] = got[at + i * 64 : at + (i + 1) * 64, :].astype(F32)
            at = FINE_AT + (3 * j + k) * 96
            tile = got[at : at + 96, :].astype(F32)
            fine[0, j, k] = tile[:64, :64]
            fine[1, j, k, :32] = tile[64:, :64]
            fine[1, j, k, 32:] = tile[:32, 64:]
            fine[2, j, k] = tile[32:, 64:]


def call(kernel, name, outs, args, scratch=(), flags=True, macs=0):
    specs = [pl.BlockSpec(memory_space=pltpu.VMEM) for _ in args]
    if flags:
        specs[0] = pl.BlockSpec(memory_space=pltpu.SMEM)
    moved = sum(a.size * a.dtype.itemsize for a in args)
    many = isinstance(outs[0][0], tuple)
    shapes = tuple(jax.ShapeDtypeStruct(*o) for o in (outs if many else (outs,)))
    return pl.pallas_call(
        kernel,
        out_shape=shapes if many else shapes[0],
        in_specs=specs,
        out_specs=tuple(pl.BlockSpec(memory_space=pltpu.VMEM) for _ in shapes)
        if many
        else pl.BlockSpec(memory_space=pltpu.VMEM),
        scratch_shapes=list(scratch),
        compiler_params=pltpu.CompilerParams(vmem_limit_bytes=VMEM),
        cost_estimate=pl.CostEstimate(flops=2 * macs, bytes_accessed=moved, transcendentals=0),
        name=name,
    )(*args)


def both_ways(low, high, axis):
    count = lax.axis_size(axis)
    ahead = [(i, (i + 1) % count) for i in range(count)]
    back = [(i, (i - 1) % count) for i in range(count)]
    return lax.ppermute(high, axis, ahead), lax.ppermute(low, axis, back)


def banded(weight):
    both = [jnp.pad(weight, ((x, 1 - x),) + ((0, 0),) * 4) for x in range(2)]
    full = jnp.stack(both)
    full = jnp.transpose(full, (2, 3, 0, 4, 1, 5))
    return full.reshape(3, 3 * 2 * weight.shape[3], 4 * weight.shape[4])


def stacked(weight):
    full = jnp.transpose(weight, (1, 2, 3, 0, 4))
    return full.reshape(3, 3 * weight.shape[3], 3 * weight.shape[4])


def on_device(inputs, fine_cot, coarse_cot, weight_fine, weight_coarse):
    slab, sub = lax.axis_index("slab"), lax.axis_index("sub")
    flags = jnp.stack([slab > 0, slab < 31, sub > 0, sub < 3]).astype(jnp.int32)
    w_fwd = banded(jnp.swapaxes(weight_fine, 3, 4))
    w_bwd = banded(jnp.flip(weight_fine, (0, 1, 2)))
    c_fwd = stacked(jnp.swapaxes(weight_coarse, 3, 4))
    c_bwd = stacked(jnp.flip(weight_coarse, (0, 1, 2)))

    xlo, xhi = both_ways(inputs[:1], inputs[1:], "slab")

    def edge(cols, n, cc):
        at = slice(0, cols) if n == 0 else slice(16 - cols, 16)
        one = slice(0, 1) if n == 0 else slice(15, 16)
        pieces = [a[:, at] for a in (xlo, inputs, xhi)] + [
            fine_cot[:, one].reshape(1, 2, 64, 128)
        ]
        pieces = [p.reshape(-1, 64, 128) for p in pieces]
        two = jnp.concatenate([coarse_cot[0, cc], coarse_cot[0, cc + 1]], axis=1)
        return jnp.concatenate(pieces + [two.reshape(2, 64, 128)], axis=0)

    got_lo, got_hi = both_ways(edge(YH, 0, 0), edge(YH, 1, 6), "sub")

    def parts(got):
        n = 4 * YH
        return got[:n].reshape(4, YH, 64, 128), got[n : n + 2], got[n + 2 :].reshape(128, 128)

    ylo, fc_lo, cc_lo = parts(got_lo)
    yhi, fc_hi, cc_hi = parts(got_hi)

    v2, slope, pooled = call(
        fine_kernel,
        "fine_forward",
        (((256, 30 * L), BF), ((128, 18 * L), F32), ((64, 7 * L), BF)),
        (flags, inputs, xlo, xhi, ylo, yhi, w_fwd),
        macs=384 * 256 * 3584 * 3,
    )
    plo, phi = both_ways(pooled, pooled, "slab")
    p2, gpc, gpack = call(
        coarse_kernel,
        "coarse_forward",
        (((192, 14 * L), BF), ((128, 12 * L), BF), ((128, 6 * L), BF)),
        (flags, pooled, plo, phi, cc_lo, coarse_cot[0], cc_hi, c_fwd),
        macs=384 * 192 * 1536 * 3,
    )
    glo, ghi = both_ways(gpack, gpack, "slab")
    coarse_part = call(
        functools.partial(coarse_corr_kernel, 1.0 / 256.0),
        "coarse_correlate",
        ((1728, L), BF),
        (p2, gpc),
        scratch=[pltpu.VMEM((384, 8 * L), BF)],
        flags=False,
        macs=384 * 192 * 1024 * 3,
    )
    gpf = call(
        gpf_kernel,
        "fine_gradient",
        ((2, 18, 64, L), BF),
        (flags, gpack, glo, ghi, c_bwd, fine_cot, fc_lo, fc_hi, slope),
        scratch=[pltpu.VMEM((384, 12 * L), BF)],
        macs=384 * 192 * 1280 * 3,
    )
    fine_part = call(
        functools.partial(fine_corr_kernel, 524288.0**-0.5),
        "fine_correlate",
        ((864, L), BF),
        (v2, gpf),
        scratch=[pltpu.VMEM((384, 16 * L), BF)],
        flags=False,
        macs=384 * 256 * 2048 * 3,
    )
    mine = jnp.concatenate(
        [coarse_part, fine_part, jnp.zeros((128 * ROWS - 2592, L), BF)], axis=0
    )
    shares = lax.all_to_all(mine, ("slab", "sub"), 0, 0, tiled=True)
    total = call(
        sum_kernel, "sum_shares", ((128, ROWS, L), BF), (shares.reshape(128, ROWS, L),), flags=False
    )
    hlo, hhi = both_ways(gpf[:1], gpf[1:], "slab")
    everything = lax.all_to_all(total.reshape(128 * ROWS, L), ("slab", "sub"), 0, 0, tiled=True)
    grad_fine, grad_coarse = call(
        unpack_kernel,
        "unpack",
        (((3, 3, 3, 64, 64), F32), ((3, 3, 3, 64, 128), F32)),
        (everything,),
        flags=False,
    )
    grad_input = call(
        input_grad_kernel,
        "input_gradient",
        ((2, 16, 64, L), BF),
        (flags, gpf, hlo, hhi, w_bwd),
        scratch=[pltpu.VMEM((256, 18 * L), BF)],
        macs=384 * 256 * 2048 * 3,
    )
    return (grad_input, grad_fine, grad_coarse)


def solution(mesh):
    in_specs = (
        P("slab", "sub", None, None),
        P("slab", "sub", None, None),
        P("slab", "sub", None, None),
        P(),
        P(),
    )
    out_specs = (P("slab", "sub", None, None), P(), P())
    return jax.shard_map(
        on_device, mesh=mesh, in_specs=in_specs, out_specs=out_specs, check_vma=False
    )
```

```python
import functools

import jax
import jax.numpy as jnp
from jax import lax
from jax.experimental import pallas as pl
from jax.experimental.pallas import tpu as pltpu
from jax.sharding import PartitionSpec as P

L = 128
YH = 7
BF = jnp.bfloat16
F32 = jnp.float32
ROWS = 24
FINE_AT = 1728
VMEM = 20 * 1024 * 1024


def iota(shape, dim):
    return lax.broadcasted_iota(jnp.int32, shape, dim)


def shifted(tile, by, lane):
    out = pltpu.roll(tile, by % L, 1)
    keep = lane >= by if by > 0 else lane < L + by
    return jnp.where(keep, out, 0.0)


def combine(acc, rows, tiles, step, lane):
    out = []
    for t in range(tiles):
        part = acc[:, t * L : (t + 1) * L]
        out.append(
            shifted(part[:rows], step, lane)
            + part[rows : 2 * rows]
            + shifted(part[2 * rows :], -step, lane)
        )
    return out


def slopes(value):
    sig = jax.nn.sigmoid(value)
    return sig, sig * (1.0 + value * (1.0 - sig))


def dot(a, b):
    return jnp.dot(a, b, preferred_element_type=F32)


def spread_matrix():
    row, col = iota((L, 2 * L), 0), iota((L, 2 * L), 1)
    return jnp.where(row == (col // L) * 64 + (col % L) // 2, 1.0, 0.0).astype(BF)


def take(ok, tile):
    return tile if ok is None else jnp.where(ok, tile, jnp.zeros_like(tile))


def pool_matrix():
    row, col = iota((1024, L), 0), iota((1024, L), 1)
    return jnp.where(col == ((row // 256) % 2) * 64 + (row % L) // 2, 1.0, 0.0).astype(BF)


def taps(ref, at, tiles):
    return jnp.concatenate([ref[:, (at + j) * L : (at + j + tiles) * L] for j in range(3)], axis=0)


def forward_chunk(weight, window, at, lane, pool):
    acc = dot(weight[...], taps(window, at, 4))
    acts, slopes_ = [], []
    for pre in combine(acc, 128, 4, 1, lane):
        sig, slp = slopes(pre)
        acts.append((pre * sig).astype(BF))
        slopes_.append(slp)
    cells = jnp.concatenate([a[:64] for a in acts] + [a[64:] for a in acts], axis=1)
    return slopes_, dot(cells, pool) * 0.125


def prepare_kernel(wf, wc, wfwd, wbwd, cfwd, cbwd):
    def fine(i, j, k):
        return wf[i, j, k] if 0 <= i < 3 else jnp.zeros((64, 64), BF)

    for j in range(3):
        for k in range(3):
            for x in range(2):
                rows = slice(k * 128 + x * 64, k * 128 + x * 64 + 64)
                for h in range(2):
                    i = 2 * h - x
                    cols = slice(j * 256 + h * L, j * 256 + (h + 1) * L)
                    pair = jnp.concatenate([fine(i, j, k), fine(i + 1, j, k)], axis=0)
                    wfwd[rows, cols] = pair.astype(F32).T.astype(BF)
                    wbwd[rows, cols] = jnp.concatenate(
                        [fine(2 - i, 2 - j, 2 - k), fine(1 - i, 2 - j, 2 - k)], axis=1
                    )
    for k in range(3):
        full = jnp.concatenate([wc[i, j, k] for j in range(3) for i in range(3)], axis=0)
        cfwd[k * 128 : (k + 1) * 128, :] = full.astype(F32).T.astype(BF)
        for j in range(3):
            for i in range(3):
                at = (3 * j + i) * L
                cbwd[k * 64 : (k + 1) * 64, at : at + L] = wc[2 - i, 2 - j, 2 - k]


def start_and_wait(pairs, sems):
    copies = [pltpu.make_async_copy(a, b, sems.at[n]) for n, (a, b) in enumerate(pairs)]
    for c in copies:
        c.start()
    for c in copies:
        c.wait()


def own_edges_kernel(own, fc, cot, low, high, sems):
    pairs = []
    for out, y, one, cc in ((low, 0, 0, 0), (high, 16 - YH, 15, 6)):
        for x in range(2):
            pairs.append((own.at[x, y : y + YH], out.at[x * YH : (x + 1) * YH]))
            pairs.append((fc.at[x, one : one + 1], out.at[2 * YH + x : 2 * YH + x + 1]))
        pairs.append((cot.at[cc : cc + 2], out.at[2 * YH + 2 : 2 * YH + 4]))
    start_and_wait(pairs, sems)


def corner_edges_kernel(xlo, xhi, low, high, sems):
    pairs = []
    for out, y in ((low, 0), (high, 16 - YH)):
        pairs.append((xlo.at[0, y : y + YH], out.at[0:YH]))
        pairs.append((xhi.at[0, y : y + YH], out.at[YH : 2 * YH]))
    start_and_wait(pairs, sems)


def interior_kernel(flags, own, xlo, xhi, weight, v2, slope, pooled):
    f = [flags[i] > 0 for i in range(2)]
    for y in range(16):
        at = slice(y * L, (y + 1) * L)
        v2[0:64, at] = take(f[0], xlo[0, y])
        v2[64:128, at] = own[0, y]
        v2[128:192, at] = own[1, y]
        v2[192:256, at] = take(f[1], xhi[0, y])
    lane, pool = iota((128, L), 1), pool_matrix()
    for t in range(3):
        slps, mean = forward_chunk(weight, v2, 4 * t + 1, lane, pool)
        for n in range(4):
            slope[:, (4 * t + n) * L : (4 * t + n + 1) * L] = slps[n]
        pooled[:, t * L : (t + 1) * L] = mean.astype(BF)


def border_kernel(
    flags, v2, mid, alo, ahi, blo, bhi, weight, slope_lo, slope_hi, pooled, vedge, window
):
    f = [flags[i] > 0 for i in range(4)]
    lane, lane64, pool = iota((128, L), 1), iota((64, L), 1), pool_matrix()
    pooled[:, 2 * L : 5 * L] = mid[...]
    for side, (a, b, ok) in enumerate(((alo, blo, f[2]), (ahi, bhi, f[3]))):
        win = window.at[side]
        first = 0 if side == 0 else 3
        for y in range(YH):
            at = slice((first + y) * L, (first + y + 1) * L)
            win[0:64, at] = take(ok & f[0], b[y])
            win[64:128, at] = take(ok, a[y])
            win[128:192, at] = take(ok, a[YH + y])
            win[192:256, at] = take(ok & f[1], b[YH + y])
        if side == 0:
            win[:, YH * L :] = v2[:, : 3 * L]
            vedge[:, :L] = win[:, 6 * L : 7 * L]
        else:
            win[:, : 3 * L] = v2[:, 13 * L :]
            vedge[:, L:] = win[:, 3 * L : 4 * L]
        for u in range(2):
            slps, mean = forward_chunk(weight, win, 4 * u, lane, pool)
            if side == 0 and u == 1:
                for n in range(3):
                    slope_lo[:, n * L : (n + 1) * L] = slps[n + 1]
            if side == 1 and u == 0:
                for n in range(3):
                    slope_hi[:, n * L : (n + 1) * L] = slps[n]
            t = u if side == 0 else 5 + u
            yc = 2 * t + lane64 // 64
            keep = ((yc >= 3) | f[2]) & ((yc < 11) | f[3])
            pooled[:, t * L : (t + 1) * L] = jnp.where(keep, mean, 0.0).astype(BF)


def spread_rows(f, lo, own, hi, tiles, out):
    rows = []
    for t in range(tiles):
        at = slice(t * L, (t + 1) * L)
        rows += [take(f[0], lo[:, at]), own[:, at], take(f[1], hi[:, at])]
    full = dot(jnp.concatenate(rows, axis=0), spread_matrix()).astype(BF)
    n = full.shape[0] // tiles
    for t in range(tiles):
        out[:, 2 * t * L : (2 * t + 2) * L] = full[t * n : (t + 1) * n]


def coarse_kernel(flags, own, lo, hi, alo, cot, ahi, weight, p2, gpc, gpack):
    f = [flags[i] > 0 for i in range(4)]
    spread_rows(f, lo, own, hi, 7, p2)
    lane = iota((128, L), 1)
    row, col = iota((2 * L, L), 0), iota((2 * L, L), 1)
    pack = jnp.where(
        (row % 2 == 0) & (col == (row // L) * 64 + (row % L) // 2), 1.0, 0.0
    ).astype(BF)
    at = 2 * YH + 2
    tiles = (
        [take(f[2], alo[at + n]) for n in range(2)]
        + [cot[n] for n in range(8)]
        + [take(f[3], ahi[at + n]) for n in range(2)]
    )
    cc = lax.dot_general(
        jnp.concatenate(tiles, axis=1),
        spread_matrix()[:64, :L],
        (((0,), (0,)), ((), ())),
        preferred_element_type=F32,
    )
    acc = dot(weight[...], taps(p2, 0, 12))
    out = []
    for n, pre in enumerate(combine(acc, 128, 12, 2, lane)):
        _, slp = slopes(pre)
        out.append((cc[n * L : (n + 1) * L] * slp).astype(BF))
        gpc[:, n * L : (n + 1) * L] = out[n]
    pairs = jnp.concatenate(
        [jnp.concatenate(out[2 * t : 2 * t + 2], axis=1) for t in range(6)], axis=0
    )
    packed = dot(pairs, pack).astype(BF)
    for t in range(6):
        gpack[:, t * L : (t + 1) * L] = packed[t * L : (t + 1) * L]


def nt(a, b):
    return lax.dot_general(a, b, (((1,), (1,)), ((), ())), preferred_element_type=F32)


def coarse_corr_kernel(scale, p2, gpc, out, g3):
    lane = iota((128, L), 1)
    for y in range(8):
        tile = gpc[:, (2 + y) * L : (3 + y) * L].astype(F32)
        at = slice(y * L, (y + 1) * L)
        g3[0:128, at] = shifted(tile, -2, lane).astype(BF)
        g3[128:256, at] = tile.astype(BF)
        g3[256:384, at] = shifted(tile, 2, lane).astype(BF)
    res = nt(taps(p2, 2, 8), g3[...]) * (0.5 * scale)
    for j in range(3):
        for k in range(3):
            at = (3 * j + k) * 192
            out[at : at + 192, :] = res[j * 192 : (j + 1) * 192, k * L : (k + 1) * L].astype(BF)


def gpf_kernel(flags, own, lo, hi, weight, fc, alo, ahi, slope_lo, slope, slope_hi, row0, row1, g2):
    f = [flags[i] > 0 for i in range(4)]
    spread_rows(f, lo, own, hi, 6, g2)
    lane = iota((64, L), 1)
    acc = dot(weight[...], taps(g2, 0, 10))
    for m, gp in enumerate(combine(acc, 64, 10, 2, lane)):
        add = gp * 0.125
        for n in (2 * m - 1, 2 * m):
            if not 0 <= n < 18:
                continue
            if n < 3:
                slp = slope_lo[:, n * L : (n + 1) * L]
            elif n < 15:
                slp = slope[:, (n - 3) * L : (n - 2) * L]
            else:
                slp = slope_hi[:, (n - 15) * L : (n - 14) * L]
            for x, out in enumerate((row0, row1)):
                edge = 2 * YH + x
                cot = alo[edge] if n == 0 else ahi[edge] if n == 17 else fc[x, n - 1]
                val = (cot.astype(F32) + add) * slp[x * 64 : (x + 1) * 64]
                if n == 0 or n == 17:
                    val = take(f[2] if n == 0 else f[3], val)
                out[n] = val.astype(BF)


def fine_corr_kernel(scale, v2, vedge, row0, row1, coarse, out, u3):
    lane = iota((64, L), 1)
    for y in range(16):
        at = slice(y * L, (y + 1) * L)
        for x, row in enumerate((row0, row1)):
            tile = row[y + 1].astype(F32)
            u3[x * 64 : x * 64 + 64, at] = shifted(tile, -1, lane).astype(BF)
            u3[128 + x * 64 : 192 + x * 64, at] = row[y + 1]
            u3[256 + x * 64 : 320 + x * 64, at] = shifted(tile, 1, lane).astype(BF)
    lane = iota((96, L), 1)
    lhs = jnp.concatenate(
        [
            jnp.concatenate([vedge[:, :L], v2[:, : 15 * L]], axis=1),
            v2[...],
            jnp.concatenate([v2[:, L:], vedge[:, L:]], axis=1),
        ],
        axis=0,
    )
    res = nt(lhs, u3[...]) * scale
    out[:FINE_AT, :] = coarse[...]
    out[2592:, :] = jnp.zeros((128 * ROWS - 2592, L), BF)
    for j in range(3):
        for k in range(3):
            part = res[j * 256 : (j + 1) * 256, k * L : (k + 1) * L]
            both = part[:192] + pltpu.roll(part[64:], 64, 1)
            packed = jnp.where(lane < 64, both[:96], pltpu.roll(both[96:], 64, 1))
            at = FINE_AT + (3 * j + k) * 96
            out[at : at + 96, :] = packed.astype(BF)


def input_grad_kernel(flags, row0, row1, lo, hi, weight, out, g2):
    f = [flags[i] > 0 for i in range(4)]
    for y in range(18):
        at = slice(y * L, (y + 1) * L)
        g2[0:64, at] = take(f[0], lo[y])
        g2[64:128, at] = row0[y]
        g2[128:192, at] = row1[y]
        g2[192:256, at] = take(f[1], hi[y])
    lane = iota((128, L), 1)
    for t in range(4):
        acc = dot(weight[...], taps(g2, 4 * t, 4))
        for n, val in enumerate(combine(acc, 128, 4, 1, lane)):
            val = val.astype(BF)
            out[0, 4 * t + n] = val[:64]
            out[1, 4 * t + n] = val[64:]


def sum_kernel(parts, out):
    total = parts[0].astype(F32)
    for n in range(1, 128):
        total = total + parts[n].astype(F32)
    total = total.astype(BF)
    for n in range(128):
        out[n] = total


def unpack_kernel(got, fine, coarse):
    for j in range(3):
        for k in range(3):
            at = (3 * j + k) * 192
            for i in range(3):
                coarse[i, j, k] = got[at + i * 64 : at + (i + 1) * 64, :].astype(F32)
            at = FINE_AT + (3 * j + k) * 96
            tile = got[at : at + 96, :].astype(F32)
            fine[0, j, k] = tile[:64, :64]
            fine[1, j, k, :32] = tile[64:, :64]
            fine[1, j, k, 32:] = tile[:32, 64:]
            fine[2, j, k] = tile[32:, 64:]


def call(kernel, name, outs, args, scratch=(), flags=True, macs=0, copies=0):
    space = pl.ANY if copies else pltpu.VMEM
    specs = [pl.BlockSpec(memory_space=space) for _ in args]
    if flags:
        specs[0] = pl.BlockSpec(memory_space=pltpu.SMEM)
    moved = sum(a.size * a.dtype.itemsize for a in args)
    shapes = tuple(jax.ShapeDtypeStruct(*o) for o in outs)
    if copies:
        scratch = [pltpu.SemaphoreType.DMA((copies,))]
    got = pl.pallas_call(
        kernel,
        out_shape=shapes,
        in_specs=specs,
        out_specs=tuple(pl.BlockSpec(memory_space=space) for _ in shapes),
        scratch_shapes=list(scratch),
        compiler_params=pltpu.CompilerParams(vmem_limit_bytes=VMEM),
        cost_estimate=pl.CostEstimate(flops=2 * macs, bytes_accessed=moved, transcendentals=0),
        name=name,
    )(*args)
    return got if len(shapes) > 1 else got[0]


def both_ways(low, high, axis):
    count = lax.axis_size(axis)
    ahead = [(i, (i + 1) % count) for i in range(count)]
    back = [(i, (i - 1) % count) for i in range(count)]
    return lax.ppermute(high, axis, ahead), lax.ppermute(low, axis, back)


def on_device(inputs, fine_cot, coarse_cot, weight_fine, weight_coarse):
    slab, sub = lax.axis_index("slab"), lax.axis_index("sub")
    flags = jnp.stack([slab > 0, slab < 31, sub > 0, sub < 3]).astype(jnp.int32)
    cot = jnp.swapaxes(coarse_cot[0], 1, 2)

    xlo, xhi = both_ways(inputs[:1], inputs[1:], "slab")
    own_edge = ((2 * YH + 4, 64, L), BF)
    low, high = call(
        own_edges_kernel,
        "own_edges",
        (own_edge, own_edge),
        (inputs, fine_cot, cot),
        flags=False,
        copies=10,
    )
    alo, ahi = both_ways(low, high, "sub")
    w_fwd, w_bwd, c_fwd, c_bwd = call(
        prepare_kernel,
        "prepare_weights",
        (((384, 768), BF), ((384, 768), BF), ((384, 576), BF), ((192, 1152), BF)),
        (weight_fine, weight_coarse),
        flags=False,
    )
    corner = ((2 * YH, 64, L), BF)
    low, high = call(
        corner_edges_kernel, "corner_edges", (corner, corner), (xlo, xhi), flags=False, copies=4
    )
    blo, bhi = both_ways(low, high, "sub")
    v2, slope, mid = call(
        interior_kernel,
        "fine_forward_interior",
        (((256, 16 * L), BF), ((128, 12 * L), F32), ((64, 3 * L), BF)),
        (flags, inputs, xlo, xhi, w_fwd),
        macs=384 * 768 * 12 * L,
    )
    slope_lo, slope_hi, pooled, vedge = call(
        border_kernel,
        "fine_forward_border",
        (((128, 3 * L), F32), ((128, 3 * L), F32), ((64, 7 * L), BF), ((256, 2 * L), BF)),
        (flags, v2, mid, alo, ahi, blo, bhi, w_fwd),
        scratch=[pltpu.VMEM((2, 256, 10 * L), BF)],
        macs=384 * 768 * 16 * L,
    )
    plo, phi = both_ways(pooled, pooled, "slab")
    p2, gpc, gpack = call(
        coarse_kernel,
        "coarse_forward",
        (((192, 14 * L), BF), ((128, 12 * L), BF), ((128, 6 * L), BF)),
        (flags, pooled, plo, phi, alo, cot, ahi, c_fwd),
        macs=384 * 576 * 12 * L,
    )
    glo, ghi = both_ways(gpack, gpack, "slab")
    coarse_part = call(
        functools.partial(coarse_corr_kernel, 1.0 / 256.0),
        "coarse_correlate",
        (((FINE_AT, L), BF),),
        (p2, gpc),
        scratch=[pltpu.VMEM((384, 8 * L), BF)],
        flags=False,
        macs=384 * 576 * 8 * L,
    )
    row0, row1 = call(
        gpf_kernel,
        "fine_gradient",
        (((18, 64, L), BF), ((18, 64, L), BF)),
        (flags, gpack, glo, ghi, c_bwd, fine_cot, alo, ahi, slope_lo, slope, slope_hi),
        scratch=[pltpu.VMEM((384, 12 * L), BF)],
        macs=192 * 1152 * 10 * L,
    )
    hlo, hhi = both_ways(row0, row1, "slab")
    mine = call(
        functools.partial(fine_corr_kernel, 524288.0**-0.5),
        "fine_correlate",
        (((128 * ROWS, L), BF),),
        (v2, vedge, row0, row1, coarse_part),
        scratch=[pltpu.VMEM((384, 16 * L), BF)],
        flags=False,
        macs=384 * 768 * 16 * L,
    )
    shares = lax.all_to_all(mine, ("slab", "sub"), 0, 0, tiled=True)
    grad_input = call(
        input_grad_kernel,
        "input_gradient",
        (((2, 16, 64, L), BF),),
        (flags, row0, row1, hlo, hhi, w_bwd),
        scratch=[pltpu.VMEM((256, 18 * L), BF)],
        macs=384 * 768 * 16 * L,
    )
    shares, grad_input = lax.optimization_barrier((shares, grad_input))
    total = call(
        sum_kernel,
        "sum_shares",
        (((128, ROWS, L), BF),),
        (shares.reshape(128, ROWS, L),),
        flags=False,
    )
    everything = lax.all_to_all(total.reshape(128 * ROWS, L), ("slab", "sub"), 0, 0, tiled=True)
    grad_fine, grad_coarse = call(
        unpack_kernel,
        "unpack",
        (((3, 3, 3, 64, 64), F32), ((3, 3, 3, 64, 128), F32)),
        (everything,),
        flags=False,
    )
    return (grad_input, grad_fine, grad_coarse)


def solution(mesh):
    in_specs = (
        P("slab", "sub", None, None),
        P("slab", "sub", None, None),
        P("slab", "sub", None, None),
        P(),
        P(),
    )
    out_specs = (P("slab", "sub", None, None), P(), P())
    return jax.shard_map(
        on_device, mesh=mesh, in_specs=in_specs, out_specs=out_specs, check_vma=False
    )
```

```python
import functools

import jax
import jax.numpy as jnp
from jax import lax
from jax.experimental import pallas as pl
from jax.experimental.pallas import tpu as pltpu
from jax.sharding import PartitionSpec as P

L = 128
YH = 7
BF = jnp.bfloat16
F32 = jnp.float32
R = 8
HALF = 864
VMEM = 20 * 1024 * 1024


def iota(shape, dim):
    return lax.broadcasted_iota(jnp.int32, shape, dim)


def shifted(tile, by, lane):
    out = pltpu.roll(tile, by % L, 1)
    keep = lane >= by if by > 0 else lane < L + by
    return jnp.where(keep, out, 0.0)


def combine(acc, rows, tiles, step, lane):
    out = []
    for t in range(tiles):
        part = acc[:, t * L : (t + 1) * L]
        out.append(
            shifted(part[:rows], step, lane)
            + part[rows : 2 * rows]
            + shifted(part[2 * rows :], -step, lane)
        )
    return out


def slopes(value):
    sig = jax.nn.sigmoid(value)
    return sig, sig * (1.0 + value * (1.0 - sig))


def dot(a, b):
    return jnp.dot(a, b, preferred_element_type=F32)


def spread_matrix():
    row, col = iota((L, 2 * L), 0), iota((L, 2 * L), 1)
    return jnp.where(row == (col // L) * 64 + (col % L) // 2, 1.0, 0.0).astype(BF)


def pick(cond, a, b):
    return jnp.where(cond, a, b)


def take(ok, tile):
    return tile if ok is None else jnp.where(ok, tile, jnp.zeros_like(tile))


def pool_matrix():
    row, col = iota((1024, L), 0), iota((1024, L), 1)
    return jnp.where(col == ((row // 256) % 2) * 64 + (row % L) // 2, 1.0, 0.0).astype(BF)


def taps(ref, at, tiles):
    return jnp.concatenate([ref[:, (at + j) * L : (at + j + tiles) * L] for j in range(3)], axis=0)


def forward_chunk(weight, window, at, lane, pool):
    acc = dot(weight[...], taps(window, at, 4))
    acts, slopes_ = [], []
    for pre in combine(acc, 128, 4, 1, lane):
        sig, slp = slopes(pre)
        acts.append((pre * sig).astype(BF))
        slopes_.append(slp)
    cells = jnp.concatenate([a[:64] for a in acts] + [a[64:] for a in acts], axis=1)
    return slopes_, dot(cells, pool) * 0.125


def prepare_kernel(wf, wc, wfwd, wbwd, cfwd, cbwd):
    def fine(i, j, k):
        return wf[i, j, k] if 0 <= i < 3 else jnp.zeros((64, 64), BF)

    for j in range(3):
        for k in range(3):
            for x in range(2):
                rows = slice(k * 128 + x * 64, k * 128 + x * 64 + 64)
                for h in range(2):
                    i = 2 * h - x
                    cols = slice(j * 256 + h * L, j * 256 + (h + 1) * L)
                    pair = jnp.concatenate([fine(i, j, k), fine(i + 1, j, k)], axis=0)
                    wfwd[rows, cols] = pair.astype(F32).T.astype(BF)
                    wbwd[rows, cols] = jnp.concatenate(
                        [fine(2 - i, 2 - j, 2 - k), fine(1 - i, 2 - j, 2 - k)], axis=1
                    )
    for k in range(3):
        full = jnp.concatenate([wc[i, j, k] for j in range(3) for i in range(3)], axis=0)
        cfwd[k * 128 : (k + 1) * 128, :] = full.astype(F32).T.astype(BF)
        for j in range(3):
            for i in range(3):
                at = (3 * j + i) * L
                cbwd[k * 64 : (k + 1) * 64, at : at + L] = wc[2 - i, 2 - j, 2 - k]


def start_and_wait(pairs, sems):
    copies = [pltpu.make_async_copy(a, b, sems.at[n]) for n, (a, b) in enumerate(pairs)]
    for c in copies:
        c.start()
    for c in copies:
        c.wait()


def own_edges_kernel(flags, own, fc, cot, first, second, sems):
    pairs = []
    for out, up in ((first, flags[5]), (second, 1 - flags[5])):
        y, one, cc = up * (16 - YH), up * 15, up * 6
        for x in range(2):
            pairs.append((own.at[x, pl.ds(y, YH)], out.at[x * YH : (x + 1) * YH]))
            pairs.append((fc.at[x, pl.ds(one, 1)], out.at[2 * YH + x : 2 * YH + x + 1]))
        pairs.append((cot.at[pl.ds(cc, 2)], out.at[2 * YH + 2 : 2 * YH + 4]))
    start_and_wait(pairs, sems)


def corner_edges_kernel(flags, xa, xb, first, second, sems):
    pairs = []
    for out, up in ((first, flags[5]), (second, 1 - flags[5])):
        y = up * (16 - YH)
        pairs.append((xa.at[pl.ds(y, YH)], out.at[0:YH]))
        pairs.append((xb.at[pl.ds(y, YH)], out.at[YH : 2 * YH]))
    start_and_wait(pairs, sems)


def interior_kernel(flags, own, xa, xb, weight, v2, slope, pooled):
    f = [flags[i] > 0 for i in range(6)]
    for y in range(16):
        at = slice(y * L, (y + 1) * L)
        v2[0:64, at] = take(f[0], pick(f[4], xb[y], xa[y]))
        v2[64:128, at] = own[0, y]
        v2[128:192, at] = own[1, y]
        v2[192:256, at] = take(f[1], pick(f[4], xa[y], xb[y]))
    lane, pool = iota((128, L), 1), pool_matrix()
    for t in range(3):
        slps, mean = forward_chunk(weight, v2, 4 * t + 1, lane, pool)
        for n in range(4):
            slope[:, (4 * t + n) * L : (4 * t + n + 1) * L] = slps[n]
        pooled[:, t * L : (t + 1) * L] = mean.astype(BF)


def border_kernel(
    flags, v2, mid, aa, ab, ba, bb, weight, slope_lo, slope_hi, pooled, vedge, window
):
    f = [flags[i] > 0 for i in range(6)]
    lane, lane64, pool = iota((128, L), 1), iota((64, L), 1), pool_matrix()
    pooled[:, 2 * L : 5 * L] = mid[...]
    for side, ok in enumerate((f[2], f[3])):
        even = f[5] if side == 1 else jnp.logical_not(f[5])
        win = window.at[side]
        first = 0 if side == 0 else 3
        for y in range(YH):
            at = slice((first + y) * L, (first + y + 1) * L)
            xs = [pick(even, ba[n * YH + y], bb[n * YH + y]) for n in range(2)]
            win[0:64, at] = take(ok & f[0], pick(f[4], xs[1], xs[0]))
            win[64:128, at] = take(ok, pick(even, aa[y], ab[y]))
            win[128:192, at] = take(ok, pick(even, aa[YH + y], ab[YH + y]))
            win[192:256, at] = take(ok & f[1], pick(f[4], xs[0], xs[1]))
        if side == 0:
            win[:, YH * L :] = v2[:, : 3 * L]
            vedge[:, :L] = win[:, 6 * L : 7 * L]
        else:
            win[:, : 3 * L] = v2[:, 13 * L :]
            vedge[:, L:] = win[:, 3 * L : 4 * L]
        for u in range(2):
            slps, mean = forward_chunk(weight, win, 4 * u, lane, pool)
            if side == 0 and u == 1:
                for n in range(3):
                    slope_lo[:, n * L : (n + 1) * L] = slps[n + 1]
            if side == 1 and u == 0:
                for n in range(3):
                    slope_hi[:, n * L : (n + 1) * L] = slps[n]
            t = u if side == 0 else 5 + u
            yc = 2 * t + lane64 // 64
            keep = ((yc >= 3) | f[2]) & ((yc < 11) | f[3])
            pooled[:, t * L : (t + 1) * L] = jnp.where(keep, mean, 0.0).astype(BF)


def spread_rows(f, own, a, b, tiles, out):
    rows = []
    for t in range(tiles):
        at = slice(t * L, (t + 1) * L)
        lo, hi = pick(f[4], b[:, at], a[:, at]), pick(f[4], a[:, at], b[:, at])
        rows += [take(f[0], lo), own[:, at], take(f[1], hi)]
    full = dot(jnp.concatenate(rows, axis=0), spread_matrix()).astype(BF)
    n = full.shape[0] // tiles
    for t in range(tiles):
        out[:, 2 * t * L : (2 * t + 2) * L] = full[t * n : (t + 1) * n]


def coarse_kernel(flags, own, a, b, aa, cot, ab, weight, p2, gpc, gpack):
    f = [flags[i] > 0 for i in range(6)]
    spread_rows(f, own, a, b, 7, p2)
    lane = iota((128, L), 1)
    row, col = iota((2 * L, L), 0), iota((2 * L, L), 1)
    pack = jnp.where(
        (row % 2 == 0) & (col == (row // L) * 64 + (row % L) // 2), 1.0, 0.0
    ).astype(BF)
    at = 2 * YH + 2
    tiles = (
        [take(f[2], pick(f[5], ab[at + n], aa[at + n])) for n in range(2)]
        + [cot[n] for n in range(8)]
        + [take(f[3], pick(f[5], aa[at + n], ab[at + n])) for n in range(2)]
    )
    cc = lax.dot_general(
        jnp.concatenate(tiles, axis=1),
        spread_matrix()[:64, :L],
        (((0,), (0,)), ((), ())),
        preferred_element_type=F32,
    )
    acc = dot(weight[...], taps(p2, 0, 12))
    out = []
    for n, pre in enumerate(combine(acc, 128, 12, 2, lane)):
        _, slp = slopes(pre)
        out.append((cc[n * L : (n + 1) * L] * slp).astype(BF))
        gpc[:, n * L : (n + 1) * L] = out[n]
    pairs = jnp.concatenate(
        [jnp.concatenate(out[2 * t : 2 * t + 2], axis=1) for t in range(6)], axis=0
    )
    packed = dot(pairs, pack).astype(BF)
    for t in range(6):
        gpack[:, t * L : (t + 1) * L] = packed[t * L : (t + 1) * L]


def nt(a, b):
    return lax.dot_general(a, b, (((1,), (1,)), ((), ())), preferred_element_type=F32)


def coarse_corr_kernel(scale, flags, p2, gpc, kept, sent0, sent1, g3, out):
    lane = iota((128, L), 1)
    for y in range(8):
        tile = gpc[:, (2 + y) * L : (3 + y) * L].astype(F32)
        at = slice(y * L, (y + 1) * L)
        g3[0:128, at] = shifted(tile, -2, lane).astype(BF)
        g3[128:256, at] = tile.astype(BF)
        g3[256:384, at] = shifted(tile, 2, lane).astype(BF)
    res = nt(taps(p2, 2, 8), g3[...]) * (0.5 * scale)
    for j in range(3):
        for k in range(3):
            at = (3 * j + k) * 192
            out[at : at + 192, :] = res[j * 192 : (j + 1) * 192, k * L : (k + 1) * L].astype(BF)
    low, high = out[:HALF, :], out[HALF:, :]
    even = flags[5] > 0
    kept[...] = pick(even, low, high)
    sent0[...] = pick(even, high[: HALF // 2], low[: HALF // 2])
    sent1[...] = pick(even, high[HALF // 2 :], low[HALF // 2 :])


def turn_kernel(v2, vedge, vt):
    for y in range(18):
        tile = vedge[:, :L] if y == 0 else vedge[:, L:] if y == 17 else v2[:, (y - 1) * L : y * L]
        vt[y * L : (y + 1) * L, :] = tile.astype(F32).T.astype(BF)


def gpf_kernel(
    scale,
    flags,
    own,
    a,
    b,
    weight,
    fc,
    aa,
    ab,
    slope_lo,
    slope,
    slope_hi,
    vt,
    kept,
    got0,
    got1,
    first,
    second,
    mine,
    g2,
    u3,
    pack,
):
    f = [flags[i] > 0 for i in range(6)]
    spread_rows(f, own, a, b, 6, g2)
    lane = iota((64, L), 1)
    acc = dot(weight[...], taps(g2, 0, 10))
    for m, gp in enumerate(combine(acc, 64, 10, 2, lane)):
        add = gp * 0.125
        for n in (2 * m - 1, 2 * m):
            if not 0 <= n < 18:
                continue
            if n < 3:
                slp = slope_lo[:, n * L : (n + 1) * L]
            elif n < 15:
                slp = slope[:, (n - 3) * L : (n - 2) * L]
            else:
                slp = slope_hi[:, (n - 15) * L : (n - 14) * L]
            rows = []
            for x in range(2):
                edge = 2 * YH + x
                if n == 0:
                    cot = pick(f[5], ab[edge], aa[edge])
                elif n == 17:
                    cot = pick(f[5], aa[edge], ab[edge])
                else:
                    cot = fc[x, n - 1]
                val = (cot.astype(F32) + add) * slp[x * 64 : (x + 1) * 64]
                if n == 0 or n == 17:
                    val = take(f[2] if n == 0 else f[3], val)
                rows.append(val.astype(BF))
                if 0 < n < 17:
                    tile, at = rows[x].astype(F32), slice((n - 1) * L, n * L)
                    u3[x * 64 : x * 64 + 64, at] = shifted(tile, -1, lane).astype(BF)
                    u3[128 + x * 64 : 192 + x * 64, at] = rows[x]
                    u3[256 + x * 64 : 320 + x * 64, at] = shifted(tile, 1, lane).astype(BF)
            first[n] = pick(f[4], rows[1], rows[0])
            second[n] = pick(f[4], rows[0], rows[1])
    halves = []
    for j in range(3):
        res = dot(u3[...], vt[j * L : (j + 16) * L, :]) * scale
        for k in range(3):
            both = res[k * L : k * L + 64] + pltpu.roll(res[k * L + 64 : (k + 1) * L], 192, 1)
            at = (3 * j + k) * 64
            pack[at : at + 64, :] = both[:, :L]
            halves.append(both[:, L:])
    halves.append(jnp.zeros((64, L), F32))
    lane = iota((64, L), 1)
    for n in range(5):
        packed = jnp.where(lane < 64, halves[2 * n], pltpu.roll(halves[2 * n + 1], 64, 1))
        pack[576 + 64 * n : 640 + 64 * n, :] = packed
    got = jnp.concatenate([got0[...], got1[...]], axis=0)
    coarse = kept[...].astype(F32) + got.astype(F32)
    none = jnp.zeros((R, L), F32)
    for n in range(128):
        at = slice(n * R, (n + 1) * R)
        top = coarse[at] if n < HALF // R else none
        low = pack[at, :] if n < 896 // R else none
        mine[n] = jnp.concatenate([top, low], axis=0).astype(BF)


def input_grad_kernel(flags, first, second, a, b, weight, out, g2):
    f = [flags[i] > 0 for i in range(6)]
    for y in range(18):
        at = slice(y * L, (y + 1) * L)
        g2[0:64, at] = take(f[0], pick(f[4], b[y], a[y]))
        g2[64:128, at] = pick(f[4], second[y], first[y])
        g2[128:192, at] = pick(f[4], first[y], second[y])
        g2[192:256, at] = take(f[1], pick(f[4], a[y], b[y]))
    lane = iota((128, L), 1)
    for t in range(4):
        acc = dot(weight[...], taps(g2, 4 * t, 4))
        for n, val in enumerate(combine(acc, 128, 4, 1, lane)):
            val = val.astype(BF)
            out[0, 4 * t + n] = val[:64]
            out[1, 4 * t + n] = val[64:]


def sum_kernel(parts, out):
    sums = []
    for core in range(2):
        total = parts[core].astype(F32)
        for n in range(core + 2, 128, 2):
            total = total + parts[n].astype(F32)
        sums.append(total)
    total = jnp.concatenate([sums[0][:R], sums[1][:R], sums[0][R:] + sums[1][R:]], axis=0)
    total = total.astype(BF)
    for n in range(128):
        out[n] = total


def unpack_kernel(got, fine, coarse):
    def coarse_rows(q):
        half, at = q // (HALF // R), q % (HALF // R)
        return got[at].astype(F32)[half * R : (half + 1) * R]

    for j in range(3):
        for k in range(3):
            for i in range(3):
                q = ((3 * j + k) * 192 + i * 64) // R
                rows = [coarse_rows(q + m) for m in range(64 // R)]
                coarse[i, j, k] = jnp.concatenate(rows, axis=0)

    def tile(n):
        rows = [got[m].astype(F32)[2 * R :] for m in range(n * 64 // R, (n + 1) * 64 // R)]
        return jnp.concatenate(rows, axis=0).T

    for n in range(9):
        part = tile(n)
        fine[0, n // 3, n % 3] = part[:64]
        fine[1, n // 3, n % 3] = part[64:]
    for n in range(5):
        part = tile(9 + n)
        for h in range(2):
            at = 2 * n + h
            if at < 9:
                fine[2, at // 3, at % 3] = part[64 * h : 64 * h + 64]


def call(kernel, name, outs, args, scratch=(), flags=True, macs=0, copies=0):
    space = pl.ANY if copies else pltpu.VMEM
    specs = [pl.BlockSpec(memory_space=space) for _ in args]
    if flags:
        specs[0] = pl.BlockSpec(memory_space=pltpu.SMEM)
    moved = sum(a.size * a.dtype.itemsize for a in args)
    shapes = tuple(jax.ShapeDtypeStruct(*o) for o in outs)
    if copies:
        scratch = [pltpu.SemaphoreType.DMA((copies,))]
    got = pl.pallas_call(
        kernel,
        out_shape=shapes,
        in_specs=specs,
        out_specs=tuple(pl.BlockSpec(memory_space=space) for _ in shapes),
        scratch_shapes=list(scratch),
        compiler_params=pltpu.CompilerParams(vmem_limit_bytes=VMEM),
        cost_estimate=pl.CostEstimate(flops=2 * macs, bytes_accessed=moved, transcendentals=0),
        name=name,
    )(*args)
    return got if len(shapes) > 1 else got[0]


def swaps(first, second, axis):
    count = lax.axis_size(axis)
    pairs = [(i, i ^ 1) for i in range(count)]
    others = [(0, 0), (count - 1, count - 1)] + [(i, ((i - 1) ^ 1) + 1) for i in range(1, count - 1)]
    other = lax.ppermute(second, axis, others)
    return lax.ppermute(first, axis, pairs), other


def on_device(inputs, fine_cot, coarse_cot, weight_fine, weight_coarse):
    slab, sub = lax.axis_index("slab"), lax.axis_index("sub")
    flags = jnp.stack(
        [slab > 0, slab < 31, sub > 0, sub < 3, slab % 2 == 0, sub % 2 == 0]
    ).astype(jnp.int32)
    cot = jnp.swapaxes(coarse_cot[0], 1, 2)

    odd = slab % 2
    xa, xb = swaps(
        lax.dynamic_index_in_dim(inputs, 1 - odd, 0, False),
        lax.dynamic_index_in_dim(inputs, odd, 0, False),
        "slab",
    )
    own_edge = ((2 * YH + 4, 64, L), BF)
    first, second = call(
        own_edges_kernel,
        "own_edges",
        (own_edge, own_edge),
        (flags, inputs, fine_cot, cot),
        copies=10,
    )
    aa, ab = swaps(first, second, "sub")
    w_fwd, w_bwd, c_fwd, c_bwd = call(
        prepare_kernel,
        "prepare_weights",
        (((384, 768), BF), ((384, 768), BF), ((384, 576), BF), ((192, 1152), BF)),
        (weight_fine, weight_coarse),
        flags=False,
    )
    corner = ((2 * YH, 64, L), BF)
    first, second = call(
        corner_edges_kernel, "corner_edges", (corner, corner), (flags, xa, xb), copies=4
    )
    ba, bb = swaps(first, second, "sub")
    v2, slope, mid = call(
        interior_kernel,
        "fine_forward_interior",
        (((256, 16 * L), BF), ((128, 12 * L), F32), ((64, 3 * L), BF)),
        (flags, inputs, xa, xb, w_fwd),
        macs=384 * 768 * 12 * L,
    )
    slope_lo, slope_hi, pooled, vedge = call(
        border_kernel,
        "fine_forward_border",
        (((128, 3 * L), F32), ((128, 3 * L), F32), ((64, 7 * L), BF), ((256, 2 * L), BF)),
        (flags, v2, mid, aa, ab, ba, bb, w_fwd),
        scratch=[pltpu.VMEM((2, 256, 10 * L), BF)],
        macs=384 * 768 * 16 * L,
    )
    pa, pb = swaps(pooled, pooled, "slab")
    vt = call(
        turn_kernel, "turn_inputs", (((18 * L, 256), BF),), (v2, vedge), flags=False
    )
    p2, gpc, gpack = call(
        coarse_kernel,
        "coarse_forward",
        (((192, 14 * L), BF), ((128, 12 * L), BF), ((128, 6 * L), BF)),
        (flags, pooled, pa, pb, aa, cot, ab, c_fwd),
        macs=384 * 576 * 12 * L,
    )
    ga, gb = swaps(gpack, gpack, "slab")
    kept, *sent = call(
        functools.partial(coarse_corr_kernel, 1.0 / 256.0),
        "coarse_correlate",
        (((HALF, L), BF), ((HALF // 2, L), BF), ((HALF // 2, L), BF)),
        (flags, p2, gpc),
        scratch=[pltpu.VMEM((384, 8 * L), BF), pltpu.VMEM((2 * HALF, L), BF)],
        macs=384 * 576 * 8 * L,
    )
    got0, got1 = (lax.ppermute(part, "sub", [(0, 1), (1, 0), (2, 3), (3, 2)]) for part in sent)
    first, second, mine = call(
        functools.partial(gpf_kernel, 524288.0**-0.5),
        "fine_gradient",
        (((18, 64, L), BF), ((18, 64, L), BF), ((128, 2 * R, L), BF)),
        (
            flags,
            gpack,
            ga,
            gb,
            c_bwd,
            fine_cot,
            aa,
            ab,
            slope_lo,
            slope,
            slope_hi,
            vt,
            kept,
            got0,
            got1,
        ),
        scratch=[
            pltpu.VMEM((384, 12 * L), BF),
            pltpu.VMEM((384, 16 * L), BF),
            pltpu.VMEM((896, L), F32),
        ],
        macs=384 * 768 * 16 * L,
    )
    ha, hb = swaps(first, second, "slab")
    shares = lax.all_to_all(mine.reshape(128 * 2 * R, L), ("slab", "sub"), 0, 0, tiled=True)
    total = call(
        sum_kernel,
        "sum_shares",
        (((128, 3 * R, L), BF),),
        (shares.reshape(128, 2 * R, L),),
        flags=False,
    )
    everything = lax.all_to_all(total.reshape(128 * 3 * R, L), ("slab", "sub"), 0, 0, tiled=True)
    grad_input = call(
        input_grad_kernel,
        "input_gradient",
        (((2, 16, 64, L), BF),),
        (flags, first, second, ha, hb, w_bwd),
        scratch=[pltpu.VMEM((256, 18 * L), BF)],
        macs=20 * 384 * 768 * 16 * L,
    )
    grad_fine, grad_coarse = call(
        unpack_kernel,
        "unpack",
        (((3, 3, 3, 64, 64), F32), ((3, 3, 3, 64, 128), F32)),
        (everything.reshape(128, 3 * R, L),),
        flags=False,
    )
    return (grad_input, grad_fine, grad_coarse)


def solution(mesh):
    in_specs = (
        P("slab", "sub", None, None),
        P("slab", "sub", None, None),
        P("slab", "sub", None, None),
        P(),
        P(),
    )
    out_specs = (P("slab", "sub", None, None), P(), P())
    return jax.shard_map(
        on_device, mesh=mesh, in_specs=in_specs, out_specs=out_specs, check_vma=False
    )
```

```python
import functools

import jax
import jax.numpy as jnp
from jax import lax
from jax.experimental import pallas as pl
from jax.experimental.pallas import tpu as pltpu
from jax.sharding import PartitionSpec as P

L = 128
YH = 7
BF = jnp.bfloat16
F32 = jnp.float32
R = 8
HALF = 864
VMEM = 20 * 1024 * 1024


def iota(shape, dim):
    return lax.broadcasted_iota(jnp.int32, shape, dim)


def shifted(tile, by, lane, width=L):
    out = pltpu.roll(tile, by % L, 1)
    z = lane % width
    return jnp.where(z >= by if by > 0 else z < width + by, out, 0.0)


def combine(acc, rows, tiles, lane, width=L):
    out = []
    for t in range(tiles):
        part = acc[:, t * L : (t + 1) * L]
        out.append(
            shifted(part[:rows], 1, lane, width)
            + part[rows : 2 * rows]
            + shifted(part[2 * rows :], -1, lane, width)
        )
    return out


def slopes(value):
    sig = jax.nn.sigmoid(value)
    return sig, sig * (1.0 + value * (1.0 - sig))


def dot(a, b):
    return jnp.dot(a, b, preferred_element_type=F32)


def spread_matrix():
    row, col = iota((L, 2 * L), 0), iota((L, 2 * L), 1)
    return jnp.where(row == (col // L) * 64 + (col % L) // 2, 1.0, 0.0).astype(BF)


def pick(cond, a, b):
    return jnp.where(cond, a, b)


def take(ok, tile):
    return tile if ok is None else jnp.where(ok, tile, jnp.zeros_like(tile))


def pack_matrix():
    row, col = iota((2 * L, L), 0), iota((2 * L, L), 1)
    keep = (row % 2 == 0) & (col == (row // L) * 64 + (row % L) // 2)
    return jnp.where(keep, 1.0, 0.0).astype(BF)


def taps(ref, at, tiles):
    return jnp.concatenate([ref[:, (at + j) * L : (at + j + tiles) * L] for j in range(3)], axis=0)


def forward(weight, cells, tiles, lane):
    acc = dot(weight[...], cells)
    sums, slps = [], []
    for pre in combine(acc, 128, tiles, lane):
        sig, slp = slopes(pre)
        act = (pre * sig).astype(BF).astype(F32)
        sums.append(act[:64] + act[64:])
        slps.append(slp)
    means = []
    for t in range(0, tiles, 2):
        total = sums[t] + sums[t + 1]
        means.append(((total + pltpu.roll(total, L - 1, 1)) * 0.125).astype(BF))
    return slps, means


def prepare_kernel(wf, wc, wfwd, wbwd, cfwd, cown, cpart):
    def fine(i, j, k):
        return wf[i, j, k] if 0 <= i < 3 else jnp.zeros((64, 64), BF)

    for j in range(3):
        for k in range(3):
            for x in range(2):
                rows = slice(k * 128 + x * 64, k * 128 + x * 64 + 64)
                for h in range(2):
                    i = 2 * h - x
                    cols = slice(j * 256 + h * L, j * 256 + (h + 1) * L)
                    pair = jnp.concatenate([fine(i, j, k), fine(i + 1, j, k)], axis=0)
                    wfwd[rows, cols] = pair.astype(F32).T.astype(BF)
                    wbwd[rows, cols] = jnp.concatenate(
                        [fine(2 - i, 2 - j, 2 - k), fine(1 - i, 2 - j, 2 - k)], axis=1
                    )
    for k in range(3):
        full = jnp.concatenate([wc[i, j, k] for j in range(3) for i in range(3)], axis=0)
        cfwd[k * 128 : (k + 1) * 128, :] = full.astype(F32).T.astype(BF)
        for j in range(3):
            at = slice(j * L, (j + 1) * L)
            cown[k * 64 : (k + 1) * 64, at] = wc[1, 2 - j, 2 - k]
            cpart[k * 128 : k * 128 + 64, at] = wc[2, 2 - j, 2 - k]
            cpart[k * 128 + 64 : (k + 1) * 128, at] = wc[0, 2 - j, 2 - k]


def start_and_wait(pairs, sems):
    copies = [pltpu.make_async_copy(a, b, sems.at[n]) for n, (a, b) in enumerate(pairs)]
    for c in copies:
        c.start()
    for c in copies:
        c.wait()


def own_edges_kernel(flags, own, fc, cot, first, second, sems):
    pairs = []
    for out, up in ((first, flags[5]), (second, 1 - flags[5])):
        y, one, cc = up * (16 - YH), up * 15, up * 6
        for x in range(2):
            pairs.append((own.at[x, pl.ds(y, YH)], out.at[x * YH : (x + 1) * YH]))
            pairs.append((fc.at[x, pl.ds(one, 1)], out.at[2 * YH + x : 2 * YH + x + 1]))
        pairs.append((cot.at[pl.ds(cc, 2)], out.at[2 * YH + 2 : 2 * YH + 4]))
    start_and_wait(pairs, sems)


def corner_edges_kernel(flags, xa, xb, first, second):
    for out, up in ((first, flags[5]), (second, 1 - flags[5])):
        for n in range(YH):
            out[n] = xa[up * (16 - YH) + n]
            out[YH + n] = xb[up * (16 - YH) + n]


def interior_kernel(flags, own, xa, xb, weight, v2, slope, pooled):
    f = [flags[i] > 0 for i in range(6)]
    for y in range(16):
        at = slice(y * L, (y + 1) * L)
        v2[0:64, at] = take(f[0], pick(f[4], xb[y], xa[y]))
        v2[64:128, at] = own[0, y]
        v2[128:192, at] = own[1, y]
        v2[192:256, at] = take(f[1], pick(f[4], xa[y], xb[y]))
    lane = iota((128, L), 1)
    slps, means = forward(weight, taps(v2, 1, 12), 12, lane)
    for n in range(12):
        slope[:, n * L : (n + 1) * L] = slps[n]
    for t in range(6):
        pooled[:, t * L : (t + 1) * L] = means[t]


def border_kernel(
    flags, v2, mid, aa, ab, ba, bb, weight, slope_lo, slope_hi, pooled, vedge, window
):
    f = [flags[i] > 0 for i in range(6)]
    lane = iota((128, L), 1)
    for side, ok in enumerate((f[2], f[3])):
        even = f[5] if side == 1 else jnp.logical_not(f[5])
        win = window.at[side]
        first = 0 if side == 0 else 3
        for y in range(YH):
            at = slice((first + y) * L, (first + y + 1) * L)
            xs = [pick(even, ba[n * YH + y], bb[n * YH + y]) for n in range(2)]
            win[0:64, at] = take(ok & f[0], pick(f[4], xs[1], xs[0]))
            win[64:128, at] = take(ok, pick(even, aa[y], ab[y]))
            win[128:192, at] = take(ok, pick(even, aa[YH + y], ab[YH + y]))
            win[192:256, at] = take(ok & f[1], pick(f[4], xs[0], xs[1]))
        if side == 0:
            win[:, YH * L :] = v2[:, : 3 * L]
            vedge[:, :L] = win[:, 6 * L : 7 * L]
        else:
            win[:, : 3 * L] = v2[:, 13 * L :]
            vedge[:, L:] = win[:, 3 * L : 4 * L]
    both = jnp.concatenate([taps(window.at[side], 0, 8) for side in range(2)], axis=1)
    slps, means = forward(weight, both, 16, lane)
    for n in range(3):
        slope_lo[:, n * L : (n + 1) * L] = slps[5 + n]
        slope_hi[:, n * L : (n + 1) * L] = slps[8 + n]
    means = (
        [take(f[2], m) for m in means[:3]]
        + [means[3]]
        + [mid[:, t * L : (t + 1) * L] for t in range(6)]
        + [means[4]]
        + [take(f[3], m) for m in means[5:]]
    )
    rows = [jnp.concatenate([means[t], means[t + 6]], axis=1) for t in range(8)]
    packed = dot(jnp.concatenate(rows, axis=0), pack_matrix()).astype(BF)
    for t in range(8):
        pooled[:, t * L : (t + 1) * L] = packed[t * 64 : (t + 1) * 64]


def beside_kernel(flags, aa, cot, ab, v2, vedge, cc, vt):
    f = [flags[i] > 0 for i in range(6)]
    at = 2 * YH + 2
    tiles = (
        [take(f[2], pick(f[5], ab[at + n], aa[at + n])) for n in range(2)]
        + [cot[n] for n in range(8)]
        + [take(f[3], pick(f[5], aa[at + n], ab[at + n])) for n in range(2)]
    )
    for t in range(6):
        pair = jnp.concatenate([tiles[t], tiles[t + 6]], axis=0)
        cc[:, t * L : (t + 1) * L] = pair.astype(F32).T
    for y in range(18):
        tile = vedge[:, :L] if y == 0 else vedge[:, L:] if y == 17 else v2[:, (y - 1) * L : y * L]
        vt[y * L : (y + 1) * L, :] = tile.astype(F32).T.astype(BF)


def coarse_kernel(flags, own, a, b, cc, weight, w_part, p2, gpc, first, second):
    f = [flags[i] > 0 for i in range(6)]
    p2[0:64, :] = take(f[0], pick(f[4], b[...], a[...]))
    p2[64:128, :] = own[...]
    p2[128:192, :] = take(f[1], pick(f[4], a[...], b[...]))
    lane = iota((128, L), 1)
    acc = dot(weight[...], taps(p2, 0, 6))
    for t, pre in enumerate(combine(acc, 128, 6, lane, 64)):
        _, slp = slopes(pre)
        tile = (cc[:, t * L : (t + 1) * L] * slp).astype(BF)
        gpc[:, t * L : (t + 1) * L] = tile
        if t < 2:
            other = pltpu.roll(tile.astype(F32), 64, 1).astype(BF)
            gpc[:, (t + 6) * L : (t + 7) * L] = other
    acc = dot(w_part[...], taps(gpc, 0, 6))
    for t, val in enumerate(combine(acc, 128, 6, lane, 64)):
        at = slice(t * L, (t + 1) * L)
        val = val.astype(BF)
        first[:, at] = pick(f[4], val[:64], val[64:])
        second[:, at] = pick(f[4], val[64:], val[:64])


def nt(a, b):
    return lax.dot_general(a, b, (((1,), (1,)), ((), ())), preferred_element_type=F32)


def coarse_corr_kernel(scale, flags, p2, gpc, w_own, own, kept, sent0, sent1, sent2, g3, out):
    lane = iota((64, L), 1)
    acc = dot(w_own[...], taps(gpc, 0, 6))
    for t, val in enumerate(combine(acc, 64, 6, lane, 64)):
        own[:, t * L : (t + 1) * L] = val
    lane = iota((128, L), 1)
    for t in range(6):
        at = slice(t * L, (t + 1) * L)
        tile = gpc[:, at].astype(F32)
        if t < 2 or t > 3:
            tile = jnp.where(lane >= 64 if t < 2 else lane < 64, tile, 0.0)
        g3[0:128, at] = shifted(tile, -1, lane, 64).astype(BF)
        g3[128:256, at] = tile.astype(BF)
        g3[256:384, at] = shifted(tile, 1, lane, 64).astype(BF)
    res = nt(taps(p2, 0, 6), g3[...]) * scale
    for j in range(3):
        for k in range(3):
            at = (3 * j + k) * 192
            out[at : at + 192, :] = res[j * 192 : (j + 1) * 192, k * L : (k + 1) * L].astype(BF)
    low, high = out[:HALF, :], out[HALF:, :]
    even = flags[5] > 0
    kept[...] = pick(even, low, high)
    sent = pick(even, high, low)
    part = HALF // 3
    sent0[...], sent1[...], sent2[...] = sent[:part], sent[part : 2 * part], sent[2 * part :]


def gpf_kernel(
    scale,
    flags,
    own,
    a,
    b,
    fc,
    aa,
    ab,
    slope_lo,
    slope,
    slope_hi,
    vt,
    kept,
    got0,
    got1,
    got2,
    first,
    second,
    mine,
    u3,
    pack,
):
    f = [flags[i] > 0 for i in range(6)]
    lane = iota((64, L), 1)
    rows = []
    for t in range(6):
        at = slice(t * L, (t + 1) * L)
        lo, hi = pick(f[4], b[:, at], a[:, at]), pick(f[4], a[:, at], b[:, at])
        total = own[:, at] + take(f[0], lo).astype(F32) + take(f[1], hi).astype(F32)
        main = total.astype(BF)
        rest = (total - main.astype(F32)).astype(BF)
        rows.append(jnp.concatenate([main, rest], axis=1))
    spread = spread_matrix()
    full = dot(jnp.concatenate(rows, axis=0), jnp.concatenate([spread, spread], axis=0))
    gps = [full[64 * t : 64 * t + 64, :L] for t in range(6)]
    gps += [full[64 * t : 64 * t + 64, L:] for t in range(4)]
    for m, gp in enumerate(gps):
        add = gp * 0.125
        for n in (2 * m - 1, 2 * m):
            if not 0 <= n < 18:
                continue
            if n < 3:
                slp = slope_lo[:, n * L : (n + 1) * L]
            elif n < 15:
                slp = slope[:, (n - 3) * L : (n - 2) * L]
            else:
                slp = slope_hi[:, (n - 15) * L : (n - 14) * L]
            rows = []
            for x in range(2):
                edge = 2 * YH + x
                if n == 0:
                    cot = pick(f[5], ab[edge], aa[edge])
                elif n == 17:
                    cot = pick(f[5], aa[edge], ab[edge])
                else:
                    cot = fc[x, n - 1]
                val = (cot.astype(F32) + add) * slp[x * 64 : (x + 1) * 64]
                if n == 0 or n == 17:
                    val = take(f[2] if n == 0 else f[3], val)
                rows.append(val.astype(BF))
                if 0 < n < 17:
                    tile, at = rows[x].astype(F32), slice((n - 1) * L, n * L)
                    u3[x * 64 : x * 64 + 64, at] = shifted(tile, -1, lane).astype(BF)
                    u3[128 + x * 64 : 192 + x * 64, at] = rows[x]
                    u3[256 + x * 64 : 320 + x * 64, at] = shifted(tile, 1, lane).astype(BF)
            first[n] = pick(f[4], rows[1], rows[0])
            second[n] = pick(f[4], rows[0], rows[1])
    halves = []
    for j in range(3):
        res = dot(u3[...], vt[j * L : (j + 16) * L, :]) * scale
        for k in range(3):
            both = res[k * L : k * L + 64] + pltpu.roll(res[k * L + 64 : (k + 1) * L], 192, 1)
            at = (3 * j + k) * 64
            pack[at : at + 64, :] = both[:, :L]
            halves.append(both[:, L:])
    halves.append(jnp.zeros((64, L), F32))
    lane = iota((64, L), 1)
    for n in range(5):
        packed = jnp.where(lane < 64, halves[2 * n], pltpu.roll(halves[2 * n + 1], 64, 1))
        pack[576 + 64 * n : 640 + 64 * n, :] = packed
    got = jnp.concatenate([got0[...], got1[...], got2[...]], axis=0)
    coarse = kept[...].astype(F32) + got.astype(F32)
    none = jnp.zeros((R, L), F32)
    for n in range(128):
        at = slice(n * R, (n + 1) * R)
        top = coarse[at] if n < HALF // R else none
        low = pack[at, :] if n < 896 // R else none
        mine[n] = jnp.concatenate([top, low], axis=0).astype(BF)


def input_grad_kernel(flags, first, second, a, b, weight, out, g2):
    f = [flags[i] > 0 for i in range(6)]
    for y in range(18):
        at = slice(y * L, (y + 1) * L)
        g2[0:64, at] = take(f[0], pick(f[4], b[y], a[y]))
        g2[64:128, at] = pick(f[4], second[y], first[y])
        g2[128:192, at] = pick(f[4], first[y], second[y])
        g2[192:256, at] = take(f[1], pick(f[4], a[y], b[y]))
    lane = iota((128, L), 1)
    for t in range(4):
        acc = dot(weight[...], taps(g2, 4 * t, 4))
        for n, val in enumerate(combine(acc, 128, 4, lane)):
            val = val.astype(BF)
            out[0, 4 * t + n] = val[:64]
            out[1, 4 * t + n] = val[64:]


def sum_kernel(parts, out):
    sums = []
    for core in range(2):
        total = parts[core].astype(F32)
        for n in range(core + 2, 128, 2):
            total = total + parts[n].astype(F32)
        sums.append(total)
    total = jnp.concatenate([sums[0][:R], sums[1][:R], sums[0][R:] + sums[1][R:]], axis=0)
    total = total.astype(BF)
    for n in range(128):
        out[n] = total


def unpack_kernel(got, fine, coarse):
    def coarse_rows(q):
        half, at = q // (HALF // R), q % (HALF // R)
        return got[at].astype(F32)[half * R : (half + 1) * R]

    for j in range(3):
        for k in range(3):
            for i in range(3):
                q = ((3 * j + k) * 192 + i * 64) // R
                rows = [coarse_rows(q + m) for m in range(64 // R)]
                coarse[i, j, k] = jnp.concatenate(rows, axis=0)

    def tile(n):
        rows = [got[m].astype(F32)[2 * R :] for m in range(n * 64 // R, (n + 1) * 64 // R)]
        return jnp.concatenate(rows, axis=0).T

    for n in range(9):
        part = tile(n)
        fine[0, n // 3, n % 3] = part[:64]
        fine[1, n // 3, n % 3] = part[64:]
    for n in range(5):
        part = tile(9 + n)
        for h in range(2):
            at = 2 * n + h
            if at < 9:
                fine[2, at // 3, at % 3] = part[64 * h : 64 * h + 64]


def call(kernel, name, outs, args, scratch=(), flags=True, macs=0, copies=0):
    space = pl.ANY if copies else pltpu.VMEM
    specs = [pl.BlockSpec(memory_space=space) for _ in args]
    if flags:
        specs[0] = pl.BlockSpec(memory_space=pltpu.SMEM)
    moved = sum(a.size * a.dtype.itemsize for a in args)
    shapes = tuple(jax.ShapeDtypeStruct(*o) for o in outs)
    if copies:
        scratch = [pltpu.SemaphoreType.DMA((copies,))]
    got = pl.pallas_call(
        kernel,
        out_shape=shapes,
        in_specs=specs,
        out_specs=tuple(pl.BlockSpec(memory_space=space) for _ in shapes),
        scratch_shapes=list(scratch),
        compiler_params=pltpu.CompilerParams(vmem_limit_bytes=VMEM),
        cost_estimate=pl.CostEstimate(flops=2 * macs, bytes_accessed=moved, transcendentals=0),
        name=name,
    )(*args)
    return got if len(shapes) > 1 else got[0]


def swaps(first, second, axis):
    count = lax.axis_size(axis)
    pairs = [(i, i ^ 1) for i in range(count)]
    others = [(0, 0), (count - 1, count - 1)] + [(i, ((i - 1) ^ 1) + 1) for i in range(1, count - 1)]
    other = lax.ppermute(second, axis, others)
    return lax.ppermute(first, axis, pairs), other


def on_device(inputs, fine_cot, coarse_cot, weight_fine, weight_coarse):
    slab, sub = lax.axis_index("slab"), lax.axis_index("sub")
    flags = jnp.stack(
        [slab > 0, slab < 31, sub > 0, sub < 3, slab % 2 == 0, sub % 2 == 0]
    ).astype(jnp.int32)
    cot = jnp.swapaxes(coarse_cot[0], 1, 2)

    odd = slab % 2
    xa, xb = swaps(
        lax.dynamic_index_in_dim(inputs, 1 - odd, 0, False),
        lax.dynamic_index_in_dim(inputs, odd, 0, False),
        "slab",
    )
    own_edge = ((2 * YH + 4, 64, L), BF)
    first, second = call(
        own_edges_kernel,
        "own_edges",
        (own_edge, own_edge),
        (flags, inputs, fine_cot, cot),
        copies=10,
    )
    aa, ab = swaps(first, second, "sub")
    w_fwd, w_bwd, c_fwd, c_own, c_part = call(
        prepare_kernel,
        "prepare_weights",
        (
            ((384, 768), BF),
            ((384, 768), BF),
            ((384, 576), BF),
            ((192, 384), BF),
            ((384, 384), BF),
        ),
        (weight_fine, weight_coarse),
        flags=False,
    )
    corner = ((2 * YH, 64, L), BF)
    first, second = call(
        corner_edges_kernel, "corner_edges", (corner, corner), (flags, xa, xb)
    )
    ba, bb = swaps(first, second, "sub")
    v2, slope, mid = call(
        interior_kernel,
        "fine_forward_interior",
        (((256, 16 * L), BF), ((128, 12 * L), F32), ((64, 6 * L), BF)),
        (flags, inputs, xa, xb, w_fwd),
        macs=384 * 768 * 12 * L,
    )
    slope_lo, slope_hi, pooled, vedge = call(
        border_kernel,
        "fine_forward_border",
        (((128, 3 * L), F32), ((128, 3 * L), F32), ((64, 8 * L), BF), ((256, 2 * L), BF)),
        (flags, v2, mid, aa, ab, ba, bb, w_fwd),
        scratch=[pltpu.VMEM((2, 256, 10 * L), BF)],
        macs=384 * 768 * 16 * L,
    )
    pa, pb = swaps(pooled, pooled, "slab")
    cc, vt = call(
        beside_kernel,
        "cotangent_and_turned_inputs",
        (((128, 6 * L), F32), ((18 * L, 256), BF)),
        (flags, aa, cot, ab, v2, vedge),
    )
    p2, gpc, first, second = call(
        coarse_kernel,
        "coarse_forward",
        (
            ((192, 8 * L), BF),
            ((128, 8 * L), BF),
            ((64, 6 * L), BF),
            ((64, 6 * L), BF),
        ),
        (flags, pooled, pa, pb, cc, c_fwd, c_part),
        macs=384 * 960 * 6 * L,
    )
    ga, gb = swaps(first, second, "slab")
    third = ((HALF // 3, L), BF)
    own, kept, *sent = call(
        functools.partial(coarse_corr_kernel, 1.0 / 256.0),
        "coarse_correlate",
        (((64, 6 * L), F32), ((HALF, L), BF), third, third, third),
        (flags, p2, gpc, c_own),
        scratch=[pltpu.VMEM((384, 6 * L), BF), pltpu.VMEM((2 * HALF, L), BF)],
        macs=384 * 768 * 6 * L,
    )
    got0, got1, got2 = (lax.ppermute(part, "sub", [(0, 1), (1, 0), (2, 3), (3, 2)]) for part in sent)
    first, second, mine = call(
        functools.partial(gpf_kernel, 524288.0**-0.5),
        "fine_gradient",
        (((18, 64, L), BF), ((18, 64, L), BF), ((128, 2 * R, L), BF)),
        (
            flags,
            own,
            ga,
            gb,
            fine_cot,
            aa,
            ab,
            slope_lo,
            slope,
            slope_hi,
            vt,
            kept,
            got0,
            got1,
            got2,
        ),
        scratch=[
            pltpu.VMEM((384, 16 * L), BF),
            pltpu.VMEM((896, L), F32),
        ],
        macs=384 * 768 * 16 * L,
    )
    ha, hb = swaps(first, second, "slab")
    shares = lax.all_to_all(mine.reshape(128 * 2 * R, L), ("slab", "sub"), 0, 0, tiled=True)
    total = call(
        sum_kernel,
        "sum_shares",
        (((128, 3 * R, L), BF),),
        (shares.reshape(128, 2 * R, L),),
        flags=False,
    )
    everything = lax.all_to_all(total.reshape(128 * 3 * R, L), ("slab", "sub"), 0, 0, tiled=True)
    grad_input = call(
        input_grad_kernel,
        "input_gradient",
        (((2, 16, 64, L), BF),),
        (flags, first, second, ha, hb, w_bwd),
        scratch=[pltpu.VMEM((256, 18 * L), BF)],
        macs=20 * 384 * 768 * 16 * L,
    )
    grad_fine, grad_coarse = call(
        unpack_kernel,
        "unpack",
        (((3, 3, 3, 64, 64), F32), ((3, 3, 3, 64, 128), F32)),
        (everything.reshape(128, 3 * R, L),),
        flags=False,
    )
    return (grad_input, grad_fine, grad_coarse)


def solution(mesh):
    in_specs = (
        P("slab", "sub", None, None),
        P("slab", "sub", None, None),
        P("slab", "sub", None, None),
        P(),
        P(),
    )
    out_specs = (P("slab", "sub", None, None), P(), P())
    return jax.shard_map(
        on_device, mesh=mesh, in_specs=in_specs, out_specs=out_specs, check_vma=False
    )
```

```python
import functools

import jax
import jax.numpy as jnp
from jax import lax
from jax.experimental import pallas as pl
from jax.experimental.pallas import tpu as pltpu
from jax.sharding import PartitionSpec as P

L = 128
YH = 5
BF = jnp.bfloat16
F32 = jnp.float32
R = 8
HALF = 864
VMEM = 20 * 1024 * 1024


def iota(shape, dim):
    return lax.broadcasted_iota(jnp.int32, shape, dim)


def shifted(tile, by, lane, width=L):
    out = pltpu.roll(tile, by % L, 1)
    z = lane % width
    return jnp.where(z >= by if by > 0 else z < width + by, out, 0.0)


def combine(acc, rows, tiles, lane, width=L):
    out = []
    for t in range(tiles):
        part = acc[:, t * L : (t + 1) * L]
        out.append(
            shifted(part[:rows], 1, lane, width)
            + part[rows : 2 * rows]
            + shifted(part[2 * rows :], -1, lane, width)
        )
    return out


def slopes(value):
    sig = jax.nn.sigmoid(value)
    return sig, sig * (1.0 + value * (1.0 - sig))


def dot(a, b):
    return jnp.dot(a, b, preferred_element_type=F32)


def spread_matrix():
    row, col = iota((L, 2 * L), 0), iota((L, 2 * L), 1)
    return jnp.where(row == (col // L) * 64 + (col % L) // 2, 1.0, 0.0).astype(BF)


def pick(cond, a, b):
    return jnp.where(cond, a, b)


def take(ok, tile):
    return tile if ok is None else jnp.where(ok, tile, jnp.zeros_like(tile))


def pack_matrix():
    row, col = iota((2 * L, L), 0), iota((2 * L, L), 1)
    keep = (row % 2 == 0) & (col == (row // L) * 64 + (row % L) // 2)
    return jnp.where(keep, 1.0, 0.0).astype(BF)


def taps(ref, at, tiles):
    return jnp.concatenate([ref[:, (at + j) * L : (at + j + tiles) * L] for j in range(3)], axis=0)


def forward(weight, cells, tiles, lane):
    acc = dot(weight[...], cells)
    sums, slps = [], []
    for pre in combine(acc, 128, tiles, lane):
        sig, slp = slopes(pre)
        act = (pre * sig).astype(BF).astype(F32)
        sums.append(act[:64] + act[64:])
        slps.append(slp)
    means = []
    for t in range(0, tiles, 2):
        total = sums[t] + sums[t + 1]
        means.append(((total + pltpu.roll(total, L - 1, 1)) * 0.125).astype(BF))
    return slps, means


def prepare_kernel(wf, wc, wfwd, wbwd, cfwd, cown, cpart):
    def fine(i, j, k):
        return wf[i, j, k] if 0 <= i < 3 else jnp.zeros((64, 64), BF)

    for j in range(3):
        for k in range(3):
            for x in range(2):
                rows = slice(k * 128 + x * 64, k * 128 + x * 64 + 64)
                for h in range(2):
                    i = 2 * h - x
                    cols = slice(j * 256 + h * L, j * 256 + (h + 1) * L)
                    pair = jnp.concatenate([fine(i, j, k), fine(i + 1, j, k)], axis=0)
                    wfwd[rows, cols] = pair.astype(F32).T.astype(BF)
                    wbwd[rows, cols] = jnp.concatenate(
                        [fine(2 - i, 2 - j, 2 - k), fine(1 - i, 2 - j, 2 - k)], axis=1
                    )
    for k in range(3):
        full = jnp.concatenate([wc[i, j, k] for j in range(3) for i in range(3)], axis=0)
        cfwd[k * 128 : (k + 1) * 128, :] = full.astype(F32).T.astype(BF)
        for j in range(3):
            at = slice(j * L, (j + 1) * L)
            cown[k * 64 : (k + 1) * 64, at] = wc[1, 2 - j, 2 - k]
            cpart[k * 128 : k * 128 + 64, at] = wc[2, 2 - j, 2 - k]
            cpart[k * 128 + 64 : (k + 1) * 128, at] = wc[0, 2 - j, 2 - k]


def start_and_wait(pairs, sems):
    copies = [pltpu.make_async_copy(a, b, sems.at[n]) for n, (a, b) in enumerate(pairs)]
    for c in copies:
        c.start()
    for c in copies:
        c.wait()


def own_edges_kernel(flags, own, cot, first, second, sems):
    pairs = []
    for out, up in ((first, flags[5]), (second, 1 - flags[5])):
        y, cc = up * (16 - YH), up * 7
        for x in range(2):
            pairs.append((own.at[x, pl.ds(y, YH)], out.at[x * YH : (x + 1) * YH]))
        pairs.append((cot.at[pl.ds(cc, 1)], out.at[2 * YH : 2 * YH + 1]))
    start_and_wait(pairs, sems)


def corner_edges_kernel(flags, xa, xb, first, second):
    for out, up in ((first, flags[5]), (second, 1 - flags[5])):
        for n in range(YH):
            out[n] = xa[up * (16 - YH) + n]
            out[YH + n] = xb[up * (16 - YH) + n]


def interior_kernel(flags, own, xa, xb, weight, v2, slope, pooled):
    f = [flags[i] > 0 for i in range(6)]
    for y in range(16):
        at = slice(y * L, (y + 1) * L)
        v2[0:64, at] = take(f[0], pick(f[4], xb[y], xa[y]))
        v2[64:128, at] = own[0, y]
        v2[128:192, at] = own[1, y]
        v2[192:256, at] = take(f[1], pick(f[4], xa[y], xb[y]))
    lane = iota((128, L), 1)
    slps, means = forward(weight, taps(v2, 1, 12), 12, lane)
    for n in range(12):
        slope[:, n * L : (n + 1) * L] = slps[n]
    for t in range(6):
        pooled[:, t * L : (t + 1) * L] = means[t]


def border_kernel(
    flags, v2, mid, aa, ab, ba, bb, weight, slope_lo, slope_hi, pooled, vedge, window
):
    f = [flags[i] > 0 for i in range(6)]
    lane = iota((128, L), 1)
    for side, ok in enumerate((f[2], f[3])):
        even = f[5] if side == 1 else jnp.logical_not(f[5])
        win = window.at[side]
        first = 0 if side == 0 else 3
        for y in range(YH):
            at = slice((first + y) * L, (first + y + 1) * L)
            xs = [pick(even, ba[n * YH + y], bb[n * YH + y]) for n in range(2)]
            win[0:64, at] = take(ok & f[0], pick(f[4], xs[1], xs[0]))
            win[64:128, at] = take(ok, pick(even, aa[y], ab[y]))
            win[128:192, at] = take(ok, pick(even, aa[YH + y], ab[YH + y]))
            win[192:256, at] = take(ok & f[1], pick(f[4], xs[0], xs[1]))
        if side == 0:
            win[:, YH * L :] = v2[:, : 3 * L]
            vedge[:, :L] = win[:, 4 * L : 5 * L]
        else:
            win[:, : 3 * L] = v2[:, 13 * L :]
            vedge[:, L:] = win[:, 3 * L : 4 * L]
    both = jnp.concatenate([taps(window.at[side], 0, 6) for side in range(2)], axis=1)
    slps, means = forward(weight, both, 12, lane)
    for n in range(2):
        slope_lo[:, n * L : (n + 1) * L] = slps[4 + n]
        slope_hi[:, n * L : (n + 1) * L] = slps[6 + n]
    means = (
        [take(f[2], m) for m in means[:2]]
        + [means[2]]
        + [mid[:, t * L : (t + 1) * L] for t in range(6)]
        + [means[3]]
        + [take(f[3], m) for m in means[4:]]
    )
    rows = [jnp.concatenate([means[t], means[t + 5]], axis=1) for t in range(7)]
    packed = dot(jnp.concatenate(rows, axis=0), pack_matrix()).astype(BF)
    for t in range(7):
        pooled[:, t * L : (t + 1) * L] = packed[t * 64 : (t + 1) * 64]


def beside_kernel(flags, aa, cot, ab, v2, vedge, cc, vt):
    f = [flags[i] > 0 for i in range(6)]
    at = 2 * YH
    tiles = (
        [take(f[2], pick(f[5], ab[at], aa[at]))]
        + [cot[n] for n in range(8)]
        + [take(f[3], pick(f[5], aa[at], ab[at]))]
    )
    for t in range(5):
        pair = jnp.concatenate([tiles[t], tiles[t + 5]], axis=0)
        cc[:, t * L : (t + 1) * L] = pair.astype(F32).T
    for y in range(18):
        tile = vedge[:, :L] if y == 0 else vedge[:, L:] if y == 17 else v2[:, (y - 1) * L : y * L]
        vt[y * L : (y + 1) * L, :] = tile.astype(F32).T.astype(BF)


def coarse_kernel(flags, own, a, b, cc, weight, w_part, p2, gpc, first, second):
    f = [flags[i] > 0 for i in range(6)]
    p2[0:64, :] = take(f[0], pick(f[4], b[...], a[...]))
    p2[64:128, :] = own[...]
    p2[128:192, :] = take(f[1], pick(f[4], a[...], b[...]))
    lane = iota((128, L), 1)
    acc = dot(weight[...], taps(p2, 0, 5))
    for t, pre in enumerate(combine(acc, 128, 5, lane, 64)):
        _, slp = slopes(pre)
        tile = (cc[:, t * L : (t + 1) * L] * slp).astype(BF)
        gpc[:, t * L : (t + 1) * L] = tile
        if t < 2:
            other = pltpu.roll(tile.astype(F32), 64, 1).astype(BF)
            gpc[:, (t + 5) * L : (t + 6) * L] = other
    acc = dot(w_part[...], taps(gpc, 0, 5))
    for t, val in enumerate(combine(acc, 128, 5, lane, 64)):
        at = slice(t * L, (t + 1) * L)
        val = val.astype(BF)
        first[:, at] = pick(f[4], val[:64], val[64:])
        second[:, at] = pick(f[4], val[64:], val[:64])


def nt(a, b):
    return lax.dot_general(a, b, (((1,), (1,)), ((), ())), preferred_element_type=F32)


def coarse_corr_kernel(scale, flags, p2, gpc, w_own, own, kept, sent0, sent1, sent2, g3, out):
    lane = iota((64, L), 1)
    acc = dot(w_own[...], taps(gpc, 0, 5))
    for t, val in enumerate(combine(acc, 64, 5, lane, 64)):
        own[:, t * L : (t + 1) * L] = val
    lane = iota((128, L), 1)
    for t in range(5):
        at = slice(t * L, (t + 1) * L)
        tile = gpc[:, at].astype(F32)
        if t == 0 or t == 4:
            tile = jnp.where(lane >= 64 if t == 0 else lane < 64, tile, 0.0)
        g3[0:128, at] = shifted(tile, -1, lane, 64).astype(BF)
        g3[128:256, at] = tile.astype(BF)
        g3[256:384, at] = shifted(tile, 1, lane, 64).astype(BF)
    res = nt(taps(p2, 0, 5), g3[...]) * scale
    for j in range(3):
        for k in range(3):
            at = (3 * j + k) * 192
            out[at : at + 192, :] = res[j * 192 : (j + 1) * 192, k * L : (k + 1) * L].astype(BF)
    low, high = out[:HALF, :], out[HALF:, :]
    even = flags[5] > 0
    kept[...] = pick(even, low, high)
    sent = pick(even, high, low)
    part = HALF // 3
    sent0[...], sent1[...], sent2[...] = sent[:part], sent[part : 2 * part], sent[2 * part :]


def gpf_kernel(
    scale,
    flags,
    own,
    a,
    b,
    fc,
    slope_lo,
    slope,
    slope_hi,
    vt,
    kept,
    got0,
    got1,
    got2,
    first,
    second,
    mine,
    u3,
    pack,
):
    f = [flags[i] > 0 for i in range(6)]
    lane = iota((64, L), 1)
    rows = []
    for t in range(5):
        at = slice(t * L, (t + 1) * L)
        lo, hi = pick(f[4], b[:, at], a[:, at]), pick(f[4], a[:, at], b[:, at])
        total = own[:, at] + take(f[0], lo).astype(F32) + take(f[1], hi).astype(F32)
        main = total.astype(BF)
        rest = (total - main.astype(F32)).astype(BF)
        rows.append(jnp.concatenate([main, rest], axis=1))
    spread = spread_matrix()
    full = dot(jnp.concatenate(rows, axis=0), jnp.concatenate([spread, spread], axis=0))
    gps = [full[64 * t : 64 * t + 64, :L] for t in range(5)]
    gps += [full[64 * t : 64 * t + 64, L:] for t in range(3)]
    for m, gp in enumerate(gps):
        add = gp * 0.125
        for n in (2 * m, 2 * m + 1):
            if n < 2:
                slp = slope_lo[:, n * L : (n + 1) * L]
            elif n < 14:
                slp = slope[:, (n - 2) * L : (n - 1) * L]
            else:
                slp = slope_hi[:, (n - 14) * L : (n - 13) * L]
            rows, at = [], slice(n * L, (n + 1) * L)
            for x in range(2):
                val = (fc[x, n].astype(F32) + add) * slp[x * 64 : (x + 1) * 64]
                rows.append(val.astype(BF))
                tile = rows[x].astype(F32)
                u3[x * 64 : x * 64 + 64, at] = shifted(tile, -1, lane).astype(BF)
                u3[128 + x * 64 : 192 + x * 64, at] = rows[x]
                u3[256 + x * 64 : 320 + x * 64, at] = shifted(tile, 1, lane).astype(BF)
            first[n] = pick(f[4], rows[1], rows[0])
            second[n] = pick(f[4], rows[0], rows[1])
    halves = []
    for j in range(3):
        res = dot(u3[...], vt[j * L : (j + 16) * L, :]) * scale
        for k in range(3):
            both = res[k * L : k * L + 64] + pltpu.roll(res[k * L + 64 : (k + 1) * L], 192, 1)
            at = (3 * j + k) * 64
            pack[at : at + 64, :] = both[:, :L]
            halves.append(both[:, L:])
    halves.append(jnp.zeros((64, L), F32))
    lane = iota((64, L), 1)
    for n in range(5):
        packed = jnp.where(lane < 64, halves[2 * n], pltpu.roll(halves[2 * n + 1], 64, 1))
        pack[576 + 64 * n : 640 + 64 * n, :] = packed
    got = jnp.concatenate([got0[...], got1[...], got2[...]], axis=0)
    coarse = kept[...].astype(F32) + got.astype(F32)
    none = jnp.zeros((R, L), F32)
    for n in range(128):
        at = slice(n * R, (n + 1) * R)
        top = coarse[at] if n < HALF // R else none
        low = pack[at, :] if n < 896 // R else none
        mine[n] = jnp.concatenate([top, low], axis=0).astype(BF)


def gradient_edges_kernel(flags, a, b, c, d, first, second):
    for out, up in ((first, flags[5]), (second, 1 - flags[5])):
        for n, rows in enumerate((a, b, c, d)):
            out[n] = rows[up * 15]


def input_grad_kernel(flags, first, second, a, b, ea, eb, weight, out, g2):
    f = [flags[i] > 0 for i in range(6)]
    for y in range(18):
        if y == 0:
            tiles, ok = [pick(f[5], eb[n], ea[n]) for n in range(4)], f[2]
        elif y == 17:
            tiles, ok = [pick(f[5], ea[n], eb[n]) for n in range(4)], f[3]
        else:
            tiles, ok = [ref[y - 1] for ref in (first, second, a, b)], None
        one, two, lo, hi = tiles
        at = slice(y * L, (y + 1) * L)
        g2[0:64, at] = take(ok, take(f[0], pick(f[4], hi, lo)))
        g2[64:128, at] = take(ok, pick(f[4], two, one))
        g2[128:192, at] = take(ok, pick(f[4], one, two))
        g2[192:256, at] = take(ok, take(f[1], pick(f[4], lo, hi)))
    lane = iota((128, L), 1)
    for t in range(4):
        acc = dot(weight[...], taps(g2, 4 * t, 4))
        for n, val in enumerate(combine(acc, 128, 4, lane)):
            val = val.astype(BF)
            out[0, 4 * t + n] = val[:64]
            out[1, 4 * t + n] = val[64:]


def sum_kernel(parts, out):
    sums = []
    for core in range(2):
        total = parts[core].astype(F32)
        for n in range(core + 2, 128, 2):
            total = total + parts[n].astype(F32)
        sums.append(total)
    total = jnp.concatenate([sums[0][:R], sums[1][:R], sums[0][R:] + sums[1][R:]], axis=0)
    total = total.astype(BF)
    for n in range(128):
        out[n] = total


def unpack_kernel(got, fine, coarse):
    def coarse_rows(q):
        half, at = q // (HALF // R), q % (HALF // R)
        return got[at].astype(F32)[half * R : (half + 1) * R]

    for j in range(3):
        for k in range(3):
            for i in range(3):
                q = ((3 * j + k) * 192 + i * 64) // R
                rows = [coarse_rows(q + m) for m in range(64 // R)]
                coarse[i, j, k] = jnp.concatenate(rows, axis=0)

    def tile(n):
        rows = [got[m].astype(F32)[2 * R :] for m in range(n * 64 // R, (n + 1) * 64 // R)]
        return jnp.concatenate(rows, axis=0).T

    for n in range(9):
        part = tile(n)
        fine[0, n // 3, n % 3] = part[:64]
        fine[1, n // 3, n % 3] = part[64:]
    for n in range(5):
        part = tile(9 + n)
        for h in range(2):
            at = 2 * n + h
            if at < 9:
                fine[2, at // 3, at % 3] = part[64 * h : 64 * h + 64]


def call(kernel, name, outs, args, scratch=(), flags=True, macs=0, copies=0):
    space = pl.ANY if copies else pltpu.VMEM
    specs = [pl.BlockSpec(memory_space=space) for _ in args]
    if flags:
        specs[0] = pl.BlockSpec(memory_space=pltpu.SMEM)
    moved = sum(a.size * a.dtype.itemsize for a in args)
    shapes = tuple(jax.ShapeDtypeStruct(*o) for o in outs)
    if copies:
        scratch = [pltpu.SemaphoreType.DMA((copies,))]
    got = pl.pallas_call(
        kernel,
        out_shape=shapes,
        in_specs=specs,
        out_specs=tuple(pl.BlockSpec(memory_space=space) for _ in shapes),
        scratch_shapes=list(scratch),
        compiler_params=pltpu.CompilerParams(vmem_limit_bytes=VMEM),
        cost_estimate=pl.CostEstimate(flops=2 * macs, bytes_accessed=moved, transcendentals=0),
        name=name,
    )(*args)
    return got if len(shapes) > 1 else got[0]


def swaps(first, second, axis):
    count = lax.axis_size(axis)
    pairs = [(i, i ^ 1) for i in range(count)]
    others = [(0, 0), (count - 1, count - 1)] + [(i, ((i - 1) ^ 1) + 1) for i in range(1, count - 1)]
    other = lax.ppermute(second, axis, others)
    return lax.ppermute(first, axis, pairs), other


def on_device(inputs, fine_cot, coarse_cot, weight_fine, weight_coarse):
    slab, sub = lax.axis_index("slab"), lax.axis_index("sub")
    flags = jnp.stack(
        [slab > 0, slab < 31, sub > 0, sub < 3, slab % 2 == 0, sub % 2 == 0]
    ).astype(jnp.int32)
    cot = jnp.swapaxes(coarse_cot[0], 1, 2)

    odd = slab % 2
    xa, xb = swaps(
        lax.dynamic_index_in_dim(inputs, 1 - odd, 0, False),
        lax.dynamic_index_in_dim(inputs, odd, 0, False),
        "slab",
    )
    own_edge = ((2 * YH + 1, 64, L), BF)
    first, second = call(
        own_edges_kernel,
        "own_edges",
        (own_edge, own_edge),
        (flags, inputs, cot),
        copies=6,
    )
    aa, ab = swaps(first, second, "sub")
    w_fwd, w_bwd, c_fwd, c_own, c_part = call(
        prepare_kernel,
        "prepare_weights",
        (
            ((384, 768), BF),
            ((384, 768), BF),
            ((384, 576), BF),
            ((192, 384), BF),
            ((384, 384), BF),
        ),
        (weight_fine, weight_coarse),
        flags=False,
    )
    corner = ((2 * YH, 64, L), BF)
    first, second = call(
        corner_edges_kernel, "corner_edges", (corner, corner), (flags, xa, xb)
    )
    ba, bb = swaps(first, second, "sub")
    v2, slope, mid = call(
        interior_kernel,
        "fine_forward_interior",
        (((256, 16 * L), BF), ((128, 12 * L), F32), ((64, 6 * L), BF)),
        (flags, inputs, xa, xb, w_fwd),
        macs=384 * 768 * 12 * L,
    )
    slope_lo, slope_hi, pooled, vedge = call(
        border_kernel,
        "fine_forward_border",
        (((128, 2 * L), F32), ((128, 2 * L), F32), ((64, 7 * L), BF), ((256, 2 * L), BF)),
        (flags, v2, mid, aa, ab, ba, bb, w_fwd),
        scratch=[pltpu.VMEM((2, 256, 8 * L), BF)],
        macs=384 * 768 * 12 * L,
    )
    pa, pb = swaps(pooled, pooled, "slab")
    cc, vt = call(
        beside_kernel,
        "cotangent_and_turned_inputs",
        (((128, 5 * L), F32), ((18 * L, 256), BF)),
        (flags, aa, cot, ab, v2, vedge),
    )
    p2, gpc, first, second = call(
        coarse_kernel,
        "coarse_forward",
        (
            ((192, 7 * L), BF),
            ((128, 7 * L), BF),
            ((64, 5 * L), BF),
            ((64, 5 * L), BF),
        ),
        (flags, pooled, pa, pb, cc, c_fwd, c_part),
        macs=384 * 960 * 6 * L,
    )
    ga, gb = swaps(first, second, "slab")
    third = ((HALF // 3, L), BF)
    own, kept, *sent = call(
        functools.partial(coarse_corr_kernel, 1.0 / 256.0),
        "coarse_correlate",
        (((64, 5 * L), F32), ((HALF, L), BF), third, third, third),
        (flags, p2, gpc, c_own),
        scratch=[pltpu.VMEM((384, 5 * L), BF), pltpu.VMEM((2 * HALF, L), BF)],
        macs=384 * 768 * 6 * L,
    )
    got0, got1, got2 = (lax.ppermute(part, "sub", [(0, 1), (1, 0), (2, 3), (3, 2)]) for part in sent)
    first, second, mine = call(
        functools.partial(gpf_kernel, 524288.0**-0.5),
        "fine_gradient",
        (((16, 64, L), BF), ((16, 64, L), BF), ((128, 2 * R, L), BF)),
        (
            flags,
            own,
            ga,
            gb,
            fine_cot,
            slope_lo,
            slope,
            slope_hi,
            vt,
            kept,
            got0,
            got1,
            got2,
        ),
        scratch=[
            pltpu.VMEM((384, 16 * L), BF),
            pltpu.VMEM((896, L), F32),
        ],
        macs=384 * 768 * 16 * L,
    )
    ha, hb = swaps(first, second, "slab")
    shares = lax.all_to_all(mine.reshape(128 * 2 * R, L), ("slab", "sub"), 0, 0, tiled=True)
    total = call(
        sum_kernel,
        "sum_shares",
        (((128, 3 * R, L), BF),),
        (shares.reshape(128, 2 * R, L),),
        flags=False,
    )
    everything = lax.all_to_all(total.reshape(128 * 3 * R, L), ("slab", "sub"), 0, 0, tiled=True)
    one, two = call(
        gradient_edges_kernel,
        "gradient_edges",
        (((4, 64, L), BF), ((4, 64, L), BF)),
        (flags, first, second, ha, hb),
        macs=20 * 384 * 768 * 16 * L,
    )
    ea, eb = swaps(one, two, "sub")
    grad_input = call(
        input_grad_kernel,
        "input_gradient",
        (((2, 16, 64, L), BF),),
        (flags, first, second, ha, hb, ea, eb, w_bwd),
        scratch=[pltpu.VMEM((256, 18 * L), BF)],
        macs=384 * 768 * 16 * L,
    )
    grad_fine, grad_coarse = call(
        unpack_kernel,
        "unpack",
        (((3, 3, 3, 64, 64), F32), ((3, 3, 3, 64, 128), F32)),
        (everything.reshape(128, 3 * R, L),),
        flags=False,
    )
    return (grad_input, grad_fine, grad_coarse)


def solution(mesh):
    in_specs = (
        P("slab", "sub", None, None),
        P("slab", "sub", None, None),
        P("slab", "sub", None, None),
        P(),
        P(),
    )
    out_specs = (P("slab", "sub", None, None), P(), P())
    return jax.shard_map(
        on_device, mesh=mesh, in_specs=in_specs, out_specs=out_specs, check_vma=False
    )
```

```python
import functools

import jax
import jax.numpy as jnp
from jax import lax
from jax.experimental import pallas as pl
from jax.experimental.pallas import tpu as pltpu
from jax.sharding import PartitionSpec as P

L = 128
YH = 5
BF = jnp.bfloat16
F32 = jnp.float32
R = 8
HALF = 864
VMEM = 20 * 1024 * 1024


def iota(shape, dim):
    return lax.broadcasted_iota(jnp.int32, shape, dim)


def shifted(tile, by, lane, width=L):
    out = pltpu.roll(tile, by % L, 1)
    z = lane % width
    return jnp.where(z >= by if by > 0 else z < width + by, out, 0.0)


def combine(acc, rows, tiles, lane, width=L):
    out = []
    for t in range(tiles):
        part = acc[:, t * L : (t + 1) * L]
        out.append(
            shifted(part[:rows], 1, lane, width)
            + part[rows : 2 * rows]
            + shifted(part[2 * rows :], -1, lane, width)
        )
    return out


def slopes(value):
    sig = jax.nn.sigmoid(value)
    return sig, sig * (1.0 + value * (1.0 - sig))


def dot(a, b):
    return jnp.dot(a, b, preferred_element_type=F32)


def spread_matrix():
    row, col = iota((L, 2 * L), 0), iota((L, 2 * L), 1)
    return jnp.where(row == (col // L) * 64 + (col % L) // 2, 1.0, 0.0).astype(BF)


def pick(cond, a, b):
    return jnp.where(cond, a, b)


def take(ok, tile):
    return tile if ok is None else jnp.where(ok, tile, jnp.zeros_like(tile))


def pack_matrix():
    row, col = iota((2 * L, L), 0), iota((2 * L, L), 1)
    keep = (row % 2 == 0) & (col == (row // L) * 64 + (row % L) // 2)
    return jnp.where(keep, 1.0, 0.0).astype(BF)


def taps(ref, at, tiles):
    return jnp.concatenate([ref[:, (at + j) * L : (at + j + tiles) * L] for j in range(3)], axis=0)


def forward(weight, cells, tiles, lane):
    acc = dot(weight[...], cells)
    sums, slps = [], []
    for pre in combine(acc, 128, tiles, lane):
        sig, slp = slopes(pre)
        act = (pre * sig).astype(BF).astype(F32)
        sums.append(act[:64] + act[64:])
        slps.append(slp)
    means = []
    for t in range(0, tiles, 2):
        total = sums[t] + sums[t + 1]
        means.append(((total + pltpu.roll(total, L - 1, 1)) * 0.125).astype(BF))
    return slps, means


def prepare_kernel(wf, wc, wfwd, wbwd, cfwd, cown, cpart):
    def fine(i, j, k):
        return wf[i, j, k] if 0 <= i < 3 else jnp.zeros((64, 64), BF)

    for j in range(3):
        for k in range(3):
            for x in range(2):
                rows = slice(k * 128 + x * 64, k * 128 + x * 64 + 64)
                for h in range(2):
                    i = 2 * h - x
                    cols = slice(j * 256 + h * L, j * 256 + (h + 1) * L)
                    pair = jnp.concatenate([fine(i, j, k), fine(i + 1, j, k)], axis=0)
                    wfwd[rows, cols] = pair.astype(F32).T.astype(BF)
                    wbwd[rows, cols] = jnp.concatenate(
                        [fine(2 - i, 2 - j, 2 - k), fine(1 - i, 2 - j, 2 - k)], axis=1
                    )
    for k in range(3):
        full = jnp.concatenate([wc[i, j, k] for j in range(3) for i in range(3)], axis=0)
        cfwd[k * 128 : (k + 1) * 128, :] = full.astype(F32).T.astype(BF)
        for j in range(3):
            at = slice(j * L, (j + 1) * L)
            cown[k * 64 : (k + 1) * 64, at] = wc[1, 2 - j, 2 - k]
            cpart[k * 128 : k * 128 + 64, at] = wc[2, 2 - j, 2 - k]
            cpart[k * 128 + 64 : (k + 1) * 128, at] = wc[0, 2 - j, 2 - k]


def start_and_wait(pairs, sems):
    copies = [pltpu.make_async_copy(a, b, sems.at[n]) for n, (a, b) in enumerate(pairs)]
    for c in copies:
        c.start()
    for c in copies:
        c.wait()


def own_edges_kernel(flags, own, cot, first, second, far, sems):
    pairs = []
    for out, up in ((first, flags[5]), (second, 1 - flags[5])):
        y, cc = up * (16 - YH), up * 7
        for x in range(2):
            pairs.append((own.at[x, pl.ds(y, YH)], out.at[x * YH : (x + 1) * YH]))
        pairs.append((cot.at[pl.ds(cc, 1)], out.at[2 * YH : 2 * YH + 1]))
    y = (1 - flags[5]) * (16 - YH)
    pairs.append((own.at[flags[4], pl.ds(y, YH)], far))
    start_and_wait(pairs, sems)


def corner_edges_kernel(flags, xa, xb, first, second):
    at = flags[5] * (16 - YH)
    for n in range(YH):
        first[n] = xa[at + n]
        first[YH + n] = xb[at + n]
        second[n] = xb[16 - YH - at + n]


def interior_kernel(flags, own, xa, xb, weight, v2, slope, pooled):
    f = [flags[i] > 0 for i in range(6)]
    for y in range(16):
        at = slice(y * L, (y + 1) * L)
        v2[0:64, at] = take(f[0], pick(f[4], xb[y], xa[y]))
        v2[64:128, at] = own[0, y]
        v2[128:192, at] = own[1, y]
        v2[192:256, at] = take(f[1], pick(f[4], xa[y], xb[y]))
    lane = iota((128, L), 1)
    slps, means = forward(weight, taps(v2, 1, 12), 12, lane)
    for n in range(12):
        slope[:, n * L : (n + 1) * L] = slps[n]
    for t in range(6):
        pooled[:, t * L : (t + 1) * L] = means[t]


def border_kernel(
    flags, v2, mid, aa, ab, nb, ba, bb, weight, slope_lo, slope_hi, pooled, vedge, window
):
    f = [flags[i] > 0 for i in range(6)]
    lane = iota((128, L), 1)
    for side, ok in enumerate((f[2], f[3])):
        even = f[5] if side == 1 else jnp.logical_not(f[5])
        win = window.at[side]
        first = 0 if side == 0 else 3
        for y in range(YH):
            at = slice((first + y) * L, (first + y + 1) * L)
            xs = [pick(even, ba[y], nb[y]), pick(even, ba[YH + y], bb[y])]
            win[0:64, at] = take(ok & f[0], pick(f[4], xs[1], xs[0]))
            win[64:128, at] = take(ok, pick(even, aa[y], ab[y]))
            win[128:192, at] = take(ok, pick(even, aa[YH + y], ab[YH + y]))
            win[192:256, at] = take(ok & f[1], pick(f[4], xs[0], xs[1]))
        if side == 0:
            win[:, YH * L :] = v2[:, : 3 * L]
            vedge[:, :L] = win[:, 4 * L : 5 * L]
        else:
            win[:, : 3 * L] = v2[:, 13 * L :]
            vedge[:, L:] = win[:, 3 * L : 4 * L]
    both = jnp.concatenate([taps(window.at[side], 0, 6) for side in range(2)], axis=1)
    slps, means = forward(weight, both, 12, lane)
    for n in range(2):
        slope_lo[:, n * L : (n + 1) * L] = slps[4 + n]
        slope_hi[:, n * L : (n + 1) * L] = slps[6 + n]
    means = (
        [take(f[2], m) for m in means[:2]]
        + [means[2]]
        + [mid[:, t * L : (t + 1) * L] for t in range(6)]
        + [means[3]]
        + [take(f[3], m) for m in means[4:]]
    )
    rows = [jnp.concatenate([means[t], means[t + 5]], axis=1) for t in range(7)]
    packed = dot(jnp.concatenate(rows, axis=0), pack_matrix()).astype(BF)
    for t in range(7):
        pooled[:, t * L : (t + 1) * L] = packed[t * 64 : (t + 1) * 64]


def beside_kernel(flags, aa, cot, ab, v2, vedge, cc, vt):
    f = [flags[i] > 0 for i in range(6)]
    at = 2 * YH
    tiles = (
        [take(f[2], pick(f[5], ab[at], aa[at]))]
        + [cot[n] for n in range(8)]
        + [take(f[3], pick(f[5], aa[at], ab[at]))]
    )
    for t in range(5):
        pair = jnp.concatenate([tiles[t], tiles[t + 5]], axis=0)
        cc[:, t * L : (t + 1) * L] = pair.astype(F32).T
    for y in range(18):
        tile = vedge[:, :L] if y == 0 else vedge[:, L:] if y == 17 else v2[:, (y - 1) * L : y * L]
        vt[y * L : (y + 1) * L, :] = tile.astype(F32).T.astype(BF)


def coarse_kernel(flags, own, a, b, cc, weight, w_part, p2, gpc, first, second):
    f = [flags[i] > 0 for i in range(6)]
    p2[0:64, :] = take(f[0], pick(f[4], b[...], a[...]))
    p2[64:128, :] = own[...]
    p2[128:192, :] = take(f[1], pick(f[4], a[...], b[...]))
    lane = iota((128, L), 1)
    acc = dot(weight[...], taps(p2, 0, 5))
    for t, pre in enumerate(combine(acc, 128, 5, lane, 64)):
        _, slp = slopes(pre)
        tile = (cc[:, t * L : (t + 1) * L] * slp).astype(BF)
        gpc[:, t * L : (t + 1) * L] = tile
        if t < 2:
            other = pltpu.roll(tile.astype(F32), 64, 1).astype(BF)
            gpc[:, (t + 5) * L : (t + 6) * L] = other
    acc = dot(w_part[...], taps(gpc, 0, 5))
    for t, val in enumerate(combine(acc, 128, 5, lane, 64)):
        at = slice(t * L, (t + 1) * L)
        val = val.astype(BF)
        first[:, at] = pick(f[4], val[:64], val[64:])
        second[:, at] = pick(f[4], val[64:], val[:64])


def nt(a, b):
    return lax.dot_general(a, b, (((1,), (1,)), ((), ())), preferred_element_type=F32)


def coarse_corr_kernel(scale, flags, p2, gpc, w_own, own, kept, sent0, sent1, sent2, g3, out):
    lane = iota((64, L), 1)
    acc = dot(w_own[...], taps(gpc, 0, 5))
    for t, val in enumerate(combine(acc, 64, 5, lane, 64)):
        own[:, t * L : (t + 1) * L] = val
    lane = iota((128, L), 1)
    for t in range(5):
        at = slice(t * L, (t + 1) * L)
        tile = gpc[:, at].astype(F32)
        if t == 0 or t == 4:
            tile = jnp.where(lane >= 64 if t == 0 else lane < 64, tile, 0.0)
        g3[0:128, at] = shifted(tile, -1, lane, 64).astype(BF)
        g3[128:256, at] = tile.astype(BF)
        g3[256:384, at] = shifted(tile, 1, lane, 64).astype(BF)
    res = nt(taps(p2, 0, 5), g3[...]) * scale
    for j in range(3):
        for k in range(3):
            at = (3 * j + k) * 192
            out[at : at + 192, :] = res[j * 192 : (j + 1) * 192, k * L : (k + 1) * L].astype(BF)
    low, high = out[:HALF, :], out[HALF:, :]
    even = flags[5] > 0
    kept[...] = pick(even, low, high)
    sent = pick(even, high, low)
    part = HALF // 3
    sent0[...], sent1[...], sent2[...] = sent[:part], sent[part : 2 * part], sent[2 * part :]


def gpf_kernel(
    scale,
    flags,
    own,
    a,
    b,
    fc,
    slope_lo,
    slope,
    slope_hi,
    vt,
    kept,
    got0,
    got1,
    got2,
    first,
    second,
    mine,
    u3,
    pack,
):
    f = [flags[i] > 0 for i in range(6)]
    lane = iota((64, L), 1)
    rows = []
    for t in range(5):
        at = slice(t * L, (t + 1) * L)
        lo, hi = pick(f[4], b[:, at], a[:, at]), pick(f[4], a[:, at], b[:, at])
        total = own[:, at] + take(f[0], lo).astype(F32) + take(f[1], hi).astype(F32)
        main = total.astype(BF)
        rest = (total - main.astype(F32)).astype(BF)
        rows.append(jnp.concatenate([main, rest], axis=1))
    spread = spread_matrix()
    full = dot(jnp.concatenate(rows, axis=0), jnp.concatenate([spread, spread], axis=0))
    gps = [full[64 * t : 64 * t + 64, :L] for t in range(5)]
    gps += [full[64 * t : 64 * t + 64, L:] for t in range(3)]
    for m, gp in enumerate(gps):
        add = gp * 0.125
        for n in (2 * m, 2 * m + 1):
            if n < 2:
                slp = slope_lo[:, n * L : (n + 1) * L]
            elif n < 14:
                slp = slope[:, (n - 2) * L : (n - 1) * L]
            else:
                slp = slope_hi[:, (n - 14) * L : (n - 13) * L]
            rows, at = [], slice(n * L, (n + 1) * L)
            for x in range(2):
                val = (fc[x, n].astype(F32) + add) * slp[x * 64 : (x + 1) * 64]
                rows.append(val.astype(BF))
                tile = rows[x].astype(F32)
                u3[x * 64 : x * 64 + 64, at] = shifted(tile, -1, lane).astype(BF)
                u3[128 + x * 64 : 192 + x * 64, at] = rows[x]
                u3[256 + x * 64 : 320 + x * 64, at] = shifted(tile, 1, lane).astype(BF)
            first[n] = pick(f[4], rows[1], rows[0])
            second[n] = pick(f[4], rows[0], rows[1])
    halves = []
    for j in range(3):
        res = dot(u3[...], vt[j * L : (j + 16) * L, :]) * scale
        for k in range(3):
            both = res[k * L : k * L + 64] + pltpu.roll(res[k * L + 64 : (k + 1) * L], 192, 1)
            at = (3 * j + k) * 64
            pack[at : at + 64, :] = both[:, :L]
            halves.append(both[:, L:])
    halves.append(jnp.zeros((64, L), F32))
    lane = iota((64, L), 1)
    for n in range(5):
        packed = jnp.where(lane < 64, halves[2 * n], pltpu.roll(halves[2 * n + 1], 64, 1))
        pack[576 + 64 * n : 640 + 64 * n, :] = packed
    got = jnp.concatenate([got0[...], got1[...], got2[...]], axis=0)
    coarse = kept[...].astype(F32) + got.astype(F32)
    none = jnp.zeros((R, L), F32)
    for n in range(128):
        at = slice(n * R, (n + 1) * R)
        top = coarse[at] if n < HALF // R else none
        low = pack[at, :] if n < 896 // R else none
        mine[n] = jnp.concatenate([top, low], axis=0).astype(BF)


def gradient_edges_kernel(flags, a, b, c, d, first, second):
    for out, up in ((first, flags[5]), (second, 1 - flags[5])):
        for n, rows in enumerate((a, b, c, d)):
            out[n] = rows[up * 15]


def input_grad_kernel(flags, first, second, a, b, ea, eb, weight, out, g2):
    f = [flags[i] > 0 for i in range(6)]
    for y in range(18):
        if y == 0:
            tiles, ok = [pick(f[5], eb[n], ea[n]) for n in range(4)], f[2]
        elif y == 17:
            tiles, ok = [pick(f[5], ea[n], eb[n]) for n in range(4)], f[3]
        else:
            tiles, ok = [ref[y - 1] for ref in (first, second, a, b)], None
        one, two, lo, hi = tiles
        at = slice(y * L, (y + 1) * L)
        g2[0:64, at] = take(ok, take(f[0], pick(f[4], hi, lo)))
        g2[64:128, at] = take(ok, pick(f[4], two, one))
        g2[128:192, at] = take(ok, pick(f[4], one, two))
        g2[192:256, at] = take(ok, take(f[1], pick(f[4], lo, hi)))
    lane = iota((128, L), 1)
    for t in range(4):
        acc = dot(weight[...], taps(g2, 4 * t, 4))
        for n, val in enumerate(combine(acc, 128, 4, lane)):
            val = val.astype(BF)
            out[0, 4 * t + n] = val[:64]
            out[1, 4 * t + n] = val[64:]


def sum_kernel(parts, out):
    sums = []
    for core in range(2):
        total = parts[core].astype(F32)
        for n in range(core + 2, 128, 2):
            total = total + parts[n].astype(F32)
        sums.append(total)
    total = jnp.concatenate([sums[0][:R], sums[1][:R], sums[0][R:] + sums[1][R:]], axis=0)
    total = total.astype(BF)
    for n in range(128):
        out[n] = total


def unpack_kernel(got, fine, coarse):
    def coarse_rows(q):
        half, at = q // (HALF // R), q % (HALF // R)
        return got[at].astype(F32)[half * R : (half + 1) * R]

    for j in range(3):
        for k in range(3):
            for i in range(3):
                q = ((3 * j + k) * 192 + i * 64) // R
                rows = [coarse_rows(q + m) for m in range(64 // R)]
                coarse[i, j, k] = jnp.concatenate(rows, axis=0)

    def tile(n):
        rows = [got[m].astype(F32)[2 * R :] for m in range(n * 64 // R, (n + 1) * 64 // R)]
        return jnp.concatenate(rows, axis=0).T

    for n in range(9):
        part = tile(n)
        fine[0, n // 3, n % 3] = part[:64]
        fine[1, n // 3, n % 3] = part[64:]
    for n in range(5):
        part = tile(9 + n)
        for h in range(2):
            at = 2 * n + h
            if at < 9:
                fine[2, at // 3, at % 3] = part[64 * h : 64 * h + 64]


def call(kernel, name, outs, args, scratch=(), flags=True, macs=0, copies=0):
    space = pl.ANY if copies else pltpu.VMEM
    specs = [pl.BlockSpec(memory_space=space) for _ in args]
    if flags:
        specs[0] = pl.BlockSpec(memory_space=pltpu.SMEM)
    moved = sum(a.size * a.dtype.itemsize for a in args)
    shapes = tuple(jax.ShapeDtypeStruct(*o) for o in outs)
    if copies:
        scratch = [pltpu.SemaphoreType.DMA((copies,))]
    got = pl.pallas_call(
        kernel,
        out_shape=shapes,
        in_specs=specs,
        out_specs=tuple(pl.BlockSpec(memory_space=space) for _ in shapes),
        scratch_shapes=list(scratch),
        compiler_params=pltpu.CompilerParams(vmem_limit_bytes=VMEM),
        cost_estimate=pl.CostEstimate(flops=2 * macs, bytes_accessed=moved, transcendentals=0),
        name=name,
    )(*args)
    return got if len(shapes) > 1 else got[0]


def swaps(first, second, axis):
    count = lax.axis_size(axis)
    pairs = [(i, i ^ 1) for i in range(count)]
    others = [(0, 0), (count - 1, count - 1)] + [(i, ((i - 1) ^ 1) + 1) for i in range(1, count - 1)]
    other = lax.ppermute(second, axis, others)
    return lax.ppermute(first, axis, pairs), other


def diagonal_swap(far):
    turn = (0, 2, 1, 3)
    pairs = [(4 * i + j, 4 * (i ^ 1) + turn[j]) for i in range(32) for j in range(4)]
    return lax.ppermute(far, ("slab", "sub"), pairs)


def on_device(inputs, fine_cot, coarse_cot, weight_fine, weight_coarse):
    slab, sub = lax.axis_index("slab"), lax.axis_index("sub")
    flags = jnp.stack(
        [slab > 0, slab < 31, sub > 0, sub < 3, slab % 2 == 0, sub % 2 == 0]
    ).astype(jnp.int32)
    cot = jnp.swapaxes(coarse_cot[0], 1, 2)

    odd = slab % 2
    xa, xb = swaps(
        lax.dynamic_index_in_dim(inputs, 1 - odd, 0, False),
        lax.dynamic_index_in_dim(inputs, odd, 0, False),
        "slab",
    )
    own_edge = ((2 * YH + 1, 64, L), BF)
    corner = ((YH, 64, L), BF)
    first, second, far = call(
        own_edges_kernel,
        "own_edges",
        (own_edge, own_edge, corner),
        (flags, inputs, cot),
        copies=7,
    )
    aa, ab = swaps(first, second, "sub")
    nb = diagonal_swap(far)
    w_fwd, w_bwd, c_fwd, c_own, c_part = call(
        prepare_kernel,
        "prepare_weights",
        (
            ((384, 768), BF),
            ((384, 768), BF),
            ((384, 576), BF),
            ((192, 384), BF),
            ((384, 384), BF),
        ),
        (weight_fine, weight_coarse),
        flags=False,
    )
    xa, xb, w_fwd = lax.optimization_barrier((xa, xb, w_fwd))
    first, second = call(
        corner_edges_kernel, "corner_edges", (((2 * YH, 64, L), BF), corner), (flags, xa, xb)
    )
    ba, bb = swaps(first, second, "sub")
    v2, slope, mid = call(
        interior_kernel,
        "fine_forward_interior",
        (((256, 16 * L), BF), ((128, 12 * L), F32), ((64, 6 * L), BF)),
        (flags, inputs, xa, xb, w_fwd),
        macs=384 * 768 * 12 * L,
    )
    slope_lo, slope_hi, pooled, vedge = call(
        border_kernel,
        "fine_forward_border",
        (((128, 2 * L), F32), ((128, 2 * L), F32), ((64, 7 * L), BF), ((256, 2 * L), BF)),
        (flags, v2, mid, aa, ab, nb, ba, bb, w_fwd),
        scratch=[pltpu.VMEM((2, 256, 8 * L), BF)],
        macs=384 * 768 * 12 * L,
    )
    pa, pb = swaps(pooled, pooled, "slab")
    cc, vt = call(
        beside_kernel,
        "cotangent_and_turned_inputs",
        (((128, 5 * L), F32), ((18 * L, 256), BF)),
        (flags, aa, cot, ab, v2, vedge),
    )
    p2, gpc, first, second = call(
        coarse_kernel,
        "coarse_forward",
        (
            ((192, 7 * L), BF),
            ((128, 7 * L), BF),
            ((64, 5 * L), BF),
            ((64, 5 * L), BF),
        ),
        (flags, pooled, pa, pb, cc, c_fwd, c_part),
        macs=384 * 960 * 6 * L,
    )
    ga, gb = swaps(first, second, "slab")
    third = ((HALF // 3, L), BF)
    own, kept, *sent = call(
        functools.partial(coarse_corr_kernel, 1.0 / 256.0),
        "coarse_correlate",
        (((64, 5 * L), F32), ((HALF, L), BF), third, third, third),
        (flags, p2, gpc, c_own),
        scratch=[pltpu.VMEM((384, 5 * L), BF), pltpu.VMEM((2 * HALF, L), BF)],
        macs=384 * 768 * 6 * L,
    )
    got0, got1, got2 = (lax.ppermute(part, "sub", [(0, 1), (1, 0), (2, 3), (3, 2)]) for part in sent)
    first, second, mine = call(
        functools.partial(gpf_kernel, 524288.0**-0.5),
        "fine_gradient",
        (((16, 64, L), BF), ((16, 64, L), BF), ((128, 2 * R, L), BF)),
        (
            flags,
            own,
            ga,
            gb,
            fine_cot,
            slope_lo,
            slope,
            slope_hi,
            vt,
            kept,
            got0,
            got1,
            got2,
        ),
        scratch=[
            pltpu.VMEM((384, 16 * L), BF),
            pltpu.VMEM((896, L), F32),
        ],
        macs=384 * 768 * 16 * L,
    )
    ha, hb = swaps(first, second, "slab")
    shares = lax.all_to_all(mine.reshape(128 * 2 * R, L), ("slab", "sub"), 0, 0, tiled=True)
    total = call(
        sum_kernel,
        "sum_shares",
        (((128, 3 * R, L), BF),),
        (shares.reshape(128, 2 * R, L),),
        flags=False,
    )
    everything = lax.all_to_all(total.reshape(128 * 3 * R, L), ("slab", "sub"), 0, 0, tiled=True)
    one, two = call(
        gradient_edges_kernel,
        "gradient_edges",
        (((4, 64, L), BF), ((4, 64, L), BF)),
        (flags, first, second, ha, hb),
        macs=20 * 384 * 768 * 16 * L,
    )
    ea, eb = swaps(one, two, "sub")
    grad_input = call(
        input_grad_kernel,
        "input_gradient",
        (((2, 16, 64, L), BF),),
        (flags, first, second, ha, hb, ea, eb, w_bwd),
        scratch=[pltpu.VMEM((256, 18 * L), BF)],
        macs=384 * 768 * 16 * L,
    )
    grad_fine, grad_coarse = call(
        unpack_kernel,
        "unpack",
        (((3, 3, 3, 64, 64), F32), ((3, 3, 3, 64, 128), F32)),
        (everything.reshape(128, 3 * R, L),),
        flags=False,
    )
    return (grad_input, grad_fine, grad_coarse)


def solution(mesh):
    in_specs = (
        P("slab", "sub", None, None),
        P("slab", "sub", None, None),
        P("slab", "sub", None, None),
        P(),
        P(),
    )
    out_specs = (P("slab", "sub", None, None), P(), P())
    return jax.shard_map(
        on_device, mesh=mesh, in_specs=in_specs, out_specs=out_specs, check_vma=False
    )
```

```python
import functools

import jax
import jax.numpy as jnp
from jax import lax
from jax.experimental import pallas as pl
from jax.experimental.pallas import tpu as pltpu
from jax.sharding import PartitionSpec as P

L = 128
YH = 5
BF = jnp.bfloat16
F32 = jnp.float32
R = 8
HALF = 864
VMEM = 20 * 1024 * 1024


def iota(shape, dim):
    return lax.broadcasted_iota(jnp.int32, shape, dim)


def shifted(tile, by, lane, width=L):
    out = pltpu.roll(tile, by % L, 1)
    z = lane % width
    return jnp.where(z >= by if by > 0 else z < width + by, out, 0.0)


def combine(acc, rows, tiles, lane, width=L):
    out = []
    for t in range(tiles):
        part = acc[:, t * L : (t + 1) * L]
        out.append(
            shifted(part[:rows], 1, lane, width)
            + part[rows : 2 * rows]
            + shifted(part[2 * rows :], -1, lane, width)
        )
    return out


def slopes(value):
    sig = jax.nn.sigmoid(value)
    return sig, sig * (1.0 + value * (1.0 - sig))


def dot(a, b):
    return jnp.dot(a, b, preferred_element_type=F32)


def spread_matrix():
    row, col = iota((L, 2 * L), 0), iota((L, 2 * L), 1)
    return jnp.where(row == (col // L) * 64 + (col % L) // 2, 1.0, 0.0).astype(BF)


def pick(cond, a, b):
    return jnp.where(cond, a, b)


def take(ok, tile):
    return tile if ok is None else jnp.where(ok, tile, jnp.zeros_like(tile))


def pack_matrix():
    row, col = iota((2 * L, L), 0), iota((2 * L, L), 1)
    keep = (row % 2 == 0) & (col == (row // L) * 64 + (row % L) // 2)
    return jnp.where(keep, 1.0, 0.0).astype(BF)


def taps(ref, at, tiles):
    return jnp.concatenate([ref[:, (at + j) * L : (at + j + tiles) * L] for j in range(3)], axis=0)


def forward(weight, cells, tiles, lane):
    acc = dot(weight[...], cells)
    sums, slps = [], []
    for pre in combine(acc, 128, tiles, lane):
        sig, slp = slopes(pre)
        act = pre * sig
        sums.append(act[:64] + act[64:])
        slps.append(slp)
    means = []
    for t in range(0, tiles, 2):
        total = sums[t] + sums[t + 1]
        means.append(((total + pltpu.roll(total, L - 1, 1)) * 0.125).astype(BF))
    return slps, means


def prepare_kernel(wf, wc, wfwd, wbwd, cfwd, cown, cpart):
    def fine(i, j, k):
        return wf[i, j, k] if 0 <= i < 3 else jnp.zeros((64, 64), BF)

    for j in range(3):
        for k in range(3):
            for x in range(2):
                rows = slice(k * 128 + x * 64, k * 128 + x * 64 + 64)
                for h in range(2):
                    i = 2 * h - x
                    cols = slice(j * 256 + h * L, j * 256 + (h + 1) * L)
                    pair = jnp.concatenate([fine(i, j, k), fine(i + 1, j, k)], axis=0)
                    wfwd[rows, cols] = pair.astype(F32).T.astype(BF)
                    wbwd[rows, cols] = jnp.concatenate(
                        [fine(2 - i, 2 - j, 2 - k), fine(1 - i, 2 - j, 2 - k)], axis=1
                    )
    for k in range(3):
        full = jnp.concatenate([wc[i, j, k] for j in range(3) for i in range(3)], axis=0)
        cfwd[k * 128 : (k + 1) * 128, :] = full.astype(F32).T.astype(BF)
        for j in range(3):
            at = slice(j * L, (j + 1) * L)
            cown[k * 64 : (k + 1) * 64, at] = wc[1, 2 - j, 2 - k]
            cpart[k * 128 : k * 128 + 64, at] = wc[2, 2 - j, 2 - k]
            cpart[k * 128 + 64 : (k + 1) * 128, at] = wc[0, 2 - j, 2 - k]


def start_and_wait(pairs, sems):
    copies = [pltpu.make_async_copy(a, b, sems.at[n]) for n, (a, b) in enumerate(pairs)]
    for c in copies:
        c.start()
    for c in copies:
        c.wait()


def own_edges_kernel(flags, own, cot, first, second, far, sems):
    pairs = []
    for out, up in ((first, flags[5]), (second, 1 - flags[5])):
        y, cc = up * (16 - YH), up * 7
        for x in range(2):
            pairs.append((own.at[x, pl.ds(y, YH)], out.at[x * YH : (x + 1) * YH]))
        pairs.append((cot.at[pl.ds(cc, 1)], out.at[2 * YH : 2 * YH + 1]))
    y = (1 - flags[5]) * (16 - YH)
    pairs.append((own.at[flags[4], pl.ds(y, YH)], far))
    start_and_wait(pairs, sems)


def corner_edges_kernel(flags, xa, xb, first, second):
    at = flags[5] * (16 - YH)
    for n in range(YH):
        first[n] = xa[at + n]
        first[YH + n] = xb[at + n]
        second[n] = xb[16 - YH - at + n]


def interior_kernel(flags, own, xa, xb, weight, v2, slope, pooled):
    f = [flags[i] > 0 for i in range(6)]
    for y in range(16):
        at = slice(y * L, (y + 1) * L)
        v2[0:64, at] = take(f[0], pick(f[4], xb[y], xa[y]))
        v2[64:128, at] = own[0, y]
        v2[128:192, at] = own[1, y]
        v2[192:256, at] = take(f[1], pick(f[4], xa[y], xb[y]))
    lane = iota((128, L), 1)
    slps, means = forward(weight, taps(v2, 1, 12), 12, lane)
    for n in range(12):
        slope[:, n * L : (n + 1) * L] = slps[n]
    for t in range(6):
        pooled[:, t * L : (t + 1) * L] = means[t]


def border_kernel(
    flags, v2, mid, aa, ab, nb, ba, bb, weight, slope_lo, slope_hi, pooled, vedge, window
):
    f = [flags[i] > 0 for i in range(6)]
    lane = iota((128, L), 1)
    for side, ok in enumerate((f[2], f[3])):
        even = f[5] if side == 1 else jnp.logical_not(f[5])
        win = window.at[side]
        first = 0 if side == 0 else 3
        for y in range(YH):
            at = slice((first + y) * L, (first + y + 1) * L)
            xs = [pick(even, ba[y], nb[y]), pick(even, ba[YH + y], bb[y])]
            win[0:64, at] = take(ok & f[0], pick(f[4], xs[1], xs[0]))
            win[64:128, at] = take(ok, pick(even, aa[y], ab[y]))
            win[128:192, at] = take(ok, pick(even, aa[YH + y], ab[YH + y]))
            win[192:256, at] = take(ok & f[1], pick(f[4], xs[0], xs[1]))
        if side == 0:
            win[:, YH * L :] = v2[:, : 3 * L]
            vedge[:, :L] = win[:, 4 * L : 5 * L]
        else:
            win[:, : 3 * L] = v2[:, 13 * L :]
            vedge[:, L:] = win[:, 3 * L : 4 * L]
    both = jnp.concatenate([taps(window.at[side], 0, 6) for side in range(2)], axis=1)
    slps, means = forward(weight, both, 12, lane)
    for n in range(2):
        slope_lo[:, n * L : (n + 1) * L] = slps[4 + n]
        slope_hi[:, n * L : (n + 1) * L] = slps[6 + n]
    means = (
        [take(f[2], m) for m in means[:2]]
        + [means[2]]
        + [mid[:, t * L : (t + 1) * L] for t in range(6)]
        + [means[3]]
        + [take(f[3], m) for m in means[4:]]
    )
    rows = [jnp.concatenate([means[t], means[t + 5]], axis=1) for t in range(7)]
    packed = dot(jnp.concatenate(rows, axis=0), pack_matrix()).astype(BF)
    for t in range(7):
        pooled[:, t * L : (t + 1) * L] = packed[t * 64 : (t + 1) * 64]


def beside_kernel(flags, aa, cot, ab, v2, vedge, cc, vt):
    f = [flags[i] > 0 for i in range(6)]
    at = 2 * YH
    tiles = (
        [take(f[2], pick(f[5], ab[at], aa[at]))]
        + [cot[n] for n in range(8)]
        + [take(f[3], pick(f[5], aa[at], ab[at]))]
    )
    for t in range(5):
        pair = jnp.concatenate([tiles[t], tiles[t + 5]], axis=0)
        cc[:, t * L : (t + 1) * L] = pair.astype(F32).T
    for y in range(18):
        tile = vedge[:, :L] if y == 0 else vedge[:, L:] if y == 17 else v2[:, (y - 1) * L : y * L]
        vt[y * L : (y + 1) * L, :] = tile.astype(F32).T.astype(BF)


def coarse_kernel(flags, own, a, b, cc, weight, w_part, p2, gpc, first, second):
    f = [flags[i] > 0 for i in range(6)]
    p2[0:64, :] = take(f[0], pick(f[4], b[...], a[...]))
    p2[64:128, :] = own[...]
    p2[128:192, :] = take(f[1], pick(f[4], a[...], b[...]))
    lane = iota((128, L), 1)
    acc = dot(weight[...], taps(p2, 0, 5))
    for t, pre in enumerate(combine(acc, 128, 5, lane, 64)):
        _, slp = slopes(pre)
        tile = (cc[:, t * L : (t + 1) * L] * slp).astype(BF)
        gpc[:, t * L : (t + 1) * L] = tile
        if t < 2:
            other = pltpu.roll(tile.astype(F32), 64, 1).astype(BF)
            gpc[:, (t + 5) * L : (t + 6) * L] = other
    acc = dot(w_part[...], taps(gpc, 0, 5))
    for t, val in enumerate(combine(acc, 128, 5, lane, 64)):
        at = slice(t * L, (t + 1) * L)
        val = val.astype(BF)
        first[:, at] = pick(f[4], val[:64], val[64:])
        second[:, at] = pick(f[4], val[64:], val[:64])


def nt(a, b):
    return lax.dot_general(a, b, (((1,), (1,)), ((), ())), preferred_element_type=F32)


def coarse_corr_kernel(scale, flags, p2, gpc, w_own, own, kept, sent0, sent1, sent2, g3, out):
    lane = iota((64, L), 1)
    acc = dot(w_own[...], taps(gpc, 0, 5))
    for t, val in enumerate(combine(acc, 64, 5, lane, 64)):
        own[:, t * L : (t + 1) * L] = val
    lane = iota((128, L), 1)
    for t in range(5):
        at = slice(t * L, (t + 1) * L)
        tile = gpc[:, at].astype(F32)
        if t == 0 or t == 4:
            tile = jnp.where(lane >= 64 if t == 0 else lane < 64, tile, 0.0)
        g3[0:128, at] = shifted(tile, -1, lane, 64).astype(BF)
        g3[128:256, at] = tile.astype(BF)
        g3[256:384, at] = shifted(tile, 1, lane, 64).astype(BF)
    res = nt(taps(p2, 0, 5), g3[...]) * scale
    for j in range(3):
        for k in range(3):
            at = (3 * j + k) * 192
            out[at : at + 192, :] = res[j * 192 : (j + 1) * 192, k * L : (k + 1) * L].astype(BF)
    low, high = out[:HALF, :], out[HALF:, :]
    even = flags[5] > 0
    kept[...] = pick(even, low, high)
    sent = pick(even, high, low)
    part = HALF // 3
    sent0[...], sent1[...], sent2[...] = sent[:part], sent[part : 2 * part], sent[2 * part :]


def gpf_kernel(
    scale,
    flags,
    own,
    a,
    b,
    fc,
    slope_lo,
    slope,
    slope_hi,
    vt,
    kept,
    got0,
    got1,
    got2,
    first,
    second,
    mine,
    u3,
    pack,
):
    f = [flags[i] > 0 for i in range(6)]
    lane = iota((64, L), 1)
    rows = []
    for t in range(5):
        at = slice(t * L, (t + 1) * L)
        lo, hi = pick(f[4], b[:, at], a[:, at]), pick(f[4], a[:, at], b[:, at])
        total = own[:, at] + take(f[0], lo).astype(F32) + take(f[1], hi).astype(F32)
        main = total.astype(BF)
        rest = (total - main.astype(F32)).astype(BF)
        rows.append(jnp.concatenate([main, rest], axis=1))
    spread = spread_matrix()
    full = dot(jnp.concatenate(rows, axis=0), jnp.concatenate([spread, spread], axis=0))
    gps = [full[64 * t : 64 * t + 64, :L] for t in range(5)]
    gps += [full[64 * t : 64 * t + 64, L:] for t in range(3)]
    for m, gp in enumerate(gps):
        add = gp * 0.125
        for n in (2 * m, 2 * m + 1):
            if n < 2:
                slp = slope_lo[:, n * L : (n + 1) * L]
            elif n < 14:
                slp = slope[:, (n - 2) * L : (n - 1) * L]
            else:
                slp = slope_hi[:, (n - 14) * L : (n - 13) * L]
            rows, at = [], slice(n * L, (n + 1) * L)
            for x in range(2):
                val = (fc[x, n].astype(F32) + add) * slp[x * 64 : (x + 1) * 64]
                rows.append(val.astype(BF))
                tile = rows[x].astype(F32)
                u3[x * 64 : x * 64 + 64, at] = shifted(tile, -1, lane).astype(BF)
                u3[128 + x * 64 : 192 + x * 64, at] = rows[x]
                u3[256 + x * 64 : 320 + x * 64, at] = shifted(tile, 1, lane).astype(BF)
            first[n] = pick(f[4], rows[1], rows[0])
            second[n] = pick(f[4], rows[0], rows[1])
    halves = []
    for j in range(3):
        res = dot(u3[...], vt[j * L : (j + 16) * L, :]) * scale
        for k in range(3):
            both = res[k * L : k * L + 64] + pltpu.roll(res[k * L + 64 : (k + 1) * L], 192, 1)
            at = (3 * j + k) * 64
            pack[at : at + 64, :] = both[:, :L]
            halves.append(both[:, L:])
    halves.append(jnp.zeros((64, L), F32))
    lane = iota((64, L), 1)
    for n in range(5):
        packed = jnp.where(lane < 64, halves[2 * n], pltpu.roll(halves[2 * n + 1], 64, 1))
        pack[576 + 64 * n : 640 + 64 * n, :] = packed
    got = jnp.concatenate([got0[...], got1[...], got2[...]], axis=0)
    coarse = kept[...].astype(F32) + got.astype(F32)
    none = jnp.zeros((R, L), F32)
    for n in range(128):
        at = slice(n * R, (n + 1) * R)
        top = coarse[at] if n < HALF // R else none
        low = pack[at, :] if n < 896 // R else none
        mine[n] = jnp.concatenate([top, low], axis=0).astype(BF)


def gradient_edges_kernel(flags, a, b, c, d, first, second):
    for out, up in ((first, flags[5]), (second, 1 - flags[5])):
        for n, rows in enumerate((a, b, c, d)):
            out[n] = rows[up * 15]


def input_grad_kernel(flags, first, second, a, b, ea, eb, weight, out, g2):
    f = [flags[i] > 0 for i in range(6)]
    for y in range(18):
        if y == 0:
            tiles, ok = [pick(f[5], eb[n], ea[n]) for n in range(4)], f[2]
        elif y == 17:
            tiles, ok = [pick(f[5], ea[n], eb[n]) for n in range(4)], f[3]
        else:
            tiles, ok = [ref[y - 1] for ref in (first, second, a, b)], None
        one, two, lo, hi = tiles
        at = slice(y * L, (y + 1) * L)
        g2[0:64, at] = take(ok, take(f[0], pick(f[4], hi, lo)))
        g2[64:128, at] = take(ok, pick(f[4], two, one))
        g2[128:192, at] = take(ok, pick(f[4], one, two))
        g2[192:256, at] = take(ok, take(f[1], pick(f[4], lo, hi)))
    lane = iota((128, L), 1)
    for t in range(4):
        acc = dot(weight[...], taps(g2, 4 * t, 4))
        for n, val in enumerate(combine(acc, 128, 4, lane)):
            val = val.astype(BF)
            out[0, 4 * t + n] = val[:64]
            out[1, 4 * t + n] = val[64:]


def sum_kernel(parts, out):
    sums = []
    for core in range(2):
        total = parts[core].astype(F32)
        for n in range(core + 2, 128, 2):
            total = total + parts[n].astype(F32)
        sums.append(total)
    total = jnp.concatenate([sums[0][:R], sums[1][:R], sums[0][R:] + sums[1][R:]], axis=0)
    total = total.astype(BF)
    for n in range(128):
        out[n] = total


def unpack_kernel(got, fine, coarse):
    def coarse_rows(q):
        half, at = q // (HALF // R), q % (HALF // R)
        return got[at].astype(F32)[half * R : (half + 1) * R]

    for j in range(3):
        for k in range(3):
            for i in range(3):
                q = ((3 * j + k) * 192 + i * 64) // R
                rows = [coarse_rows(q + m) for m in range(64 // R)]
                coarse[i, j, k] = jnp.concatenate(rows, axis=0)

    def tile(n):
        rows = [got[m].astype(F32)[2 * R :] for m in range(n * 64 // R, (n + 1) * 64 // R)]
        return jnp.concatenate(rows, axis=0).T

    for n in range(9):
        part = tile(n)
        fine[0, n // 3, n % 3] = part[:64]
        fine[1, n // 3, n % 3] = part[64:]
    for n in range(5):
        part = tile(9 + n)
        for h in range(2):
            at = 2 * n + h
            if at < 9:
                fine[2, at // 3, at % 3] = part[64 * h : 64 * h + 64]


def call(kernel, name, outs, args, scratch=(), flags=True, macs=0, copies=0):
    space = pl.ANY if copies else pltpu.VMEM
    specs = [pl.BlockSpec(memory_space=space) for _ in args]
    if flags:
        specs[0] = pl.BlockSpec(memory_space=pltpu.SMEM)
    moved = sum(a.size * a.dtype.itemsize for a in args)
    shapes = tuple(jax.ShapeDtypeStruct(*o) for o in outs)
    if copies:
        scratch = [pltpu.SemaphoreType.DMA((copies,))]
    got = pl.pallas_call(
        kernel,
        out_shape=shapes,
        in_specs=specs,
        out_specs=tuple(pl.BlockSpec(memory_space=space) for _ in shapes),
        scratch_shapes=list(scratch),
        compiler_params=pltpu.CompilerParams(vmem_limit_bytes=VMEM),
        cost_estimate=pl.CostEstimate(flops=2 * macs, bytes_accessed=moved, transcendentals=0),
        name=name,
    )(*args)
    return got if len(shapes) > 1 else got[0]


def swaps(first, second, axis):
    count = lax.axis_size(axis)
    pairs = [(i, i ^ 1) for i in range(count)]
    others = [(0, 0), (count - 1, count - 1)] + [(i, ((i - 1) ^ 1) + 1) for i in range(1, count - 1)]
    other = lax.ppermute(second, axis, others)
    return lax.ppermute(first, axis, pairs), other


def diagonal_swap(far):
    turn = (0, 2, 1, 3)
    pairs = [(4 * i + j, 4 * (i ^ 1) + turn[j]) for i in range(32) for j in range(4)]
    return lax.ppermute(far, ("slab", "sub"), pairs)


def on_device(inputs, fine_cot, coarse_cot, weight_fine, weight_coarse):
    slab, sub = lax.axis_index("slab"), lax.axis_index("sub")
    flags = jnp.stack(
        [slab > 0, slab < 31, sub > 0, sub < 3, slab % 2 == 0, sub % 2 == 0]
    ).astype(jnp.int32)
    cot = jnp.swapaxes(coarse_cot[0], 1, 2)

    odd = slab % 2
    xa, xb = swaps(
        lax.dynamic_index_in_dim(inputs, 1 - odd, 0, False),
        lax.dynamic_index_in_dim(inputs, odd, 0, False),
        "slab",
    )
    own_edge = ((2 * YH + 1, 64, L), BF)
    corner = ((YH, 64, L), BF)
    first, second, far = call(
        own_edges_kernel,
        "own_edges",
        (own_edge, own_edge, corner),
        (flags, inputs, cot),
        copies=7,
    )
    aa, ab = swaps(first, second, "sub")
    nb = diagonal_swap(far)
    w_fwd, w_bwd, c_fwd, c_own, c_part = call(
        prepare_kernel,
        "prepare_weights",
        (
            ((384, 768), BF),
            ((384, 768), BF),
            ((384, 576), BF),
            ((192, 384), BF),
            ((384, 384), BF),
        ),
        (weight_fine, weight_coarse),
        flags=False,
    )
    xa, xb, w_fwd = lax.optimization_barrier((xa, xb, w_fwd))
    first, second = call(
        corner_edges_kernel, "corner_edges", (((2 * YH, 64, L), BF), corner), (flags, xa, xb)
    )
    ba, bb = swaps(first, second, "sub")
    v2, slope, mid = call(
        interior_kernel,
        "fine_forward_interior",
        (((256, 16 * L), BF), ((128, 12 * L), F32), ((64, 6 * L), BF)),
        (flags, inputs, xa, xb, w_fwd),
        macs=384 * 768 * 12 * L,
    )
    slope_lo, slope_hi, pooled, vedge = call(
        border_kernel,
        "fine_forward_border",
        (((128, 2 * L), F32), ((128, 2 * L), F32), ((64, 7 * L), BF), ((256, 2 * L), BF)),
        (flags, v2, mid, aa, ab, nb, ba, bb, w_fwd),
        scratch=[pltpu.VMEM((2, 256, 8 * L), BF)],
        macs=384 * 768 * 12 * L,
    )
    pa, pb = swaps(pooled, pooled, "slab")
    cc, vt = call(
        beside_kernel,
        "cotangent_and_turned_inputs",
        (((128, 5 * L), F32), ((18 * L, 256), BF)),
        (flags, aa, cot, ab, v2, vedge),
    )
    p2, gpc, first, second = call(
        coarse_kernel,
        "coarse_forward",
        (
            ((192, 7 * L), BF),
            ((128, 7 * L), BF),
            ((64, 5 * L), BF),
            ((64, 5 * L), BF),
        ),
        (flags, pooled, pa, pb, cc, c_fwd, c_part),
        macs=384 * 960 * 6 * L,
    )
    ga, gb = swaps(first, second, "slab")
    third = ((HALF // 3, L), BF)
    own, kept, *sent = call(
        functools.partial(coarse_corr_kernel, 1.0 / 256.0),
        "coarse_correlate",
        (((64, 5 * L), F32), ((HALF, L), BF), third, third, third),
        (flags, p2, gpc, c_own),
        scratch=[pltpu.VMEM((384, 5 * L), BF), pltpu.VMEM((2 * HALF, L), BF)],
        macs=384 * 768 * 6 * L,
    )
    got0, got1, got2 = (lax.ppermute(part, "sub", [(0, 1), (1, 0), (2, 3), (3, 2)]) for part in sent)
    first, second, mine = call(
        functools.partial(gpf_kernel, 524288.0**-0.5),
        "fine_gradient",
        (((16, 64, L), BF), ((16, 64, L), BF), ((128, 2 * R, L), BF)),
        (
            flags,
            own,
            ga,
            gb,
            fine_cot,
            slope_lo,
            slope,
            slope_hi,
            vt,
            kept,
            got0,
            got1,
            got2,
        ),
        scratch=[
            pltpu.VMEM((384, 16 * L), BF),
            pltpu.VMEM((896, L), F32),
        ],
        macs=384 * 768 * 16 * L,
    )
    ha, hb = swaps(first, second, "slab")
    shares = lax.all_to_all(mine.reshape(128 * 2 * R, L), ("slab", "sub"), 0, 0, tiled=True)
    total = call(
        sum_kernel,
        "sum_shares",
        (((128, 3 * R, L), BF),),
        (shares.reshape(128, 2 * R, L),),
        flags=False,
    )
    everything = lax.all_to_all(total.reshape(128 * 3 * R, L), ("slab", "sub"), 0, 0, tiled=True)
    one, two = call(
        gradient_edges_kernel,
        "gradient_edges",
        (((4, 64, L), BF), ((4, 64, L), BF)),
        (flags, first, second, ha, hb),
        macs=20 * 384 * 768 * 16 * L,
    )
    ea, eb = swaps(one, two, "sub")
    grad_input = call(
        input_grad_kernel,
        "input_gradient",
        (((2, 16, 64, L), BF),),
        (flags, first, second, ha, hb, ea, eb, w_bwd),
        scratch=[pltpu.VMEM((256, 18 * L), BF)],
        macs=384 * 768 * 16 * L,
    )
    grad_fine, grad_coarse = call(
        unpack_kernel,
        "unpack",
        (((3, 3, 3, 64, 64), F32), ((3, 3, 3, 64, 128), F32)),
        (everything.reshape(128, 3 * R, L),),
        flags=False,
    )
    return (grad_input, grad_fine, grad_coarse)


def solution(mesh):
    in_specs = (
        P("slab", "sub", None, None),
        P("slab", "sub", None, None),
        P("slab", "sub", None, None),
        P(),
        P(),
    )
    out_specs = (P("slab", "sub", None, None), P(), P())
    return jax.shard_map(
        on_device, mesh=mesh, in_specs=in_specs, out_specs=out_specs, check_vma=False
    )
```

```python
import functools

import jax
import jax.numpy as jnp
from jax import lax
from jax.experimental import pallas as pl
from jax.experimental.pallas import tpu as pltpu
from jax.sharding import PartitionSpec as P

L = 128
YH = 5
BF = jnp.bfloat16
F32 = jnp.float32
R = 8
HALF = 864
VMEM = 20 * 1024 * 1024


def iota(shape, dim):
    return lax.broadcasted_iota(jnp.int32, shape, dim)


def shifted(tile, by, lane, width=L):
    out = pltpu.roll(tile, by % L, 1)
    z = lane % width
    return jnp.where(z >= by if by > 0 else z < width + by, out, 0.0)


def combine(acc, rows, tiles, lane, width=L):
    out = []
    for t in range(tiles):
        part = acc[:, t * L : (t + 1) * L]
        out.append(
            shifted(part[:rows], 1, lane, width)
            + part[rows : 2 * rows]
            + shifted(part[2 * rows :], -1, lane, width)
        )
    return out


def slopes(value):
    sig = jax.nn.sigmoid(value)
    return sig, sig * (1.0 + value * (1.0 - sig))


def dot(a, b):
    return jnp.dot(a, b, preferred_element_type=F32)


def spread_matrix():
    row, col = iota((L, 2 * L), 0), iota((L, 2 * L), 1)
    return jnp.where(row == (col // L) * 64 + (col % L) // 2, 1.0, 0.0).astype(BF)


def pick(cond, a, b):
    return jnp.where(cond, a, b)


def take(ok, tile):
    return tile if ok is None else jnp.where(ok, tile, jnp.zeros_like(tile))


def pack_matrix():
    row, col = iota((2 * L, L), 0), iota((2 * L, L), 1)
    keep = (row % 2 == 0) & (col == (row // L) * 64 + (row % L) // 2)
    return jnp.where(keep, 1.0, 0.0).astype(BF)


def taps(ref, at, tiles):
    return jnp.concatenate([ref[:, (at + j) * L : (at + j + tiles) * L] for j in range(3)], axis=0)


def forward(weight, cells, tiles, lane):
    acc = dot(weight[...], cells)
    sums, slps = [], []
    for pre in combine(acc, 128, tiles, lane):
        sig, slp = slopes(pre)
        act = pre * sig
        sums.append(act[:64] + act[64:])
        slps.append(slp)
    means = []
    for t in range(0, tiles, 2):
        total = sums[t] + sums[t + 1]
        means.append(((total + pltpu.roll(total, L - 1, 1)) * 0.125).astype(BF))
    return slps, means


def prepare_kernel(wf, wc, wfwd, wbwd, cfwd, cown, cpart):
    def fine(i, j, k):
        return wf[i, j, k] if 0 <= i < 3 else jnp.zeros((64, 64), BF)

    for j in range(3):
        for k in range(3):
            for x in range(2):
                rows = slice(k * 128 + x * 64, k * 128 + x * 64 + 64)
                for h in range(2):
                    i = 2 * h - x
                    cols = slice(j * 256 + h * L, j * 256 + (h + 1) * L)
                    pair = jnp.concatenate([fine(i, j, k), fine(i + 1, j, k)], axis=0)
                    wfwd[rows, cols] = pair.astype(F32).T.astype(BF)
                    wbwd[rows, cols] = jnp.concatenate(
                        [fine(2 - i, 2 - j, 2 - k), fine(1 - i, 2 - j, 2 - k)], axis=1
                    )
    for k in range(3):
        full = jnp.concatenate([wc[i, j, k] for j in range(3) for i in range(3)], axis=0)
        cfwd[k * 128 : (k + 1) * 128, :] = full.astype(F32).T.astype(BF)
        for j in range(3):
            at = slice(j * L, (j + 1) * L)
            cown[k * 64 : (k + 1) * 64, at] = wc[1, 2 - j, 2 - k]
            cpart[k * 128 : k * 128 + 64, at] = wc[2, 2 - j, 2 - k]
            cpart[k * 128 + 64 : (k + 1) * 128, at] = wc[0, 2 - j, 2 - k]


def start_and_wait(pairs, sems):
    copies = [pltpu.make_async_copy(a, b, sems.at[n]) for n, (a, b) in enumerate(pairs)]
    for c in copies:
        c.start()
    for c in copies:
        c.wait()


def own_edges_kernel(flags, own, cot, first, second, far, sems):
    pairs = []
    for out, up in ((first, flags[5]), (second, 1 - flags[5])):
        y, cc = up * (16 - YH), up * 7
        for x in range(2):
            pairs.append((own.at[x, pl.ds(y, YH)], out.at[x * YH : (x + 1) * YH]))
        pairs.append((cot.at[pl.ds(cc, 1)], out.at[2 * YH : 2 * YH + 1]))
    y = (1 - flags[5]) * (16 - YH)
    pairs.append((own.at[flags[4], pl.ds(y, YH)], far))
    start_and_wait(pairs, sems)


def corner_edges_kernel(flags, xa, xb, first, second):
    at = flags[5] * (16 - YH)
    for n in range(YH):
        first[n] = xa[at + n]
        first[YH + n] = xb[at + n]
        second[n] = xb[16 - YH - at + n]


def interior_kernel(flags, own, xa, xb, weight, v2, slope, pooled):
    f = [flags[i] > 0 for i in range(6)]
    for y in range(16):
        at = slice(y * L, (y + 1) * L)
        v2[0:64, at] = take(f[0], pick(f[4], xb[y], xa[y]))
        v2[64:128, at] = own[0, y]
        v2[128:192, at] = own[1, y]
        v2[192:256, at] = take(f[1], pick(f[4], xa[y], xb[y]))
    lane = iota((128, L), 1)
    slps, means = forward(weight, taps(v2, 1, 12), 12, lane)
    for n in range(12):
        slope[:, n * L : (n + 1) * L] = slps[n]
    for t in range(6):
        pooled[:, t * L : (t + 1) * L] = means[t]


def border_kernel(
    flags, v2, mid, aa, ab, nb, ba, bb, weight, slope_lo, slope_hi, pooled, vedge, window
):
    f = [flags[i] > 0 for i in range(6)]
    lane = iota((128, L), 1)
    for side, ok in enumerate((f[2], f[3])):
        even = f[5] if side == 1 else jnp.logical_not(f[5])
        win = window.at[side]
        first = 0 if side == 0 else 3
        for y in range(YH):
            at = slice((first + y) * L, (first + y + 1) * L)
            xs = [pick(even, ba[y], nb[y]), pick(even, ba[YH + y], bb[y])]
            win[0:64, at] = take(ok & f[0], pick(f[4], xs[1], xs[0]))
            win[64:128, at] = take(ok, pick(even, aa[y], ab[y]))
            win[128:192, at] = take(ok, pick(even, aa[YH + y], ab[YH + y]))
            win[192:256, at] = take(ok & f[1], pick(f[4], xs[0], xs[1]))
        if side == 0:
            win[:, YH * L :] = v2[:, : 3 * L]
            vedge[:, :L] = win[:, 4 * L : 5 * L]
        else:
            win[:, : 3 * L] = v2[:, 13 * L :]
            vedge[:, L:] = win[:, 3 * L : 4 * L]
    both = jnp.concatenate([taps(window.at[side], 0, 6) for side in range(2)], axis=1)
    slps, means = forward(weight, both, 12, lane)
    for n in range(2):
        slope_lo[:, n * L : (n + 1) * L] = slps[4 + n]
        slope_hi[:, n * L : (n + 1) * L] = slps[6 + n]
    means = (
        [take(f[2], m) for m in means[:2]]
        + [means[2]]
        + [mid[:, t * L : (t + 1) * L] for t in range(6)]
        + [means[3]]
        + [take(f[3], m) for m in means[4:]]
    )
    rows = [jnp.concatenate([means[t], means[t + 5]], axis=1) for t in range(7)]
    packed = dot(jnp.concatenate(rows, axis=0), pack_matrix()).astype(BF)
    for t in range(7):
        pooled[:, t * L : (t + 1) * L] = packed[t * 64 : (t + 1) * 64]


def beside_kernel(flags, aa, cot, ab, v2, vedge, cc, vt):
    f = [flags[i] > 0 for i in range(6)]
    at = 2 * YH
    tiles = (
        [take(f[2], pick(f[5], ab[at], aa[at]))]
        + [cot[n] for n in range(8)]
        + [take(f[3], pick(f[5], aa[at], ab[at]))]
    )
    for t in range(5):
        pair = jnp.concatenate([tiles[t], tiles[t + 5]], axis=0)
        cc[:, t * L : (t + 1) * L] = pair.astype(F32).T
    for y in range(18):
        tile = vedge[:, :L] if y == 0 else vedge[:, L:] if y == 17 else v2[:, (y - 1) * L : y * L]
        vt[y * L : (y + 1) * L, :] = tile.astype(F32).T.astype(BF)


def coarse_kernel(flags, own, a, b, cc, weight, w_part, p2, gpc, first, second):
    f = [flags[i] > 0 for i in range(6)]
    p2[0:64, :] = take(f[0], pick(f[4], b[...], a[...]))
    p2[64:128, :] = own[...]
    p2[128:192, :] = take(f[1], pick(f[4], a[...], b[...]))
    lane = iota((128, L), 1)
    acc = dot(weight[...], taps(p2, 0, 5))
    for t, pre in enumerate(combine(acc, 128, 5, lane, 64)):
        _, slp = slopes(pre)
        tile = (cc[:, t * L : (t + 1) * L] * slp).astype(BF)
        gpc[:, t * L : (t + 1) * L] = tile
        if t < 2:
            other = pltpu.roll(tile.astype(F32), 64, 1).astype(BF)
            gpc[:, (t + 5) * L : (t + 6) * L] = other
    acc = dot(w_part[...], taps(gpc, 0, 5))
    for t, val in enumerate(combine(acc, 128, 5, lane, 64)):
        at = slice(t * L, (t + 1) * L)
        val = val.astype(BF)
        first[:, at] = pick(f[4], val[:64], val[64:])
        second[:, at] = pick(f[4], val[64:], val[:64])


def nt(a, b):
    return lax.dot_general(a, b, (((1,), (1,)), ((), ())), preferred_element_type=F32)


def coarse_corr_kernel(scale, flags, p2, gpc, w_own, own, kept, sent0, sent1, sent2, g3, out):
    lane = iota((64, L), 1)
    acc = dot(w_own[...], taps(gpc, 0, 5))
    for t, val in enumerate(combine(acc, 64, 5, lane, 64)):
        own[:, t * L : (t + 1) * L] = val
    lane = iota((128, L), 1)
    for t in range(5):
        at = slice(t * L, (t + 1) * L)
        tile = gpc[:, at].astype(F32)
        if t == 0 or t == 4:
            tile = jnp.where(lane >= 64 if t == 0 else lane < 64, tile, 0.0)
        g3[0:128, at] = shifted(tile, -1, lane, 64).astype(BF)
        g3[128:256, at] = tile.astype(BF)
        g3[256:384, at] = shifted(tile, 1, lane, 64).astype(BF)
    res = nt(taps(p2, 0, 5), g3[...]) * scale
    for j in range(3):
        for k in range(3):
            at = (3 * j + k) * 192
            out[at : at + 192, :] = res[j * 192 : (j + 1) * 192, k * L : (k + 1) * L].astype(BF)
    low, high = out[:HALF, :], out[HALF:, :]
    even = flags[5] > 0
    kept[...] = pick(even, low, high)
    sent = pick(even, high, low)
    part = HALF // 3
    sent0[...], sent1[...], sent2[...] = sent[:part], sent[part : 2 * part], sent[2 * part :]


def gpf_kernel(
    scale,
    flags,
    own,
    a,
    b,
    fc,
    slope_lo,
    slope,
    slope_hi,
    vt,
    kept,
    got0,
    got1,
    got2,
    first,
    second,
    mine,
    u3,
    pack,
    held,
    sems,
):
    f = [flags[i] > 0 for i in range(6)]
    lane = iota((64, L), 1)
    rows = []
    for t in range(5):
        at = slice(t * L, (t + 1) * L)
        lo, hi = pick(f[4], b[:, at], a[:, at]), pick(f[4], a[:, at], b[:, at])
        total = own[:, at] + take(f[0], lo).astype(F32) + take(f[1], hi).astype(F32)
        main = total.astype(BF)
        rest = (total - main.astype(F32)).astype(BF)
        rows.append(jnp.concatenate([main, rest], axis=1))
    spread = spread_matrix()
    full = dot(jnp.concatenate(rows, axis=0), jnp.concatenate([spread, spread], axis=0))
    gps = [full[64 * t : 64 * t + 64, :L] for t in range(5)]
    gps += [full[64 * t : 64 * t + 64, L:] for t in range(3)]
    for m, gp in enumerate(gps):
        add = gp * 0.125
        for n in (2 * m, 2 * m + 1):
            if n < 2:
                slp = slope_lo[:, n * L : (n + 1) * L]
            elif n < 14:
                slp = slope[:, (n - 2) * L : (n - 1) * L]
            else:
                slp = slope_hi[:, (n - 14) * L : (n - 13) * L]
            rows, at = [], slice(n * L, (n + 1) * L)
            for x in range(2):
                val = (fc[x, n].astype(F32) + add) * slp[x * 64 : (x + 1) * 64]
                rows.append(val.astype(BF))
                tile = rows[x].astype(F32)
                u3[x * 64 : x * 64 + 64, at] = shifted(tile, -1, lane).astype(BF)
                u3[128 + x * 64 : 192 + x * 64, at] = rows[x]
                u3[256 + x * 64 : 320 + x * 64, at] = shifted(tile, 1, lane).astype(BF)
            first[n] = pick(f[4], rows[1], rows[0])
            second[n] = pick(f[4], rows[0], rows[1])
    got = jnp.concatenate([got0[...], got1[...], got2[...]], axis=0)
    coarse = kept[...].astype(F32) + got.astype(F32)
    none = jnp.zeros((R, L), F32)
    copies = []

    def send(start, stop):
        for n in range(start, stop):
            at = slice(n * R, (n + 1) * R)
            top = coarse[at] if n < HALF // R else none
            low = pack[at, :] if n < 896 // R else none
            held[n] = jnp.concatenate([top, low], axis=0).astype(BF)
        part = pl.ds(start, stop - start)
        copies.append(pltpu.make_async_copy(held.at[part], mine.at[part], sems.at[len(copies)]))
        copies[-1].start()

    halves = []
    for j in range(3):
        res = dot(u3[...], vt[j * L : (j + 16) * L, :]) * scale
        for k in range(3):
            both = res[k * L : k * L + 64] + pltpu.roll(res[k * L + 64 : (k + 1) * L], 192, 1)
            at = (3 * j + k) * 64
            pack[at : at + 64, :] = both[:, :L]
            halves.append(both[:, L:])
        send(24 * j, 24 * j + 24)
    halves.append(jnp.zeros((64, L), F32))
    lane = iota((64, L), 1)
    for n in range(5):
        packed = jnp.where(lane < 64, halves[2 * n], pltpu.roll(halves[2 * n + 1], 64, 1))
        pack[576 + 64 * n : 640 + 64 * n, :] = packed
    send(72, 128)
    for copy in copies:
        copy.wait()


def gradient_edges_kernel(flags, a, b, c, d, first, second):
    for out, up in ((first, flags[5]), (second, 1 - flags[5])):
        for n, rows in enumerate((a, b, c, d)):
            out[n] = rows[up * 15]


def input_grad_kernel(flags, first, second, a, b, ea, eb, weight, out, g2):
    f = [flags[i] > 0 for i in range(6)]
    for y in range(18):
        if y == 0:
            tiles, ok = [pick(f[5], eb[n], ea[n]) for n in range(4)], f[2]
        elif y == 17:
            tiles, ok = [pick(f[5], ea[n], eb[n]) for n in range(4)], f[3]
        else:
            tiles, ok = [ref[y - 1] for ref in (first, second, a, b)], None
        one, two, lo, hi = tiles
        at = slice(y * L, (y + 1) * L)
        g2[0:64, at] = take(ok, take(f[0], pick(f[4], hi, lo)))
        g2[64:128, at] = take(ok, pick(f[4], two, one))
        g2[128:192, at] = take(ok, pick(f[4], one, two))
        g2[192:256, at] = take(ok, take(f[1], pick(f[4], lo, hi)))
    lane = iota((128, L), 1)
    for t in range(4):
        acc = dot(weight[...], taps(g2, 4 * t, 4))
        for n, val in enumerate(combine(acc, 128, 4, lane)):
            val = val.astype(BF)
            out[0, 4 * t + n] = val[:64]
            out[1, 4 * t + n] = val[64:]


def sum_kernel(parts, out):
    sums = []
    for core in range(2):
        total = parts[core].astype(F32)
        for n in range(core + 2, 128, 2):
            total = total + parts[n].astype(F32)
        sums.append(total)
    total = jnp.concatenate([sums[0][:R], sums[1][:R], sums[0][R:] + sums[1][R:]], axis=0)
    total = total.astype(BF)
    for n in range(128):
        out[n] = total


def unpack_kernel(got, fine, coarse):
    def coarse_rows(q):
        half, at = q // (HALF // R), q % (HALF // R)
        return got[at].astype(F32)[half * R : (half + 1) * R]

    for j in range(3):
        for k in range(3):
            for i in range(3):
                q = ((3 * j + k) * 192 + i * 64) // R
                rows = [coarse_rows(q + m) for m in range(64 // R)]
                coarse[i, j, k] = jnp.concatenate(rows, axis=0)

    def tile(n):
        rows = [got[m].astype(F32)[2 * R :] for m in range(n * 64 // R, (n + 1) * 64 // R)]
        return jnp.concatenate(rows, axis=0).T

    for n in range(9):
        part = tile(n)
        fine[0, n // 3, n % 3] = part[:64]
        fine[1, n // 3, n % 3] = part[64:]
    for n in range(5):
        part = tile(9 + n)
        for h in range(2):
            at = 2 * n + h
            if at < 9:
                fine[2, at // 3, at % 3] = part[64 * h : 64 * h + 64]


def call(kernel, name, outs, args, scratch=(), flags=True, macs=0, copies=0, far=()):
    space = pl.ANY if copies else pltpu.VMEM
    specs = [pl.BlockSpec(memory_space=space) for _ in args]
    if flags:
        specs[0] = pl.BlockSpec(memory_space=pltpu.SMEM)
    moved = sum(a.size * a.dtype.itemsize for a in args)
    shapes = tuple(jax.ShapeDtypeStruct(*o) for o in outs)
    if copies:
        scratch = [pltpu.SemaphoreType.DMA((copies,))]
    got = pl.pallas_call(
        kernel,
        out_shape=shapes,
        in_specs=specs,
        out_specs=tuple(
            pl.BlockSpec(memory_space=pl.ANY if n in far else space) for n in range(len(shapes))
        ),
        scratch_shapes=list(scratch),
        compiler_params=pltpu.CompilerParams(vmem_limit_bytes=VMEM),
        cost_estimate=pl.CostEstimate(flops=2 * macs, bytes_accessed=moved, transcendentals=0),
        name=name,
    )(*args)
    return got if len(shapes) > 1 else got[0]


def swaps(first, second, axis):
    count = lax.axis_size(axis)
    pairs = [(i, i ^ 1) for i in range(count)]
    others = [(0, 0), (count - 1, count - 1)] + [(i, ((i - 1) ^ 1) + 1) for i in range(1, count - 1)]
    other = lax.ppermute(second, axis, others)
    return lax.ppermute(first, axis, pairs), other


def diagonal_swap(far):
    turn = (0, 2, 1, 3)
    pairs = [(4 * i + j, 4 * (i ^ 1) + turn[j]) for i in range(32) for j in range(4)]
    return lax.ppermute(far, ("slab", "sub"), pairs)


def on_device(inputs, fine_cot, coarse_cot, weight_fine, weight_coarse):
    slab, sub = lax.axis_index("slab"), lax.axis_index("sub")
    flags = jnp.stack(
        [slab > 0, slab < 31, sub > 0, sub < 3, slab % 2 == 0, sub % 2 == 0]
    ).astype(jnp.int32)
    cot = jnp.swapaxes(coarse_cot[0], 1, 2)

    odd = slab % 2
    xa, xb = swaps(
        lax.dynamic_index_in_dim(inputs, 1 - odd, 0, False),
        lax.dynamic_index_in_dim(inputs, odd, 0, False),
        "slab",
    )
    own_edge = ((2 * YH + 1, 64, L), BF)
    corner = ((YH, 64, L), BF)
    first, second, far = call(
        own_edges_kernel,
        "own_edges",
        (own_edge, own_edge, corner),
        (flags, inputs, cot),
        copies=7,
    )
    aa, ab = swaps(first, second, "sub")
    nb = diagonal_swap(far)
    w_fwd, w_bwd, c_fwd, c_own, c_part = call(
        prepare_kernel,
        "prepare_weights",
        (
            ((384, 768), BF),
            ((384, 768), BF),
            ((384, 576), BF),
            ((192, 384), BF),
            ((384, 384), BF),
        ),
        (weight_fine, weight_coarse),
        flags=False,
    )
    xa, xb, w_fwd = lax.optimization_barrier((xa, xb, w_fwd))
    first, second = call(
        corner_edges_kernel, "corner_edges", (((2 * YH, 64, L), BF), corner), (flags, xa, xb)
    )
    ba, bb = swaps(first, second, "sub")
    v2, slope, mid = call(
        interior_kernel,
        "fine_forward_interior",
        (((256, 16 * L), BF), ((128, 12 * L), F32), ((64, 6 * L), BF)),
        (flags, inputs, xa, xb, w_fwd),
        macs=384 * 768 * 12 * L,
    )
    slope_lo, slope_hi, pooled, vedge = call(
        border_kernel,
        "fine_forward_border",
        (((128, 2 * L), F32), ((128, 2 * L), F32), ((64, 7 * L), BF), ((256, 2 * L), BF)),
        (flags, v2, mid, aa, ab, nb, ba, bb, w_fwd),
        scratch=[pltpu.VMEM((2, 256, 8 * L), BF)],
        macs=384 * 768 * 12 * L,
    )
    pa, pb = swaps(pooled, pooled, "slab")
    cc, vt = call(
        beside_kernel,
        "cotangent_and_turned_inputs",
        (((128, 5 * L), F32), ((18 * L, 256), BF)),
        (flags, aa, cot, ab, v2, vedge),
    )
    p2, gpc, first, second = call(
        coarse_kernel,
        "coarse_forward",
        (
            ((192, 7 * L), BF),
            ((128, 7 * L), BF),
            ((64, 5 * L), BF),
            ((64, 5 * L), BF),
        ),
        (flags, pooled, pa, pb, cc, c_fwd, c_part),
        macs=384 * 960 * 6 * L,
    )
    ga, gb = swaps(first, second, "slab")
    third = ((HALF // 3, L), BF)
    own, kept, *sent = call(
        functools.partial(coarse_corr_kernel, 1.0 / 256.0),
        "coarse_correlate",
        (((64, 5 * L), F32), ((HALF, L), BF), third, third, third),
        (flags, p2, gpc, c_own),
        scratch=[pltpu.VMEM((384, 5 * L), BF), pltpu.VMEM((2 * HALF, L), BF)],
        macs=384 * 768 * 6 * L,
    )
    got0, got1, got2 = (lax.ppermute(part, "sub", [(0, 1), (1, 0), (2, 3), (3, 2)]) for part in sent)
    first, second, mine = call(
        functools.partial(gpf_kernel, 524288.0**-0.5),
        "fine_gradient",
        (((16, 64, L), BF), ((16, 64, L), BF), ((128, 2 * R, L), BF)),
        (
            flags,
            own,
            ga,
            gb,
            fine_cot,
            slope_lo,
            slope,
            slope_hi,
            vt,
            kept,
            got0,
            got1,
            got2,
        ),
        scratch=[
            pltpu.VMEM((384, 16 * L), BF),
            pltpu.VMEM((896, L), F32),
            pltpu.VMEM((128, 2 * R, L), BF),
            pltpu.SemaphoreType.DMA((4,)),
        ],
        far=(2,),
        macs=384 * 768 * 16 * L,
    )
    ha, hb = swaps(first, second, "slab")
    shares = lax.all_to_all(mine.reshape(128 * 2 * R, L), ("slab", "sub"), 0, 0, tiled=True)
    total = call(
        sum_kernel,
        "sum_shares",
        (((128, 3 * R, L), BF),),
        (shares.reshape(128, 2 * R, L),),
        flags=False,
    )
    everything = lax.all_to_all(total.reshape(128 * 3 * R, L), ("slab", "sub"), 0, 0, tiled=True)
    one, two = call(
        gradient_edges_kernel,
        "gradient_edges",
        (((4, 64, L), BF), ((4, 64, L), BF)),
        (flags, first, second, ha, hb),
        macs=20 * 384 * 768 * 16 * L,
    )
    ea, eb = swaps(one, two, "sub")
    grad_input = call(
        input_grad_kernel,
        "input_gradient",
        (((2, 16, 64, L), BF),),
        (flags, first, second, ha, hb, ea, eb, w_bwd),
        scratch=[pltpu.VMEM((256, 18 * L), BF)],
        macs=384 * 768 * 16 * L,
    )
    grad_fine, grad_coarse = call(
        unpack_kernel,
        "unpack",
        (((3, 3, 3, 64, 64), F32), ((3, 3, 3, 64, 128), F32)),
        (everything.reshape(128, 3 * R, L),),
        flags=False,
    )
    return (grad_input, grad_fine, grad_coarse)


def solution(mesh):
    in_specs = (
        P("slab", "sub", None, None),
        P("slab", "sub", None, None),
        P("slab", "sub", None, None),
        P(),
        P(),
    )
    out_specs = (P("slab", "sub", None, None), P(), P())
    return jax.shard_map(
        on_device, mesh=mesh, in_specs=in_specs, out_specs=out_specs, check_vma=False
    )
```

```python
import functools

import jax
import jax.numpy as jnp
from jax import lax
from jax.experimental import pallas as pl
from jax.experimental.pallas import tpu as pltpu
from jax.sharding import PartitionSpec as P

L = 128
YH = 5
BF = jnp.bfloat16
F32 = jnp.float32
R = 8
HALF = 864
VMEM = 20 * 1024 * 1024


def iota(shape, dim):
    return lax.broadcasted_iota(jnp.int32, shape, dim)


def shifted(tile, by, lane, width=L):
    out = pltpu.roll(tile, by % L, 1)
    z = lane % width
    return jnp.where(z >= by if by > 0 else z < width + by, out, 0.0)


def combine(acc, rows, tiles, lane, width=L):
    out = []
    for t in range(tiles):
        part = acc[:, t * L : (t + 1) * L]
        out.append(
            shifted(part[:rows], 1, lane, width)
            + part[rows : 2 * rows]
            + shifted(part[2 * rows :], -1, lane, width)
        )
    return out


def slopes(value):
    sig = jax.nn.sigmoid(value)
    return sig, sig * (1.0 + value * (1.0 - sig))


def dot(a, b):
    return jnp.dot(a, b, preferred_element_type=F32)


def spread_matrix():
    row, col = iota((L, 2 * L), 0), iota((L, 2 * L), 1)
    return jnp.where(row == (col // L) * 64 + (col % L) // 2, 1.0, 0.0).astype(BF)


def pick(cond, a, b):
    return jnp.where(cond, a, b)


def take(ok, tile):
    return tile if ok is None else jnp.where(ok, tile, jnp.zeros_like(tile))


def pack_matrix():
    row, col = iota((2 * L, L), 0), iota((2 * L, L), 1)
    keep = (row % 2 == 0) & (col == (row // L) * 64 + (row % L) // 2)
    return jnp.where(keep, 1.0, 0.0).astype(BF)


def taps(ref, at, tiles):
    return jnp.concatenate([ref[:, (at + j) * L : (at + j + tiles) * L] for j in range(3)], axis=0)


def forward(weight, cells, tiles, lane):
    acc = dot(weight[...], cells)
    sums, slps = [], []
    for pre in combine(acc, 128, tiles, lane):
        sig, slp = slopes(pre)
        act = pre * sig
        sums.append(act[:64] + act[64:])
        slps.append(slp)
    means = []
    for t in range(0, tiles, 2):
        total = sums[t] + sums[t + 1]
        means.append(((total + pltpu.roll(total, L - 1, 1)) * 0.125).astype(BF))
    return slps, means


def prepare_kernel(wf, wc, wfwd, wbwd, cfwd, cown, cpart):
    def fine(i, j, k):
        return wf[i, j, k] if 0 <= i < 3 else jnp.zeros((64, 64), BF)

    for j in range(3):
        for k in range(3):
            for x in range(2):
                rows = slice(k * 128 + x * 64, k * 128 + x * 64 + 64)
                for h in range(2):
                    i = 2 * h - x
                    cols = slice(j * 256 + h * L, j * 256 + (h + 1) * L)
                    pair = jnp.concatenate([fine(i, j, k), fine(i + 1, j, k)], axis=0)
                    wfwd[rows, cols] = pair.astype(F32).T.astype(BF)
                    wbwd[rows, cols] = jnp.concatenate(
                        [fine(2 - i, 2 - j, 2 - k), fine(1 - i, 2 - j, 2 - k)], axis=1
                    )
    for k in range(3):
        full = jnp.concatenate([wc[i, j, k] for j in range(3) for i in range(3)], axis=0)
        cfwd[k * 128 : (k + 1) * 128, :] = full.astype(F32).T.astype(BF)
        for j in range(3):
            at = slice(j * L, (j + 1) * L)
            cown[k * 64 : (k + 1) * 64, at] = wc[1, 2 - j, 2 - k]
            cpart[k * 128 : k * 128 + 64, at] = wc[2, 2 - j, 2 - k]
            cpart[k * 128 + 64 : (k + 1) * 128, at] = wc[0, 2 - j, 2 - k]


def start_and_wait(pairs, sems):
    copies = [pltpu.make_async_copy(a, b, sems.at[n]) for n, (a, b) in enumerate(pairs)]
    for c in copies:
        c.start()
    for c in copies:
        c.wait()


def own_edges_kernel(flags, own, cot, first, second, far, sems):
    pairs = []
    for out, up in ((first, flags[5]), (second, 1 - flags[5])):
        y, cc = up * (16 - YH), up * 7
        for x in range(2):
            pairs.append((own.at[x, pl.ds(y, YH)], out.at[x * YH : (x + 1) * YH]))
        pairs.append((cot.at[pl.ds(cc, 1)], out.at[2 * YH : 2 * YH + 1]))
    y = (1 - flags[5]) * (16 - YH)
    pairs.append((own.at[flags[4], pl.ds(y, YH)], far))
    start_and_wait(pairs, sems)


def corner_edges_kernel(flags, xa, xb, first, second):
    at = flags[5] * (16 - YH)
    for n in range(YH):
        first[n] = xa[at + n]
        first[YH + n] = xb[at + n]
        second[n] = xb[16 - YH - at + n]


def interior_kernel(flags, own, xa, xb, weight, v2, slope, pooled):
    f = [flags[i] > 0 for i in range(6)]
    for y in range(16):
        at = slice(y * L, (y + 1) * L)
        v2[0:64, at] = take(f[0], pick(f[4], xb[y], xa[y]))
        v2[64:128, at] = own[0, y]
        v2[128:192, at] = own[1, y]
        v2[192:256, at] = take(f[1], pick(f[4], xa[y], xb[y]))
    lane = iota((128, L), 1)
    slps, means = forward(weight, taps(v2, 1, 12), 12, lane)
    for n in range(12):
        slope[:, n * L : (n + 1) * L] = slps[n]
    for t in range(6):
        pooled[:, t * L : (t + 1) * L] = means[t]


def border_kernel(
    flags, v2, mid, aa, ab, nb, ba, bb, weight, slope_lo, slope_hi, pooled, vedge, window
):
    f = [flags[i] > 0 for i in range(6)]
    lane = iota((128, L), 1)
    for side, ok in enumerate((f[2], f[3])):
        even = f[5] if side == 1 else jnp.logical_not(f[5])
        win = window.at[side]
        first = 0 if side == 0 else 3
        for y in range(YH):
            at = slice((first + y) * L, (first + y + 1) * L)
            xs = [pick(even, ba[y], nb[y]), pick(even, ba[YH + y], bb[y])]
            win[0:64, at] = take(ok & f[0], pick(f[4], xs[1], xs[0]))
            win[64:128, at] = take(ok, pick(even, aa[y], ab[y]))
            win[128:192, at] = take(ok, pick(even, aa[YH + y], ab[YH + y]))
            win[192:256, at] = take(ok & f[1], pick(f[4], xs[0], xs[1]))
        if side == 0:
            win[:, YH * L :] = v2[:, : 3 * L]
            vedge[:, :L] = win[:, 4 * L : 5 * L]
        else:
            win[:, : 3 * L] = v2[:, 13 * L :]
            vedge[:, L:] = win[:, 3 * L : 4 * L]
    both = jnp.concatenate([taps(window.at[side], 0, 6) for side in range(2)], axis=1)
    slps, means = forward(weight, both, 12, lane)
    for n in range(2):
        slope_lo[:, n * L : (n + 1) * L] = slps[4 + n]
        slope_hi[:, n * L : (n + 1) * L] = slps[6 + n]
    means = (
        [take(f[2], m) for m in means[:2]]
        + [means[2]]
        + [mid[:, t * L : (t + 1) * L] for t in range(6)]
        + [means[3]]
        + [take(f[3], m) for m in means[4:]]
    )
    rows = [jnp.concatenate([means[t], means[t + 5]], axis=1) for t in range(7)]
    packed = dot(jnp.concatenate(rows, axis=0), pack_matrix()).astype(BF)
    for t in range(7):
        pooled[:, t * L : (t + 1) * L] = packed[t * 64 : (t + 1) * 64]


def beside_kernel(flags, aa, cot, ab, v2, vedge, cc, vt):
    f = [flags[i] > 0 for i in range(6)]
    at = 2 * YH
    tiles = (
        [take(f[2], pick(f[5], ab[at], aa[at]))]
        + [cot[n] for n in range(8)]
        + [take(f[3], pick(f[5], aa[at], ab[at]))]
    )
    for t in range(5):
        pair = jnp.concatenate([tiles[t], tiles[t + 5]], axis=0)
        cc[:, t * L : (t + 1) * L] = pair.astype(F32).T
    for y in range(18):
        tile = vedge[:, :L] if y == 0 else vedge[:, L:] if y == 17 else v2[:, (y - 1) * L : y * L]
        vt[y * L : (y + 1) * L, :] = tile.astype(F32).T.astype(BF)


def coarse_kernel(flags, own, a, b, cc, weight, w_part, p2, gpc, first, second):
    f = [flags[i] > 0 for i in range(6)]
    p2[0:64, :] = take(f[0], pick(f[4], b[...], a[...]))
    p2[64:128, :] = own[...]
    p2[128:192, :] = take(f[1], pick(f[4], a[...], b[...]))
    lane = iota((128, L), 1)
    acc = dot(weight[...], taps(p2, 0, 5))
    for t, pre in enumerate(combine(acc, 128, 5, lane, 64)):
        _, slp = slopes(pre)
        tile = (cc[:, t * L : (t + 1) * L] * slp).astype(BF)
        gpc[:, t * L : (t + 1) * L] = tile
        if t < 2:
            other = pltpu.roll(tile.astype(F32), 64, 1).astype(BF)
            gpc[:, (t + 5) * L : (t + 6) * L] = other
    acc = dot(w_part[...], taps(gpc, 0, 5))
    for t, val in enumerate(combine(acc, 128, 5, lane, 64)):
        at = slice(t * L, (t + 1) * L)
        val = val.astype(BF)
        first[:, at] = pick(f[4], val[:64], val[64:])
        second[:, at] = pick(f[4], val[64:], val[:64])


def nt(a, b):
    return lax.dot_general(a, b, (((1,), (1,)), ((), ())), preferred_element_type=F32)


def coarse_corr_kernel(scale, flags, p2, gpc, w_own, own, kept, sent0, sent1, sent2, g3, out):
    lane = iota((64, L), 1)
    acc = dot(w_own[...], taps(gpc, 0, 5))
    for t, val in enumerate(combine(acc, 64, 5, lane, 64)):
        own[:, t * L : (t + 1) * L] = val
    lane = iota((128, L), 1)
    for t in range(5):
        at = slice(t * L, (t + 1) * L)
        tile = gpc[:, at].astype(F32)
        if t == 0 or t == 4:
            tile = jnp.where(lane >= 64 if t == 0 else lane < 64, tile, 0.0)
        g3[0:128, at] = shifted(tile, -1, lane, 64).astype(BF)
        g3[128:256, at] = tile.astype(BF)
        g3[256:384, at] = shifted(tile, 1, lane, 64).astype(BF)
    res = nt(taps(p2, 0, 5), g3[...]) * scale
    for j in range(3):
        for k in range(3):
            at = (3 * j + k) * 192
            out[at : at + 192, :] = res[j * 192 : (j + 1) * 192, k * L : (k + 1) * L].astype(BF)
    low, high = out[:HALF, :], out[HALF:, :]
    even = flags[5] > 0
    kept[...] = pick(even, low, high)
    sent = pick(even, high, low)
    part = HALF // 3
    sent0[...], sent1[...], sent2[...] = sent[:part], sent[part : 2 * part], sent[2 * part :]


def gpf_kernel(
    scale,
    flags,
    own,
    a,
    b,
    fc,
    slope_lo,
    slope,
    slope_hi,
    vt,
    kept,
    got0,
    got1,
    got2,
    first,
    second,
    mine,
    u3,
    pack,
):
    f = [flags[i] > 0 for i in range(6)]
    lane = iota((64, L), 1)
    rows = []
    for t in range(5):
        at = slice(t * L, (t + 1) * L)
        lo, hi = pick(f[4], b[:, at], a[:, at]), pick(f[4], a[:, at], b[:, at])
        total = own[:, at] + take(f[0], lo).astype(F32) + take(f[1], hi).astype(F32)
        main = total.astype(BF)
        rest = (total - main.astype(F32)).astype(BF)
        rows.append(jnp.concatenate([main, rest], axis=1))
    spread = spread_matrix()
    full = dot(jnp.concatenate(rows, axis=0), jnp.concatenate([spread, spread], axis=0))
    gps = [full[64 * t : 64 * t + 64, :L] for t in range(5)]
    gps += [full[64 * t : 64 * t + 64, L:] for t in range(3)]
    for m, gp in enumerate(gps):
        add = gp * 0.125
        for n in (2 * m, 2 * m + 1):
            if n < 2:
                slp = slope_lo[:, n * L : (n + 1) * L]
            elif n < 14:
                slp = slope[:, (n - 2) * L : (n - 1) * L]
            else:
                slp = slope_hi[:, (n - 14) * L : (n - 13) * L]
            rows, at = [], slice(n * L, (n + 1) * L)
            for x in range(2):
                val = (fc[x, n].astype(F32) + add) * slp[x * 64 : (x + 1) * 64]
                rows.append(val.astype(BF))
                tile = rows[x].astype(F32)
                u3[x * 64 : x * 64 + 64, at] = shifted(tile, -1, lane).astype(BF)
                u3[128 + x * 64 : 192 + x * 64, at] = rows[x]
                u3[256 + x * 64 : 320 + x * 64, at] = shifted(tile, 1, lane).astype(BF)
            first[n] = pick(f[4], rows[1], rows[0])
            second[n] = pick(f[4], rows[0], rows[1])
    halves = []
    for j in range(3):
        res = dot(u3[...], vt[j * L : (j + 16) * L, :]) * scale
        for k in range(3):
            both = res[k * L : k * L + 64] + pltpu.roll(res[k * L + 64 : (k + 1) * L], 192, 1)
            at = (3 * j + k) * 64
            pack[at : at + 64, :] = both[:, :L]
            halves.append(both[:, L:])
    halves.append(jnp.zeros((64, L), F32))
    lane = iota((64, L), 1)
    for n in range(5):
        packed = jnp.where(lane < 64, halves[2 * n], pltpu.roll(halves[2 * n + 1], 64, 1))
        pack[576 + 64 * n : 640 + 64 * n, :] = packed
    got = jnp.concatenate([got0[...], got1[...], got2[...]], axis=0)
    coarse = kept[...].astype(F32) + got.astype(F32)
    none = jnp.zeros((R, L), F32)
    for n in range(128):
        at = slice(n * R, (n + 1) * R)
        top = coarse[at] if n < HALF // R else none
        low = pack[at, :] if n < 896 // R else none
        mine[n] = jnp.concatenate([top, low], axis=0).astype(BF)


def gradient_edges_kernel(flags, a, b, c, d, first, second):
    for out, up in ((first, flags[5]), (second, 1 - flags[5])):
        for n, rows in enumerate((a, b, c, d)):
            out[n] = rows[up * 15]


def input_grad_kernel(flags, first, second, a, b, ea, eb, weight, out, g2):
    f = [flags[i] > 0 for i in range(6)]
    for y in range(18):
        if y == 0:
            tiles, ok = [pick(f[5], eb[n], ea[n]) for n in range(4)], f[2]
        elif y == 17:
            tiles, ok = [pick(f[5], ea[n], eb[n]) for n in range(4)], f[3]
        else:
            tiles, ok = [ref[y - 1] for ref in (first, second, a, b)], None
        one, two, lo, hi = tiles
        at = slice(y * L, (y + 1) * L)
        g2[0:64, at] = take(ok, take(f[0], pick(f[4], hi, lo)))
        g2[64:128, at] = take(ok, pick(f[4], two, one))
        g2[128:192, at] = take(ok, pick(f[4], one, two))
        g2[192:256, at] = take(ok, take(f[1], pick(f[4], lo, hi)))
    lane = iota((128, L), 1)
    for t in range(4):
        acc = dot(weight[...], taps(g2, 4 * t, 4))
        for n, val in enumerate(combine(acc, 128, 4, lane)):
            val = val.astype(BF)
            out[0, 4 * t + n] = val[:64]
            out[1, 4 * t + n] = val[64:]


def sum_kernel(parts, out):
    sums = []
    for core in range(2):
        total = parts[core].astype(F32)
        for n in range(core + 2, 128, 2):
            total = total + parts[n].astype(F32)
        sums.append(total)
    total = jnp.concatenate([sums[0][:R], sums[1][:R], sums[0][R:] + sums[1][R:]], axis=0)
    total = total.astype(BF)
    for n in range(128):
        out[n] = total


def unpack_kernel(got, fine, coarse, fine_v, coarse_v, sems):
    copies = []

    def send(held, out, i):
        copies.append(pltpu.make_async_copy(held.at[i], out.at[i], sems.at[len(copies)]))
        copies[-1].start()

    def coarse_rows(q):
        half, at = q // (HALF // R), q % (HALF // R)
        return got[at].astype(F32)[half * R : (half + 1) * R]

    def tile(n):
        rows = [got[m].astype(F32)[2 * R :] for m in range(n * 64 // R, (n + 1) * 64 // R)]
        return jnp.concatenate(rows, axis=0).T

    for n in range(9):
        part = tile(n)
        fine_v[0, n // 3, n % 3] = part[:64]
        fine_v[1, n // 3, n % 3] = part[64:]
    send(fine_v, fine, 0)
    send(fine_v, fine, 1)
    for n in range(5):
        part = tile(9 + n)
        for h in range(2):
            at = 2 * n + h
            if at < 9:
                fine_v[2, at // 3, at % 3] = part[64 * h : 64 * h + 64]
    send(fine_v, fine, 2)
    for i in range(3):
        for n in range(9):
            q = (n * 192 + i * 64) // R
            rows = [coarse_rows(q + m) for m in range(64 // R)]
            coarse_v[i, n // 3, n % 3] = jnp.concatenate(rows, axis=0)
        send(coarse_v, coarse, i)
    for copy in copies:
        copy.wait()


def call(kernel, name, outs, args, scratch=(), flags=True, macs=0, copies=0, far=()):
    space = pl.ANY if copies else pltpu.VMEM
    specs = [pl.BlockSpec(memory_space=space) for _ in args]
    if flags:
        specs[0] = pl.BlockSpec(memory_space=pltpu.SMEM)
    moved = sum(a.size * a.dtype.itemsize for a in args)
    shapes = tuple(jax.ShapeDtypeStruct(*o) for o in outs)
    if copies:
        scratch = [pltpu.SemaphoreType.DMA((copies,))]
    got = pl.pallas_call(
        kernel,
        out_shape=shapes,
        in_specs=specs,
        out_specs=tuple(
            pl.BlockSpec(memory_space=pl.ANY if n in far else space) for n in range(len(shapes))
        ),
        scratch_shapes=list(scratch),
        compiler_params=pltpu.CompilerParams(vmem_limit_bytes=VMEM),
        cost_estimate=pl.CostEstimate(flops=2 * macs, bytes_accessed=moved, transcendentals=0),
        name=name,
    )(*args)
    return got if len(shapes) > 1 else got[0]


def swaps(first, second, axis):
    count = lax.axis_size(axis)
    pairs = [(i, i ^ 1) for i in range(count)]
    others = [(0, 0), (count - 1, count - 1)] + [(i, ((i - 1) ^ 1) + 1) for i in range(1, count - 1)]
    other = lax.ppermute(second, axis, others)
    return lax.ppermute(first, axis, pairs), other


def diagonal_swap(far):
    turn = (0, 2, 1, 3)
    pairs = [(4 * i + j, 4 * (i ^ 1) + turn[j]) for i in range(32) for j in range(4)]
    return lax.ppermute(far, ("slab", "sub"), pairs)


def on_device(inputs, fine_cot, coarse_cot, weight_fine, weight_coarse):
    slab, sub = lax.axis_index("slab"), lax.axis_index("sub")
    flags = jnp.stack(
        [slab > 0, slab < 31, sub > 0, sub < 3, slab % 2 == 0, sub % 2 == 0]
    ).astype(jnp.int32)
    cot = jnp.swapaxes(coarse_cot[0], 1, 2)

    odd = slab % 2
    xa, xb = swaps(
        lax.dynamic_index_in_dim(inputs, 1 - odd, 0, False),
        lax.dynamic_index_in_dim(inputs, odd, 0, False),
        "slab",
    )
    own_edge = ((2 * YH + 1, 64, L), BF)
    corner = ((YH, 64, L), BF)
    first, second, far = call(
        own_edges_kernel,
        "own_edges",
        (own_edge, own_edge, corner),
        (flags, inputs, cot),
        copies=7,
    )
    aa, ab = swaps(first, second, "sub")
    nb = diagonal_swap(far)
    w_fwd, w_bwd, c_fwd, c_own, c_part = call(
        prepare_kernel,
        "prepare_weights",
        (
            ((384, 768), BF),
            ((384, 768), BF),
            ((384, 576), BF),
            ((192, 384), BF),
            ((384, 384), BF),
        ),
        (weight_fine, weight_coarse),
        flags=False,
    )
    xa, xb, w_fwd = lax.optimization_barrier((xa, xb, w_fwd))
    first, second = call(
        corner_edges_kernel, "corner_edges", (((2 * YH, 64, L), BF), corner), (flags, xa, xb)
    )
    ba, bb = swaps(first, second, "sub")
    v2, slope, mid = call(
        interior_kernel,
        "fine_forward_interior",
        (((256, 16 * L), BF), ((128, 12 * L), F32), ((64, 6 * L), BF)),
        (flags, inputs, xa, xb, w_fwd),
        macs=384 * 768 * 12 * L,
    )
    slope_lo, slope_hi, pooled, vedge = call(
        border_kernel,
        "fine_forward_border",
        (((128, 2 * L), F32), ((128, 2 * L), F32), ((64, 7 * L), BF), ((256, 2 * L), BF)),
        (flags, v2, mid, aa, ab, nb, ba, bb, w_fwd),
        scratch=[pltpu.VMEM((2, 256, 8 * L), BF)],
        macs=384 * 768 * 12 * L,
    )
    pa, pb = swaps(pooled, pooled, "slab")
    cc, vt = call(
        beside_kernel,
        "cotangent_and_turned_inputs",
        (((128, 5 * L), F32), ((18 * L, 256), BF)),
        (flags, aa, cot, ab, v2, vedge),
    )
    p2, gpc, first, second = call(
        coarse_kernel,
        "coarse_forward",
        (
            ((192, 7 * L), BF),
            ((128, 7 * L), BF),
            ((64, 5 * L), BF),
            ((64, 5 * L), BF),
        ),
        (flags, pooled, pa, pb, cc, c_fwd, c_part),
        macs=384 * 960 * 6 * L,
    )
    ga, gb = swaps(first, second, "slab")
    third = ((HALF // 3, L), BF)
    own, kept, *sent = call(
        functools.partial(coarse_corr_kernel, 1.0 / 256.0),
        "coarse_correlate",
        (((64, 5 * L), F32), ((HALF, L), BF), third, third, third),
        (flags, p2, gpc, c_own),
        scratch=[pltpu.VMEM((384, 5 * L), BF), pltpu.VMEM((2 * HALF, L), BF)],
        macs=384 * 768 * 6 * L,
    )
    got0, got1, got2 = (lax.ppermute(part, "sub", [(0, 1), (1, 0), (2, 3), (3, 2)]) for part in sent)
    first, second, mine = call(
        functools.partial(gpf_kernel, 524288.0**-0.5),
        "fine_gradient",
        (((16, 64, L), BF), ((16, 64, L), BF), ((128, 2 * R, L), BF)),
        (
            flags,
            own,
            ga,
            gb,
            fine_cot,
            slope_lo,
            slope,
            slope_hi,
            vt,
            kept,
            got0,
            got1,
            got2,
        ),
        scratch=[
            pltpu.VMEM((384, 16 * L), BF),
            pltpu.VMEM((896, L), F32),
        ],
        macs=384 * 768 * 16 * L,
    )
    ha, hb = swaps(first, second, "slab")
    shares = lax.all_to_all(mine.reshape(128 * 2 * R, L), ("slab", "sub"), 0, 0, tiled=True)
    total = call(
        sum_kernel,
        "sum_shares",
        (((128, 3 * R, L), BF),),
        (shares.reshape(128, 2 * R, L),),
        flags=False,
    )
    everything = lax.all_to_all(total.reshape(128 * 3 * R, L), ("slab", "sub"), 0, 0, tiled=True)
    one, two = call(
        gradient_edges_kernel,
        "gradient_edges",
        (((4, 64, L), BF), ((4, 64, L), BF)),
        (flags, first, second, ha, hb),
        macs=20 * 384 * 768 * 16 * L,
    )
    ea, eb = swaps(one, two, "sub")
    grad_input = call(
        input_grad_kernel,
        "input_gradient",
        (((2, 16, 64, L), BF),),
        (flags, first, second, ha, hb, ea, eb, w_bwd),
        scratch=[pltpu.VMEM((256, 18 * L), BF)],
        macs=384 * 768 * 16 * L,
    )
    grad_fine, grad_coarse = call(
        unpack_kernel,
        "unpack",
        (((3, 3, 3, 64, 64), F32), ((3, 3, 3, 64, 128), F32)),
        (everything.reshape(128, 3 * R, L),),
        scratch=[
            pltpu.VMEM((3, 3, 3, 64, 64), F32),
            pltpu.VMEM((3, 3, 3, 64, 128), F32),
            pltpu.SemaphoreType.DMA((6,)),
        ],
        flags=False,
        far=(0, 1),
    )
    return (grad_input, grad_fine, grad_coarse)


def solution(mesh):
    in_specs = (
        P("slab", "sub", None, None),
        P("slab", "sub", None, None),
        P("slab", "sub", None, None),
        P(),
        P(),
    )
    out_specs = (P("slab", "sub", None, None), P(), P())
    return jax.shard_map(
        on_device, mesh=mesh, in_specs=in_specs, out_specs=out_specs, check_vma=False
    )
```
